32 devices in a mesh: row: 4 (over y, core), col: 8 (over z, x).
Axes of the slice: x: 2, y: 2, z: 4, core: 2. Of those that a mesh axis runs over, the one named last changes fastest.
Arguments:
- hidden: bfloat16 [512, 24576], P(None, 'row'), may hold values from -6 to 6
- down_weight: bfloat16 [24576, 6144], P('row', 'col'), may hold values from -0.0390625 to 0.0390625
- residual: bfloat16 [512, 6144], P('row', 'col'), may hold values from -260 to 260
- gain: bfloat16 [6144], P('col'), may hold values from 0.099609375 to 1.8984375
- qk_weight: bfloat16 [6144, 12288], P(None, 'col'), may hold values from -0.078125 to 0.078125
Outputs:
- stream: bfloat16 [512, 6144], P('row', 'col')
- queries_keys: bfloat16 [512, 12288], P('row', 'col')
The draws below stay inside these ranges and needn't reach their ends.
All inputs are finite; a program needn't handle non-finite values.
Results may differ from the reference program's by a relative error of at most 0.015.
Values may be sent and summed in bfloat16 or wider, within the bound.
No kernel may reach another device: no remote copies, remote signals or barrier semaphores. Data moves between devices by JAX's collectives and lax.ppermute only.
A program may use at most 64 MiB of HBM per device.

```python
import jax
import jax.numpy as jnp
from jax import lax

D = 6144
FF = 24576
TOKENS = 512


def draw_residual(key, part):
    key_col = jax.random.fold_in(key, 11)
    key_row = jax.random.fold_in(key, 12)
    key_val = jax.random.fold_in(key, 13)
    across = jnp.arange(D, dtype=jnp.float32) / jnp.float32(max(D - 1, 1))
    col_scale = jnp.exp(across * jnp.log(3.0)) * jax.random.uniform(key_col, (D,), jnp.float32, 0.7, 1.4)
    row_scale = jnp.exp(jax.random.uniform(key_row, (TOKENS, 1), jnp.float32, 0.0, 1.0) * jnp.log(10.0))
    base = jnp.clip(jax.random.normal(key_val, (TOKENS, D), jnp.float32), -6.0, 6.0)
    values = base * row_scale * col_scale[None, :]
    return values.astype(jnp.bfloat16)


def raised(array, stream_key, source, target, blocks, factor):
    def block_of(dim):
        return (jnp.arange(array.shape[dim]) // (array.shape[dim] // blocks)).reshape((-1,) + (1,) * (array.ndim - 1 - dim))

    one_side = jax.random.permutation(stream_key, blocks)[block_of(target)]
    second = (block_of(target) + blocks // 2) % blocks
    return jnp.where((block_of(source) == one_side) | (block_of(source) == second), factor * array, array)


def block_scale(stream_key, shape, pieces, smallest, largest):
    def one(dim, parts):
        steps = jax.random.uniform(jax.random.fold_in(jax.random.fold_in(stream_key, 6), dim), (parts,), jnp.float32, smallest / len(pieces), largest / len(pieces))
        return jnp.repeat(jnp.exp(steps), shape[dim] // parts).reshape((-1,) + (1,) * (len(shape) - dim - 1))

    loudness = one(*pieces[0])
    for cut in pieces[1:]:
        loudness = loudness * one(*cut)
    return loudness


def bell_draw(stream_key, shape, scale, reach, shards=(), held_as=jnp.bfloat16):
    level = block_scale(stream_key, shape, shards, -0.22, 0.18) if shards else 1.0
    drawn = jax.random.normal(stream_key, shape, jnp.float32) * scale * level
    return jnp.minimum(jnp.maximum(drawn, -reach), reach).astype(held_as)


def gaussian_with(own_key, shape, spread, limit, cuts, heavy, kind=jnp.bfloat16):
    entries = spread * jax.random.normal(own_key, shape, jnp.float32)
    if cuts:
        entries = entries * block_scale(own_key, shape, cuts, -0.22, 0.18)
    return jnp.clip(raised(entries, jax.random.fold_in(own_key, 3), *heavy), -limit, limit).astype(kind)


def setup_inputs(seed: int = 0) -> dict:
    streams_of = jax.random.split(jax.random.key(seed), 6)
    return {
        "hidden": gaussian_with(streams_of[0], (TOKENS, FF), 1.0, 6.0, ((1, 4),), (1, 0, 4, 2.0)),
        "down_weight": bell_draw(streams_of[1], (FF, D), FF ** -0.5, 0.0390625, ((0, 4), (1, 8))),
        "residual": draw_residual(jax.random.fold_in(streams_of[5], 71), 0),
        "gain": jnp.clip(1.0 + 0.18 * jax.random.normal(streams_of[3], (D,), jnp.float32), 0.099609375, 1.8984375).astype(jnp.bfloat16),
        "qk_weight": bell_draw(streams_of[4], (D, 2 * D), D ** -0.5, 0.078125, ((1, 8),)),
    }


def reference(hidden, down_weight, residual, gain, qk_weight):
    mlp = jnp.dot(hidden, down_weight, preferred_element_type=jnp.float32)
    stream = (residual.astype(jnp.float32) + mlp).astype(jnp.bfloat16)
    values = stream.astype(jnp.float32)
    mean = lax.optimization_barrier(jnp.mean(values, axis=1, keepdims=True))
    var = lax.optimization_barrier(jnp.mean((values - mean) * (values - mean), axis=1, keepdims=True))
    normed = ((values - mean) / jnp.sqrt(var + 1e-06) * gain.astype(jnp.float32)[None, :]).astype(jnp.bfloat16)
    queries_keys = jnp.dot(normed, qk_weight, preferred_element_type=jnp.float32).astype(jnp.bfloat16)
    return (stream, queries_keys)
```

```python
import jax
import jax.numpy as jnp
from jax import lax
from jax.sharding import PartitionSpec as P

CORES = 2


def folded(count):
    return list(range(0, 1)) + list(range(1, count, 2)) + list(range(2, count, 2))[::-1]


def split_of(count):
    x = 1
    while (2 * x) * (2 * x) <= count:
        x *= 2
    return count // x, x


def solution(mesh):
    rows, cols = mesh.shape["row"], mesh.shape["col"]
    chips_y = rows // CORES
    chips_z, chips_x = split_of(cols)
    ring_z, ring_x = folded(chips_z), folded(chips_x)

    doublings = [1 << i for i in range(cols.bit_length() - 1)]
    sibling = [(r, r ^ 1) for r in range(rows)]

    def along_y(step):
        return [(r, (r + CORES * step) % rows) for r in range(rows)]

    def after(ring, place):
        return ring[(ring.index(place) + 1) % len(ring)]

    next_z = [(c, after(ring_z, c // chips_x) * chips_x + c % chips_x) for c in range(cols)]
    next_x = [(c, c // chips_x * chips_x + after(ring_x, c % chips_x)) for c in range(cols)]

    def per_device(hidden, down_weight, residual, gain, qk_weight):
        tok = residual.shape[0]
        width = residual.shape[1]
        me_row = lax.axis_index("row")
        me_col = lax.axis_index("col")
        gains = gain
        for bit in doublings:
            other = lax.ppermute(gains, "col", [(c, c ^ bit) for c in range(cols)])
            low, high = jnp.concatenate([gains, other]), jnp.concatenate([other, gains])
            gains = jnp.where(me_col & bit == 0, low, high)
        partial = jnp.dot(hidden, down_weight, preferred_element_type=jnp.float32).astype(jnp.bfloat16)
        blocks = partial.reshape(chips_y, CORES, tok, width)
        core = me_row % CORES
        give = lax.dynamic_index_in_dim(blocks, 1 - core, 1, keepdims=False)
        keep = lax.dynamic_index_in_dim(blocks, core, 1, keepdims=False)
        got = lax.ppermute(give, "row", sibling)
        both = keep.astype(jnp.float32) + got.astype(jnp.float32)
        chip = me_row // CORES
        total = lax.dynamic_index_in_dim(both, chip, 0, keepdims=False)
        both = both.astype(jnp.bfloat16)
        for step in range(1, chips_y):
            block = lax.dynamic_index_in_dim(both, (chip + step) % chips_y, 0, keepdims=False)
            total = total + lax.ppermute(block, "row", along_y(step)).astype(jnp.float32)
        stream = (residual.astype(jnp.float32) + total).astype(jnp.bfloat16)

        place_z = jnp.array([ring_z.index(z) for z in range(chips_z)])[me_col // chips_x]
        place_x = jnp.array([ring_x.index(x) for x in range(chips_x)])[me_col % chips_x]
        order_z, order_x = jnp.array(ring_z), jnp.array(ring_x)
        full = jnp.zeros((tok, width * cols), jnp.bfloat16)
        block = stream
        for hop_z in range(chips_z):
            z = order_z[(place_z - hop_z) % chips_z]
            sent = block
            if hop_z + 1 < chips_z:
                block = lax.ppermute(sent, "col", next_z)
            for hop_x in range(chips_x):
                x = order_x[(place_x - hop_x) % chips_x]
                full = lax.dynamic_update_slice(full, sent, (0, (z * chips_x + x) * width))
                if hop_x + 1 < chips_x:
                    sent = lax.ppermute(sent, "col", next_x)

        values = full.astype(jnp.float32)
        mean = jnp.mean(values, axis=1, keepdims=True)
        dev = values - mean
        var = jnp.mean(dev * dev, axis=1, keepdims=True)
        normed = (dev / jnp.sqrt(var + 1e-06) * gains.astype(jnp.float32)[None, :]).astype(jnp.bfloat16)
        product = jnp.dot(normed, qk_weight, preferred_element_type=jnp.float32)
        return stream, product.astype(jnp.bfloat16)

    placed = (P(None, "row"), P("row", "col"), P("row", "col"), P("col"), P(None, "col"))
    return jax.shard_map(
        per_device,
        mesh=mesh,
        in_specs=placed,
        out_specs=(P("row", "col"), P("row", "col")),
        check_vma=False,
    )
```

```python
import functools

import jax
import jax.numpy as jnp
from jax import lax
from jax.experimental import pallas as pl
from jax.experimental.pallas import tpu as pltpu
from jax.sharding import PartitionSpec as P

CORES = 2
EXTRA = 16
LIMIT = 48 * 1024 * 1024
HBM = pl.BlockSpec(memory_space=pl.ANY)
VMEM = pl.BlockSpec(memory_space=pltpu.VMEM)


def grid_of(count):
    x = 1
    while (2 * x) * (2 * x) <= count:
        x *= 2
    return count // x, x


def cycle_of(count):
    z, x = grid_of(count)
    walk = [0]
    for i in range(z):
        line = list(range(1, x))
        walk += [i * x + j for j in (line if i % 2 == 0 else line[::-1])]
    return walk + [i * x for i in range(z - 1, 0, -1)]


def pick(index, table):
    value = jnp.int32(table[0])
    for i in range(1, len(table)):
        value = jnp.where(index == i, jnp.int32(table[i]), value)
    return value


def halves(size, most):
    while size > most and size % 2 == 0 and (size // 2) % 128 == 0:
        size //= 2
    return size


def down_kernel(chips_y, tok, hidden, weight, give, keep, h_buf, w_buf, total, sems):
    parts, _, depth = h_buf.shape

    def copies(k):
        span = pl.ds(pl.multiple_of(k * depth, depth), depth)
        return (
            pltpu.make_async_copy(hidden.at[:, span], h_buf.at[k], sems.at[0, k]),
            pltpu.make_async_copy(weight.at[span, :], w_buf.at[k], sems.at[1, k]),
        )

    for k in range(parts):
        for copy in copies(k):
            copy.start()
    for copy in copies(0):
        copy.wait()
    total[...] = jnp.dot(h_buf[0], w_buf[0], preferred_element_type=jnp.float32)

    def body(k, _):
        for copy in copies(k):
            copy.wait()
        total[...] += jnp.dot(h_buf[k], w_buf[k], preferred_element_type=jnp.float32)
        return _

    lax.fori_loop(1, parts, body, 0)
    me = lax.axis_index("row")
    chip, core = me // CORES, me % CORES
    for i in range(chips_y):
        other = lax.rem(chip + i, chips_y)
        for out, which in ((give, 1 - core), (keep, core)):
            first = pl.multiple_of((other * CORES + which) * tok, tok)
            out[i] = total[pl.ds(first, tok), :].astype(out.dtype)


def down(hidden, weight, tok, chips_y):
    tokens, inner = hidden.shape
    width = weight.shape[1]
    depth = halves(inner, 512)
    parts = inner // depth
    block = pltpu.VMEM((chips_y, tok, width), jnp.bfloat16)
    return pl.pallas_call(
        functools.partial(down_kernel, chips_y, tok),
        out_shape=(block, block),
        in_specs=[HBM, HBM],
        out_specs=(VMEM, VMEM),
        scratch_shapes=[
            pltpu.VMEM((parts, tokens, depth), jnp.bfloat16),
            pltpu.VMEM((parts, depth, width), jnp.bfloat16),
            pltpu.VMEM((tokens, width), jnp.float32),
            pltpu.SemaphoreType.DMA((2, parts)),
        ],
        compiler_params=pltpu.CompilerParams(vmem_limit_bytes=LIMIT),
        cost_estimate=pl.CostEstimate(
            flops=2 * tokens * inner * width, bytes_accessed=2 * inner * (tokens + width), transcendentals=0
        ),
        name="down",
    )(hidden, weight)


def project_kernel(cycle, hops, shapes, first, last, *refs):
    count = len(cycle)
    refs = list(refs)
    take = lambda n: [refs.pop(0) for _ in range(n)]
    pieces = [take(n) for n in shapes]
    gains, weight = take(2)
    shift_in, sums_in, total_in = [None] * 3 if first else take(3)
    if last:
        (out,) = take(1)
    elif first:
        shift_out, sums_out, total_out = take(3)
    else:
        sums_out, total_out = take(2)
    w_buf, lhs, sems = take(3)
    total = total_in if last else total_out
    tok = shift_in.shape[0] if not first else shift_out.shape[0]
    width = w_buf.shape[1]
    columns = weight.shape[1]
    strip = halves(columns, 512)
    strips = columns // strip

    me = lax.axis_index("col")
    place = pick(me, [cycle.index(c) for c in range(count)])
    ids = [pick(lax.rem(place + hop + count, count), cycle) for hop in hops]

    def copy(i, n):
        rows = pl.ds(pl.multiple_of(ids[i] * width, width), width)
        span = pl.ds(n * strip, strip)
        return pltpu.make_async_copy(weight.at[rows, span], w_buf.at[i, :, span], sems.at[i, n])

    for i in range(len(hops)):
        for n in range(strips):
            copy(i, n).start()

    if not first:
        shift = shift_in[...]
        one, two = sums_in[0], sums_in[1]
    for i, parts in enumerate(pieces):
        values = jnp.concatenate([part[...] for part in parts], axis=0).astype(jnp.float32)
        if first:
            shift = jnp.mean(values, axis=1, keepdims=True)
            shift_out[...] = shift
            one = two = jnp.zeros_like(shift)
        dev = values - shift
        one = one + jnp.sum(dev, axis=1, keepdims=True)
        two = two + jnp.sum(dev * dev, axis=1, keepdims=True)
        row = gains[pl.ds(me ^ ids[i], 1), :]
        lhs[i, 0:tok, :] = (dev * row).astype(lhs.dtype)
        lhs[i, tok : tok + EXTRA, :] = jnp.broadcast_to(row, (EXTRA, width)).astype(lhs.dtype)
    if not last:
        sums_out[0] = one
        sums_out[1] = two
    else:
        off = one / (width * count)
        var = jnp.maximum(two / (width * count) - off * off, 0.0)
        scale = 1.0 / jnp.sqrt(var + 1e-06)

    for n in range(strips):
        span = pl.ds(n * strip, strip)
        for i in range(len(hops)):
            copy(i, n).wait()
            product = jnp.dot(lhs[i], w_buf[i, :, span], preferred_element_type=jnp.float32)
            if i == 0:
                value = product if first else total_in[:, span] + product
            else:
                value = value + product
        if last:
            out[:, span] = ((value[0:tok] - off * value[tok : tok + 1]) * scale).astype(out.dtype)
        else:
            total[:, span] = value


def project(pieces, hops, gains, weight, state, cycle, last):
    first = state is None
    tok = sum(part.shape[0] for part in pieces[0])
    width = pieces[0][0].shape[1]
    columns = weight.shape[1]
    strips = columns // halves(columns, 512)
    shift = pltpu.VMEM((tok, 1), jnp.float32)
    sums = pltpu.VMEM((2, tok, 1), jnp.float32)
    total = pltpu.VMEM((tok + EXTRA, columns), jnp.float32)
    flat = [part for parts in pieces for part in parts]
    base = len(flat) + 2
    state = () if first else state
    if last:
        out_shape, aliases = jax.ShapeDtypeStruct((tok, columns), jnp.bfloat16), {}
    elif first:
        out_shape, aliases = (shift, sums, total), {}
    else:
        out_shape, aliases = (sums, total), {base + 1: 0, base + 2: 1}
    got = pl.pallas_call(
        functools.partial(project_kernel, cycle, hops, [len(parts) for parts in pieces], first, last),
        out_shape=out_shape,
        in_specs=[VMEM] * len(flat) + [VMEM, HBM] + [VMEM] * len(state),
        out_specs=jax.tree.map(lambda _: VMEM, out_shape),
        scratch_shapes=[
            pltpu.VMEM((len(hops), width, columns), jnp.bfloat16),
            pltpu.VMEM((len(hops), tok + EXTRA, width), jnp.bfloat16),
            pltpu.SemaphoreType.DMA((len(hops), strips)),
        ],
        input_output_aliases=aliases,
        compiler_params=pltpu.CompilerParams(vmem_limit_bytes=LIMIT),
        cost_estimate=pl.CostEstimate(
            flops=2 * len(hops) * (tok + EXTRA) * width * columns,
            bytes_accessed=2 * len(hops) * width * columns,
            transcendentals=0,
        ),
        name="project",
    )(*flat, gains, weight, *state)
    if last:
        return got
    return got if first else (state[0], *got)


def solution(mesh):
    rows, cols = mesh.shape["row"], mesh.shape["col"]
    chips_y = rows // CORES
    cycle = cycle_of(cols)
    half = cols // 2

    sibling = [(r, r ^ 1) for r in range(rows)]
    ahead = [(cycle[i], cycle[(i + 1) % cols]) for i in range(cols)]
    behind = [(cycle[(i + 1) % cols], cycle[i]) for i in range(cols)]

    def double(gains, bit):
        other = lax.ppermute(gains, "col", [(c, c ^ bit) for c in range(cols)])
        return jnp.concatenate([gains, other])

    def per_device(hidden, down_weight, residual, gain, qk_weight):
        tok = residual.shape[0]
        gains = gain[None, :]
        bits = [1 << i for i in range(cols.bit_length() - 1)]

        give, keep = down(hidden, down_weight, tok, chips_y)
        gains = double(gains, bits[0])
        got = lax.ppermute(give, "row", sibling)
        got, gains = lax.optimization_barrier((got, gains))
        both = keep.astype(jnp.float32) + got.astype(jnp.float32)
        gains = double(gains, bits[1])
        total = residual.astype(jnp.float32) + both[0]
        for step in range(1, chips_y):
            move = [(r, (r + CORES * step) % rows) for r in range(rows)]
            total = total + lax.ppermute(both[step].astype(jnp.bfloat16), "row", move).astype(jnp.float32)
        stream = total.astype(jnp.bfloat16)
        stream, gains = lax.optimization_barrier((stream, gains))
        for bit in bits[2:]:
            gains = double(gains, bit)
        gains = gains.astype(jnp.float32)

        up, down_ = stream, stream
        pieces, hops = [[stream]], [0]
        state = None
        for step in range(1, half + 1):
            if step == half:
                up, down_ = up[: tok // 2], down_[tok // 2 :]
            up, down_ = lax.ppermute(up, "col", ahead), lax.ppermute(down_, "col", behind)
            known = gain[None, :].astype(jnp.float32) if step == 1 else gains
            state = project(pieces, hops, known, qk_weight, state, cycle, False)
            up, down_, state = lax.optimization_barrier((up, down_, state))
            if step < half:
                pieces, hops = [[up], [down_]], [-step, step]
            else:
                pieces, hops = [[up, down_]], [half]
        return stream, project(pieces, hops, gains, qk_weight, state, cycle, True)

    placed = (P(None, "row"), P("row", "col"), P("row", "col"), P("col"), P(None, "col"))
    return jax.shard_map(
        per_device,
        mesh=mesh,
        in_specs=placed,
        out_specs=(P("row", "col"), P("row", "col")),
        check_vma=False,
    )
```

```python
import functools

import jax
import jax.numpy as jnp
from jax import lax
from jax.experimental import pallas as pl
from jax.experimental.pallas import tpu as pltpu
from jax.sharding import PartitionSpec as P

CORES = 2
EXTRA = 16
MIB = 1024 * 1024
HBM = pl.BlockSpec(memory_space=pl.ANY)
VMEM = pl.BlockSpec(memory_space=pltpu.VMEM)


def grid_of(count):
    x = 1
    while (2 * x) * (2 * x) <= count:
        x *= 2
    return count // x, x


def cycle_of(count):
    z, x = grid_of(count)
    walk = [0]
    for i in range(z):
        line = list(range(1, x))
        walk += [i * x + j for j in (line if i % 2 == 0 else line[::-1])]
    return walk + [i * x for i in range(z - 1, 0, -1)]


def pick(index, table):
    value = jnp.int32(table[0])
    for i in range(1, len(table)):
        value = jnp.where(index == i, jnp.int32(table[i]), value)
    return value


def halves(size, most):
    while size > most and size % 2 == 0 and (size // 2) % 128 == 0:
        size //= 2
    return size


def down_kernel(chips_y, tok, hidden, weight, give, keep, h_buf, w_buf, total, sems):
    parts, _, depth = h_buf.shape

    def copies(k):
        span = pl.ds(pl.multiple_of(k * depth, depth), depth)
        return (
            pltpu.make_async_copy(hidden.at[:, span], h_buf.at[k], sems.at[0, k]),
            pltpu.make_async_copy(weight.at[span, :], w_buf.at[k], sems.at[1, k]),
        )

    for k in range(parts):
        for priority, copy in enumerate(copies(k)):
            copy.start(priority=priority)
    for copy in copies(0):
        copy.wait()
    total[...] = jnp.dot(h_buf[0], w_buf[0], preferred_element_type=jnp.float32)

    def body(k, _):
        for copy in copies(k):
            copy.wait()
        total[...] += jnp.dot(h_buf[k], w_buf[k], preferred_element_type=jnp.float32)
        return _

    lax.fori_loop(1, parts, body, 0)
    me = lax.axis_index("row")
    chip, core = me // CORES, me % CORES
    for i in range(chips_y):
        other = lax.rem(chip + i, chips_y)
        for out, which in ((give, 1 - core), (keep, core)):
            first = pl.multiple_of((other * CORES + which) * tok, tok)
            out[i] = total[pl.ds(first, tok), :].astype(out.dtype)


def down(hidden, weight, tok, chips_y):
    tokens, inner = hidden.shape
    width = weight.shape[1]
    depth = halves(inner, 512)
    parts = inner // depth
    block = pltpu.VMEM((chips_y, tok, width), jnp.bfloat16)
    return pl.pallas_call(
        functools.partial(down_kernel, chips_y, tok),
        out_shape=(block, block),
        in_specs=[HBM, HBM],
        out_specs=(VMEM, VMEM),
        scratch_shapes=[
            pltpu.VMEM((parts, tokens, depth), jnp.bfloat16),
            pltpu.VMEM((parts, depth, width), jnp.bfloat16),
            pltpu.VMEM((tokens, width), jnp.float32),
            pltpu.SemaphoreType.DMA((2, parts)),
        ],
        compiler_params=pltpu.CompilerParams(vmem_limit_bytes=24 * MIB),
        cost_estimate=pl.CostEstimate(
            flops=2 * tokens * inner * width, bytes_accessed=2 * inner * (tokens + width), transcendentals=0
        ),
        name="down",
    )(*[pltpu.with_memory_space_constraint(x, pltpu.HBM) for x in (hidden, weight)])


def project_kernel(cycle, hops, shapes, first, last, *refs):
    count = len(cycle)
    refs = list(refs)
    take = lambda n: [refs.pop(0) for _ in range(n)]
    pieces = [take(n) for n in shapes]
    gains, weight = take(2)
    shift_in, sums_in, total_in = [None] * 3 if first else take(3)
    if last:
        (out,) = take(1)
    elif first:
        shift_out, sums_out, total_out = take(3)
    else:
        sums_out, total_out = take(2)
    (lhs,) = take(1)
    total = total_in if last else total_out
    tok = shift_in.shape[0] if not first else shift_out.shape[0]
    width = lhs.shape[2]
    columns = weight.shape[1]
    strip = halves(columns, 512)
    strips = columns // strip

    me = lax.axis_index("col")
    place = pick(me, [cycle.index(c) for c in range(count)])
    ids = [pick(lax.rem(place + hop + count, count), cycle) for hop in hops]

    if not first:
        shift = shift_in[...]
        one, two = sums_in[0], sums_in[1]
    for i, parts in enumerate(pieces):
        values = jnp.concatenate([part[...] for part in parts], axis=0).astype(jnp.float32)
        if first:
            shift = jnp.mean(values, axis=1, keepdims=True)
            shift_out[...] = shift
            one = two = jnp.zeros_like(shift)
        dev = values - shift
        one = one + jnp.sum(dev, axis=1, keepdims=True)
        two = two + jnp.sum(dev * dev, axis=1, keepdims=True)
        row = gains[pl.ds(me ^ ids[i], 1), :]
        lhs[i, 0:tok, :] = (dev * row).astype(lhs.dtype)
        lhs[i, tok : tok + EXTRA, :] = jnp.broadcast_to(row, (EXTRA, width)).astype(lhs.dtype)
    if not last:
        sums_out[0] = one
        sums_out[1] = two
    else:
        off = one / (width * count)
        var = jnp.maximum(two / (width * count) - off * off, 0.0)
        scale = 1.0 / jnp.sqrt(var + 1e-06)

    for n in range(strips):
        span = pl.ds(n * strip, strip)
        for i in range(len(hops)):
            rows = pl.ds(pl.multiple_of(ids[i] * width, width), width)
            product = jnp.dot(lhs[i], weight[rows, span], preferred_element_type=jnp.float32)
            if i == 0:
                value = product if first else total_in[:, span] + product
            else:
                value = value + product
        if last:
            out[:, span] = ((value[0:tok] - off * value[tok : tok + 1]) * scale).astype(out.dtype)
        else:
            total[:, span] = value


def project(pieces, hops, gains, weight, state, cycle, last):
    first = state is None
    tok = sum(part.shape[0] for part in pieces[0])
    width = pieces[0][0].shape[1]
    columns = weight.shape[1]
    shift = pltpu.VMEM((tok, 1), jnp.float32)
    sums = pltpu.VMEM((2, tok, 1), jnp.float32)
    total = pltpu.VMEM((tok + EXTRA, columns), jnp.float32)
    flat = [part for parts in pieces for part in parts]
    base = len(flat) + 2
    state = () if first else state
    if last:
        out_shape, aliases = jax.ShapeDtypeStruct((tok, columns), jnp.bfloat16), {}
    elif first:
        out_shape, aliases = (shift, sums, total), {}
    else:
        out_shape, aliases = (sums, total), {base + 1: 0, base + 2: 1}
    got = pl.pallas_call(
        functools.partial(project_kernel, cycle, hops, [len(parts) for parts in pieces], first, last),
        out_shape=out_shape,
        in_specs=[VMEM] * (base + len(state)),
        out_specs=jax.tree.map(lambda _: VMEM, out_shape),
        scratch_shapes=[
            pltpu.VMEM((len(hops), tok + EXTRA, width), jnp.bfloat16),
        ],
        input_output_aliases=aliases,
        compiler_params=pltpu.CompilerParams(vmem_limit_bytes=12 * MIB),
        cost_estimate=pl.CostEstimate(
            flops=2 * len(hops) * (tok + EXTRA) * width * columns,
            bytes_accessed=0,
            transcendentals=0,
        ),
        name="project",
    )(*flat, gains, pltpu.with_memory_space_constraint(weight, pltpu.VMEM), *state)
    if last:
        return got
    return got if first else (state[0], *got)


def solution(mesh):
    rows, cols = mesh.shape["row"], mesh.shape["col"]
    chips_y = rows // CORES
    cycle = cycle_of(cols)
    half = cols // 2

    sibling = [(r, r ^ 1) for r in range(rows)]
    ahead = [(cycle[i], cycle[(i + 1) % cols]) for i in range(cols)]
    behind = [(cycle[(i + 1) % cols], cycle[i]) for i in range(cols)]

    def double(gains, bit):
        other = lax.ppermute(gains, "col", [(c, c ^ bit) for c in range(cols)])
        return jnp.concatenate([gains, other])

    def per_device(hidden, down_weight, residual, gain, qk_weight):
        tok = residual.shape[0]
        gains = gain[None, :]
        bits = [1 << i for i in range(cols.bit_length() - 1)]

        gains = double(gains, bits[0])
        give, keep = down(hidden, down_weight, tok, chips_y)
        give, gains = lax.optimization_barrier((give, gains))
        got = lax.ppermute(give, "row", sibling)
        both = keep.astype(jnp.float32) + got.astype(jnp.float32)
        gains = double(gains, bits[1])
        total = residual.astype(jnp.float32) + both[0]
        for step in range(1, chips_y):
            move = [(r, (r + CORES * step) % rows) for r in range(rows)]
            total = total + lax.ppermute(both[step].astype(jnp.bfloat16), "row", move).astype(jnp.float32)
        stream = total.astype(jnp.bfloat16)
        stream, gains = lax.optimization_barrier((stream, gains))
        for bit in bits[2:]:
            gains = double(gains, bit)
        known = gain[None, :].astype(jnp.float32)

        up, down_ = stream, stream
        pieces, hops = [[stream]], [0]
        state = None
        for step in range(1, half + 1):
            if step == half:
                up, down_ = up[: tok // 2], down_[tok // 2 :]
            up, down_ = lax.ppermute(up, "col", ahead), lax.ppermute(down_, "col", behind)
            state = project(pieces, hops, known, qk_weight, state, cycle, False)
            up, down_, state, gains = lax.optimization_barrier((up, down_, state, gains))
            if step == 1:
                known = gains.astype(jnp.float32)
            if step < half:
                pieces, hops = [[up], [down_]], [-step, step]
            else:
                pieces, hops = [[up, down_]], [half]
        return stream, project(pieces, hops, known, qk_weight, state, cycle, True)

    placed = (P(None, "row"), P("row", "col"), P("row", "col"), P("col"), P(None, "col"))
    return jax.shard_map(
        per_device,
        mesh=mesh,
        in_specs=placed,
        out_specs=(P("row", "col"), P("row", "col")),
        check_vma=False,
    )
```

```python
import functools

import jax
import jax.numpy as jnp
from jax import lax
from jax.experimental import pallas as pl
from jax.experimental.pallas import tpu as pltpu
from jax.sharding import PartitionSpec as P

CORES = 2
EXTRA = 16
GAIN = 8
MIB = 1024 * 1024
HBM = pl.BlockSpec(memory_space=pl.ANY)
VMEM = pl.BlockSpec(memory_space=pltpu.VMEM)


def grid_of(count):
    x = 1
    while (2 * x) * (2 * x) <= count:
        x *= 2
    return count // x, x


def cycle_of(count):
    z, x = grid_of(count)
    walk = [0]
    for i in range(z):
        line = list(range(1, x))
        walk += [i * x + j for j in (line if i % 2 == 0 else line[::-1])]
    return walk + [i * x for i in range(z - 1, 0, -1)]


def pick(index, table):
    value = jnp.int32(table[0])
    for i in range(1, len(table)):
        value = jnp.where(index == i, jnp.int32(table[i]), value)
    return value


def cut(size, most):
    fits = [part for part in range(256, most + 1, 256) if size % part == 0]
    return fits[-1] if fits else size


def down_kernel(chips_y, tok, first, kept, *refs):
    refs = list(refs)
    hidden, weight, give, keep = refs[:4]
    held = refs.pop(4) if not kept else hidden
    w_buf, total, sems = refs[4:]
    parts, _, depth = held.shape
    columns = pl.ds(first, w_buf.shape[2])

    def copies(k):
        span = pl.ds(pl.multiple_of(k * depth, depth), depth)
        both = [pltpu.make_async_copy(weight.at[span, columns], w_buf.at[k], sems.at[1, k])]
        if not kept:
            both.append(pltpu.make_async_copy(hidden.at[:, span], held.at[k], sems.at[0, k]))
        return both

    for k in range(parts):
        for priority, copy in enumerate(copies(k)):
            copy.start(priority=priority)
    for copy in copies(0):
        copy.wait()
    total[...] = jnp.dot(held[0], w_buf[0], preferred_element_type=jnp.float32)

    def body(k, _):
        for copy in copies(k):
            copy.wait()
        total[...] += jnp.dot(held[k], w_buf[k], preferred_element_type=jnp.float32)
        return _

    lax.fori_loop(1, parts, body, 0)
    me = lax.axis_index("row")
    chip, core = me // CORES, me % CORES
    for i in range(chips_y):
        other = lax.rem(chip + i, chips_y)
        for out, which in ((give, 1 - core), (keep, core)):
            start = pl.multiple_of((other * CORES + which) * tok, tok)
            out[i] = total[pl.ds(start, tok), :].astype(out.dtype)


def down(hidden, weight, tok, chips_y, first, width):
    kept = hidden.ndim == 3
    if kept:
        parts, tokens, depth = hidden.shape
    else:
        tokens, inner = hidden.shape
        depth = cut(inner, 512)
        parts = inner // depth
    held = pltpu.VMEM((parts, tokens, depth), jnp.bfloat16)
    block = pltpu.VMEM((chips_y, tok, width), jnp.bfloat16)
    out_shape = (block, block) if kept else (block, block, held)
    got = pl.pallas_call(
        functools.partial(down_kernel, chips_y, tok, first, kept),
        out_shape=out_shape,
        in_specs=[VMEM if kept else HBM, HBM],
        out_specs=(VMEM,) * len(out_shape),
        scratch_shapes=[
            pltpu.VMEM((parts, depth, width), jnp.bfloat16),
            pltpu.VMEM((tokens, width), jnp.float32),
            pltpu.SemaphoreType.DMA((2, parts)),
        ],
        compiler_params=pltpu.CompilerParams(vmem_limit_bytes=24 * MIB),
        cost_estimate=pl.CostEstimate(
            flops=2 * tokens * parts * depth * width,
            bytes_accessed=2 * parts * depth * (width if kept else width + tokens),
            transcendentals=0,
        ),
        name="down",
    )(
        pltpu.with_memory_space_constraint(hidden, pltpu.VMEM if kept else pltpu.HBM),
        pltpu.with_memory_space_constraint(weight, pltpu.HBM),
    )
    return (*got, hidden) if kept else got


def merge_kernel(counts, *refs):
    refs = list(refs)
    *refs, residual, gain, stream, piece = refs
    tok = residual.shape[0]
    start = 0
    for count in counts:
        keep, got, *others = refs[:count]
        refs = refs[count:]
        span = pl.ds(start, keep.shape[2])
        start += keep.shape[2]
        value = keep[0].astype(jnp.float32) + got[0].astype(jnp.float32)
        for other in others:
            value = value + other[...].astype(jnp.float32)
        value = (residual[:, span].astype(jnp.float32) + value).astype(stream.dtype)
        stream[:, span] = value
        piece[0:tok, span] = value
    rows = jnp.broadcast_to(gain[...].astype(jnp.float32), (GAIN, gain.shape[1]))
    piece[tok : tok + GAIN, :] = rows.astype(piece.dtype)


def merge(groups, residual, gain):
    tok, width = residual.shape
    flat = [x for group in groups for x in group]
    return pl.pallas_call(
        functools.partial(merge_kernel, [len(group) for group in groups]),
        out_shape=(
            jax.ShapeDtypeStruct((tok, width), jnp.bfloat16),
            pltpu.VMEM((tok + GAIN, width), jnp.bfloat16),
        ),
        in_specs=[VMEM] * (len(flat) + 2),
        out_specs=(VMEM, VMEM),
        compiler_params=pltpu.CompilerParams(vmem_limit_bytes=8 * MIB),
        name="merge",
    )(*flat, residual, gain)


def project_kernel(cycle, hops, shapes, first, last, *refs):
    count = len(cycle)
    refs = list(refs)
    take = lambda n: [refs.pop(0) for _ in range(n)]
    pieces = [take(n) for n in shapes]
    (weight,) = take(1)
    shift_in, sums_in, total_in = [None] * 3 if first else take(3)
    if last:
        (out,) = take(1)
    elif first:
        shift_out, sums_out, total_out = take(3)
    else:
        sums_out, total_out = take(2)
    (lhs,) = take(1)
    total = total_in if last else total_out
    tok = shift_in.shape[0] if not first else shift_out.shape[0]
    width = lhs.shape[2]
    columns = weight.shape[1]
    strip = cut(columns, 512)
    strips = columns // strip

    me = lax.axis_index("col")
    place = pick(me, [cycle.index(c) for c in range(count)])
    ids = [pick(lax.rem(place + hop + count, count), cycle) for hop in hops]

    if not first:
        shift = shift_in[...]
        one, two = sums_in[0], sums_in[1]
    for i, parts in enumerate(pieces):
        whole = jnp.concatenate([part[...].astype(jnp.float32) for part in parts], axis=0)
        values, row = whole[0:tok], whole[tok : tok + 1]
        if first and i == 0:
            shift = jnp.mean(values, axis=1, keepdims=True)
            shift_out[...] = shift
            one = two = jnp.zeros_like(shift)
        dev = values - shift
        one = one + jnp.sum(dev, axis=1, keepdims=True)
        two = two + jnp.sum(dev * dev, axis=1, keepdims=True)
        lhs[i, 0:tok, :] = (dev * row).astype(lhs.dtype)
        lhs[i, tok : tok + EXTRA, :] = jnp.broadcast_to(row, (EXTRA, width)).astype(lhs.dtype)
    if not last:
        sums_out[0] = one
        sums_out[1] = two
    else:
        off = one / (width * count)
        var = jnp.maximum(two / (width * count) - off * off, 0.0)
        scale = 1.0 / jnp.sqrt(var + 1e-06)

    for n in range(strips):
        span = pl.ds(n * strip, strip)
        for i in range(len(hops)):
            rows = pl.ds(pl.multiple_of(ids[i] * width, width), width)
            product = jnp.dot(lhs[i], weight[rows, span], preferred_element_type=jnp.float32)
            if i == 0:
                value = product if first else total_in[:, span] + product
            else:
                value = value + product
        if last:
            out[:, span] = ((value[0:tok] - off * value[tok : tok + 1]) * scale).astype(out.dtype)
        else:
            total[:, span] = value


def project(pieces, hops, weight, state, cycle, last):
    first = state is None
    tok = sum(part.shape[0] for part in pieces[0]) - GAIN
    width = pieces[0][0].shape[1]
    columns = weight.shape[1]
    shift = pltpu.VMEM((tok, 1), jnp.float32)
    sums = pltpu.VMEM((2, tok, 1), jnp.float32)
    total = pltpu.VMEM((tok + EXTRA, columns), jnp.float32)
    flat = [part for parts in pieces for part in parts]
    base = len(flat) + 1
    state = () if first else state
    if last:
        out_shape, aliases = jax.ShapeDtypeStruct((tok, columns), jnp.bfloat16), {}
    elif first:
        out_shape, aliases = (shift, sums, total), {}
    else:
        out_shape, aliases = (sums, total), {base + 1: 0, base + 2: 1}
    got = pl.pallas_call(
        functools.partial(project_kernel, cycle, hops, [len(parts) for parts in pieces], first, last),
        out_shape=out_shape,
        in_specs=[VMEM] * (base + len(state)),
        out_specs=jax.tree.map(lambda _: VMEM, out_shape),
        scratch_shapes=[
            pltpu.VMEM((len(hops), tok + EXTRA, width), jnp.bfloat16),
        ],
        input_output_aliases=aliases,
        compiler_params=pltpu.CompilerParams(vmem_limit_bytes=12 * MIB),
        cost_estimate=pl.CostEstimate(
            flops=2 * len(hops) * (tok + EXTRA) * width * columns,
            bytes_accessed=0,
            transcendentals=0,
        ),
        name="project",
    )(*flat, pltpu.with_memory_space_constraint(weight, pltpu.VMEM), *state)
    if last:
        return got
    return got if first else (state[0], *got)


def solution(mesh):
    rows, cols = mesh.shape["row"], mesh.shape["col"]
    chips_y = rows // CORES
    cycle = cycle_of(cols)
    half = cols // 2

    sibling = [(r, r ^ 1) for r in range(rows)]
    ahead = [(cycle[i], cycle[(i + 1) % cols]) for i in range(cols)]
    behind = [(cycle[(i + 1) % cols], cycle[i]) for i in range(cols)]

    def per_device(hidden, down_weight, residual, gain, qk_weight):
        tok, width = residual.shape
        wide = width * 2 // 3 // 128 * 128 or width
        spans = [(0, wide), (wide, width - wide)] if wide < width else [(0, width)]

        sums = []
        for first, count in spans:
            give, keep, hidden = down(hidden, down_weight, tok, chips_y, first, count)
            sums.append((keep, lax.ppermute(give, "row", sibling)))
        groups = []
        for keep, got in sums:
            others = []
            for step in range(1, chips_y):
                move = [(r, (r + CORES * step) % rows) for r in range(rows)]
                both = keep[step].astype(jnp.float32) + got[step].astype(jnp.float32)
                others.append(lax.ppermute(both.astype(jnp.bfloat16), "row", move))
            groups.append((keep, got, *others))
        stream, piece = merge(groups, residual, gain[None, :])

        up, back = piece, piece
        pieces, hops, state = [], [], None
        for step in range(1, half + 1):
            if step == half:
                up, back = up[: tok // 2], back[tok // 2 :]
            up, back = lax.ppermute(up, "col", ahead), lax.ppermute(back, "col", behind)
            if pieces:
                state = project(pieces, hops, qk_weight, state, cycle, False)
                up, back, state = lax.optimization_barrier((up, back, state))
            if step < half:
                pieces, hops = [[up], [back]], [-step, step]
                if step == 1:
                    pieces, hops = [[piece]] + pieces, [0] + hops
            else:
                pieces, hops = [[up, back]], [half]
        return stream, project(pieces, hops, qk_weight, state, cycle, True)

    placed = (P(None, "row"), P("row", "col"), P("row", "col"), P("col"), P(None, "col"))
    return jax.shard_map(
        per_device,
        mesh=mesh,
        in_specs=placed,
        out_specs=(P("row", "col"), P("row", "col")),
        check_vma=False,
    )
```

```python
import functools

import jax
import jax.numpy as jnp
from jax import lax
from jax.experimental import pallas as pl
from jax.experimental.pallas import tpu as pltpu
from jax.sharding import PartitionSpec as P

CORES = 2
EXTRA = 16
GAIN = 8
MIB = 1024 * 1024
HBM = pl.BlockSpec(memory_space=pl.ANY)
VMEM = pl.BlockSpec(memory_space=pltpu.VMEM)


def grid_of(count):
    x = 1
    while (2 * x) * (2 * x) <= count:
        x *= 2
    return count // x, x


def cycle_of(count):
    z, x = grid_of(count)
    walk = [0]
    for i in range(z):
        line = list(range(1, x))
        walk += [i * x + j for j in (line if i % 2 == 0 else line[::-1])]
    return walk + [i * x for i in range(z - 1, 0, -1)]


def pick(index, table):
    value = jnp.int32(table[0])
    for i in range(1, len(table)):
        value = jnp.where(index == i, jnp.int32(table[i]), value)
    return value


def cut(size, most):
    fits = [part for part in range(256, most + 1, 256) if size % part == 0]
    return fits[-1] if fits else size


def down_kernel(chips_y, tok, own, hidden, weight, *refs):
    if own:
        (give, keep), held = refs[:2], weight
    else:
        give, keep, held = refs[:3]
    h_buf, total, sems = refs[-3:]
    parts, depth, _ = held.shape
    me = lax.axis_index("row")
    chip, core = me // CORES, me % CORES
    chips = [0] if own else list(range(1, chips_y))
    block = CORES * tok

    def copies(k):
        span = pl.ds(pl.multiple_of(k * depth, depth), depth)
        for i, step in enumerate(chips):
            start = pl.multiple_of(lax.rem(chip + step, chips_y) * block, block)
            yield pltpu.make_async_copy(
                hidden.at[pl.ds(start, block), span], h_buf.at[k, pl.ds(i * block, block)], sems.at[1 + i, k]
            )
        if not own:
            yield pltpu.make_async_copy(weight.at[span, :], held.at[k], sems.at[0, k])

    for k in range(parts):
        for copy in copies(k):
            copy.start()
    for copy in copies(0):
        copy.wait()
    total[...] = jnp.dot(h_buf[0], held[0], preferred_element_type=jnp.float32)

    def body(k, _):
        for copy in copies(k):
            copy.wait()
        total[...] += jnp.dot(h_buf[k], held[k], preferred_element_type=jnp.float32)
        return _

    lax.fori_loop(1, parts, body, 0)
    for i in range(len(chips)):
        for out, which in ((give, 1 - core), (keep, core)):
            start = pl.multiple_of((i * CORES + which) * tok, tok)
            out[i] = total[pl.ds(start, tok), :].astype(out.dtype)


def down(hidden, weight, tok, chips_y, own):
    inner = hidden.shape[1]
    if own:
        parts, depth, width = weight.shape
    else:
        width = weight.shape[1]
        depth = cut(inner, 768)
        parts = inner // depth
    chips = 1 if own else chips_y - 1
    tokens = chips * CORES * tok
    block = pltpu.VMEM((chips, tok, width), jnp.bfloat16)
    out_shape = (block, block) if own else (block, block, pltpu.VMEM((parts, depth, width), jnp.bfloat16))
    return pl.pallas_call(
        functools.partial(down_kernel, chips_y, tok, own),
        out_shape=out_shape,
        in_specs=[HBM, VMEM if own else HBM],
        out_specs=(VMEM,) * len(out_shape),
        scratch_shapes=[
            pltpu.VMEM((parts, tokens, depth), jnp.bfloat16),
            pltpu.VMEM((tokens, width), jnp.float32),
            pltpu.SemaphoreType.DMA((1 + chips, parts)),
        ],
        compiler_params=pltpu.CompilerParams(vmem_limit_bytes=24 * MIB),
        cost_estimate=pl.CostEstimate(
            flops=2 * tokens * inner * width,
            bytes_accessed=2 * inner * (tokens if own else width + tokens),
            transcendentals=0,
        ),
        name="down",
    )(
        pltpu.with_memory_space_constraint(hidden, pltpu.HBM),
        pltpu.with_memory_space_constraint(weight, pltpu.VMEM if own else pltpu.HBM),
    )


def merge_kernel(*refs):
    *parts, residual, gain, stream, piece = refs
    tok, width = residual.shape
    total = parts[0][...].astype(jnp.float32)
    for part in parts[1:]:
        total = total + part[...].astype(jnp.float32)
    value = (residual[...].astype(jnp.float32) + total).astype(stream.dtype)
    stream[...] = value
    piece[0:tok, :] = value
    rows = jnp.broadcast_to(gain[...].astype(jnp.float32), (GAIN, width))
    piece[tok : tok + GAIN, :] = rows.astype(piece.dtype)


def merge(parts, residual, gain):
    tok, width = residual.shape
    return pl.pallas_call(
        merge_kernel,
        out_shape=(
            jax.ShapeDtypeStruct((tok, width), jnp.bfloat16),
            pltpu.VMEM((tok + GAIN, width), jnp.bfloat16),
        ),
        in_specs=[VMEM] * (len(parts) + 2),
        out_specs=(VMEM, VMEM),
        compiler_params=pltpu.CompilerParams(vmem_limit_bytes=8 * MIB),
        name="merge",
    )(*parts, residual, gain)


def project_kernel(cycle, hops, shapes, first, last, *refs):
    count = len(cycle)
    refs = list(refs)
    take = lambda n: [refs.pop(0) for _ in range(n)]
    pieces = [take(n) for n in shapes]
    (weight,) = take(1)
    shift_in, sums_in, total_in = [None] * 3 if first else take(3)
    if last:
        (out,) = take(1)
    elif first:
        shift_out, sums_out, total_out = take(3)
    else:
        sums_out, total_out = take(2)
    (lhs,) = take(1)
    total = total_in if last else total_out
    tok = shift_in.shape[0] if not first else shift_out.shape[0]
    width = lhs.shape[2]
    columns = weight.shape[1]
    strip = cut(columns, 512)
    strips = columns // strip

    me = lax.axis_index("col")
    place = pick(me, [cycle.index(c) for c in range(count)])
    ids = [pick(lax.rem(place + hop + count, count), cycle) for hop in hops]

    if not first:
        shift = shift_in[...]
        one, two = sums_in[0], sums_in[1]
    for i, parts in enumerate(pieces):
        whole = jnp.concatenate([part[...].astype(jnp.float32) for part in parts], axis=0)
        values, row = whole[0:tok], whole[tok : tok + 1]
        if first and i == 0:
            shift = jnp.mean(values, axis=1, keepdims=True)
            shift_out[...] = shift
            one = two = jnp.zeros_like(shift)
        dev = values - shift
        one = one + jnp.sum(dev, axis=1, keepdims=True)
        two = two + jnp.sum(dev * dev, axis=1, keepdims=True)
        lhs[i, 0:tok, :] = (dev * row).astype(lhs.dtype)
        lhs[i, tok : tok + EXTRA, :] = jnp.broadcast_to(row, (EXTRA, width)).astype(lhs.dtype)
    if not last:
        sums_out[0] = one
        sums_out[1] = two
    else:
        off = one / (width * count)
        var = jnp.maximum(two / (width * count) - off * off, 0.0)
        scale = 1.0 / jnp.sqrt(var + 1e-06)

    for n in range(strips):
        span = pl.ds(n * strip, strip)
        for i in range(len(hops)):
            rows = pl.ds(pl.multiple_of(ids[i] * width, width), width)
            product = jnp.dot(lhs[i], weight[rows, span], preferred_element_type=jnp.float32)
            if i == 0:
                value = product if first else total_in[:, span] + product
            else:
                value = value + product
        if last:
            out[:, span] = ((value[0:tok] - off * value[tok : tok + 1]) * scale).astype(out.dtype)
        else:
            total[:, span] = value


def project(pieces, hops, weight, state, cycle, last):
    first = state is None
    tok = sum(part.shape[0] for part in pieces[0]) - GAIN
    width = pieces[0][0].shape[1]
    columns = weight.shape[1]
    shift = pltpu.VMEM((tok, 1), jnp.float32)
    sums = pltpu.VMEM((2, tok, 1), jnp.float32)
    total = pltpu.VMEM((tok + EXTRA, columns), jnp.float32)
    flat = [part for parts in pieces for part in parts]
    base = len(flat) + 1
    state = () if first else state
    if last:
        out_shape, aliases = jax.ShapeDtypeStruct((tok, columns), jnp.bfloat16), {}
    elif first:
        out_shape, aliases = (shift, sums, total), {}
    else:
        out_shape, aliases = (sums, total), {base + 1: 0, base + 2: 1}
    got = pl.pallas_call(
        functools.partial(project_kernel, cycle, hops, [len(parts) for parts in pieces], first, last),
        out_shape=out_shape,
        in_specs=[VMEM] * (base + len(state)),
        out_specs=jax.tree.map(lambda _: VMEM, out_shape),
        scratch_shapes=[
            pltpu.VMEM((len(hops), tok + EXTRA, width), jnp.bfloat16),
        ],
        input_output_aliases=aliases,
        compiler_params=pltpu.CompilerParams(vmem_limit_bytes=12 * MIB),
        cost_estimate=pl.CostEstimate(
            flops=2 * len(hops) * (tok + EXTRA) * width * columns,
            bytes_accessed=0,
            transcendentals=0,
        ),
        name="project",
    )(*flat, pltpu.with_memory_space_constraint(weight, pltpu.VMEM), *state)
    if last:
        return got
    return got if first else (state[0], *got)


def solution(mesh):
    rows, cols = mesh.shape["row"], mesh.shape["col"]
    chips_y = rows // CORES
    cycle = cycle_of(cols)
    half = cols // 2

    sibling = [(r, r ^ 1) for r in range(rows)]
    ahead = [(cycle[i], cycle[(i + 1) % cols]) for i in range(cols)]
    behind = [(cycle[(i + 1) % cols], cycle[i]) for i in range(cols)]

    def per_device(hidden, down_weight, residual, gain, qk_weight):
        tok = residual.shape[0]

        cross, same, down_weight = down(hidden, down_weight, tok, chips_y, False)
        parts = []
        for step in range(1, chips_y):
            for blocks, flip in ((same, 0), (cross, 1)):
                move = [(r, ((r + CORES * step) % rows) ^ flip) for r in range(rows)]
                parts.append(lax.ppermute(blocks[step - 1], "row", move))
        give, keep = down(hidden, down_weight, tok, chips_y, True)
        parts += [keep[0], lax.ppermute(give[0], "row", sibling)]
        stream, piece = merge(parts, residual, gain[None, :])

        up, back = piece, piece
        pieces, hops, state = [], [], None
        for step in range(1, half + 1):
            if step == half:
                up, back = up[: tok // 2], back[tok // 2 :]
            up, back = lax.ppermute(up, "col", ahead), lax.ppermute(back, "col", behind)
            if pieces:
                state = project(pieces, hops, qk_weight, state, cycle, False)
                up, back, state = lax.optimization_barrier((up, back, state))
            if step < half:
                pieces, hops = [[up], [back]], [-step, step]
                if step == 1:
                    pieces, hops = [[piece]] + pieces, [0] + hops
            else:
                pieces, hops = [[up, back]], [half]
        return stream, project(pieces, hops, qk_weight, state, cycle, True)

    placed = (P(None, "row"), P("row", "col"), P("row", "col"), P("col"), P(None, "col"))
    return jax.shard_map(
        per_device,
        mesh=mesh,
        in_specs=placed,
        out_specs=(P("row", "col"), P("row", "col")),
        check_vma=False,
    )
```

```python
import functools

import jax
import jax.numpy as jnp
from jax import lax
from jax.experimental import pallas as pl
from jax.experimental.pallas import tpu as pltpu
from jax.sharding import PartitionSpec as P

CORES = 2
EXTRA = 16
GAIN = 8
MIB = 1024 * 1024
HBM = pl.BlockSpec(memory_space=pl.ANY)
VMEM = pl.BlockSpec(memory_space=pltpu.VMEM)


def grid_of(count):
    x = 1
    while (2 * x) * (2 * x) <= count:
        x *= 2
    return count // x, x


def cycle_of(count):
    z, x = grid_of(count)
    walk = [0]
    for i in range(z):
        line = list(range(1, x))
        walk += [i * x + j for j in (line if i % 2 == 0 else line[::-1])]
    return walk + [i * x for i in range(z - 1, 0, -1)]


def pick(index, table):
    value = jnp.int32(table[0])
    for i in range(1, len(table)):
        value = jnp.where(index == i, jnp.int32(table[i]), value)
    return value


def cut(size, most):
    fits = [part for part in range(256, most + 1, 256) if size % part == 0]
    return fits[-1] if fits else size


def down_kernel(chips_y, tok, own, hidden, weight, *refs):
    if own:
        (give, keep), held = refs[:2], weight
    else:
        give, keep, held = refs[:3]
    h_buf, total, sems = refs[-3:]
    parts, depth, _ = held.shape
    me = lax.axis_index("row")
    chip, core = me // CORES, me % CORES
    chips = [0] if own else list(range(1, chips_y))
    block = CORES * tok

    def copies(k):
        span = pl.ds(k * depth, depth)
        for i, step in enumerate(chips):
            start = pl.multiple_of(lax.rem(chip + step, chips_y) * block, block)
            yield pltpu.make_async_copy(
                hidden.at[pl.ds(start, block), span], h_buf.at[k, pl.ds(i * block, block)], sems.at[1 + i, k]
            )
        if not own:
            yield pltpu.make_async_copy(weight.at[span, :], held.at[k], sems.at[0, k])

    for k in range(parts):
        for copy in copies(k):
            copy.start()
    width = held.shape[2]
    strip = cut(width, 256)
    for k in range(parts):
        for copy in copies(k):
            copy.wait()
        for n in range(0, width, strip):
            span = pl.ds(n, strip)
            product = jnp.dot(h_buf[k], held[k, :, span], preferred_element_type=jnp.float32)
            total[:, span] = product if k == 0 else total[:, span] + product
    for i in range(len(chips)):
        for out, which in ((give, 1 - core), (keep, core)):
            start = pl.multiple_of((i * CORES + which) * tok, tok)
            out[i] = total[pl.ds(start, tok), :].astype(out.dtype)


def down(hidden, weight, tok, chips_y, own):
    inner = hidden.shape[1]
    if own:
        parts, depth, width = weight.shape
    else:
        width = weight.shape[1]
        depth = cut(inner, 768)
        parts = inner // depth
    chips = 1 if own else chips_y - 1
    tokens = chips * CORES * tok
    block = pltpu.VMEM((chips, tok, width), jnp.bfloat16)
    out_shape = (block, block) if own else (block, block, pltpu.VMEM((parts, depth, width), jnp.bfloat16))
    return pl.pallas_call(
        functools.partial(down_kernel, chips_y, tok, own),
        out_shape=out_shape,
        in_specs=[HBM, VMEM if own else HBM],
        out_specs=(VMEM,) * len(out_shape),
        scratch_shapes=[
            pltpu.VMEM((parts, tokens, depth), jnp.bfloat16),
            pltpu.VMEM((tokens, width), jnp.float32),
            pltpu.SemaphoreType.DMA((1 + chips, parts)),
        ],
        compiler_params=pltpu.CompilerParams(vmem_limit_bytes=24 * MIB),
        cost_estimate=pl.CostEstimate(
            flops=2 * tokens * inner * width,
            bytes_accessed=2 * inner * (tokens if own else width + tokens),
            transcendentals=0,
        ),
        name="down",
    )(
        pltpu.with_memory_space_constraint(hidden, pltpu.HBM),
        pltpu.with_memory_space_constraint(weight, pltpu.VMEM if own else pltpu.HBM),
    )


def merge_kernel(*refs):
    *parts, residual, gain, stream, upper, lower = refs
    tok, width = residual.shape
    total = parts[0][...].astype(jnp.float32)
    for part in parts[1:]:
        total = total + part[...].astype(jnp.float32)
    value = (residual[...].astype(jnp.float32) + total).astype(stream.dtype)
    stream[...] = value
    upper[...] = value[: tok // 2]
    lower[0 : tok // 2, :] = value[tok // 2 :]
    rows = jnp.broadcast_to(gain[...].astype(jnp.float32), (GAIN, width))
    lower[tok // 2 : tok // 2 + GAIN, :] = rows.astype(lower.dtype)


def merge(parts, residual, gain):
    tok, width = residual.shape
    return pl.pallas_call(
        merge_kernel,
        out_shape=[pltpu.VMEM((n, width), jnp.bfloat16) for n in (tok, tok // 2, tok // 2 + GAIN)],
        in_specs=[VMEM] * (len(parts) + 2),
        out_specs=[VMEM] * 3,
        compiler_params=pltpu.CompilerParams(vmem_limit_bytes=8 * MIB),
        name="merge",
    )(*parts, residual, gain)


def project_kernel(cycle, hops, shapes, first, last, *refs):
    count = len(cycle)
    refs = list(refs)
    take = lambda n: [refs.pop(0) for _ in range(n)]
    pieces = [take(n) for n in shapes]
    (weight,) = take(1)
    shift_in, sums_in, total_in = [None] * 3 if first else take(3)
    if last:
        (out,) = take(1)
    elif first:
        shift_out, sums_out, total_out = take(3)
    else:
        sums_out, total_out = take(2)
    (lhs,) = take(1)
    total = total_in if last else total_out
    tok = shift_in.shape[0] if not first else shift_out.shape[0]
    width = lhs.shape[2]
    columns = weight.shape[1]
    strip = cut(columns, 512)
    strips = columns // strip

    me = lax.axis_index("col")
    place = pick(me, [cycle.index(c) for c in range(count)])
    ids = [pick(lax.rem(place + hop + count, count), cycle) for hop in hops]

    if not first:
        shift = shift_in[...]
        one, two = sums_in[0], sums_in[1]
    for i, parts in enumerate(pieces):
        whole = jnp.concatenate([part[...].astype(jnp.float32) for part in parts], axis=0)
        values, row = whole[0:tok], whole[tok : tok + 1]
        if first and i == 0:
            shift = jnp.mean(values, axis=1, keepdims=True)
            shift_out[...] = shift
            one = two = jnp.zeros_like(shift)
        dev = values - shift
        one = one + jnp.sum(dev, axis=1, keepdims=True)
        two = two + jnp.sum(dev * dev, axis=1, keepdims=True)
        lhs[i, 0:tok, :] = (dev * row).astype(lhs.dtype)
        lhs[i, tok : tok + EXTRA, :] = jnp.broadcast_to(row, (EXTRA, width)).astype(lhs.dtype)
    if not last:
        sums_out[0] = one
        sums_out[1] = two
    else:
        off = one / (width * count)
        var = jnp.maximum(two / (width * count) - off * off, 0.0)
        scale = 1.0 / jnp.sqrt(var + 1e-06)

    for n in range(strips):
        span = pl.ds(n * strip, strip)
        for i in range(len(hops)):
            rows = pl.ds(pl.multiple_of(ids[i] * width, width), width)
            product = jnp.dot(lhs[i], weight[rows, span], preferred_element_type=jnp.float32)
            if i == 0:
                value = product if first else total_in[:, span] + product
            else:
                value = value + product
        if last:
            out[:, span] = ((value[0:tok] - off * value[tok : tok + 1]) * scale).astype(out.dtype)
        else:
            total[:, span] = value


def project(pieces, hops, weight, state, cycle, last):
    first = state is None
    tok = sum(part.shape[0] for part in pieces[0]) - GAIN
    width = pieces[0][0].shape[1]
    columns = weight.shape[1]
    shift = pltpu.VMEM((tok, 1), jnp.float32)
    sums = pltpu.VMEM((2, tok, 1), jnp.float32)
    total = pltpu.VMEM((tok + EXTRA, columns), jnp.float32)
    flat = [part for parts in pieces for part in parts]
    base = len(flat) + 1
    state = () if first else state
    if last:
        out_shape, aliases = jax.ShapeDtypeStruct((tok, columns), jnp.bfloat16), {}
    elif first:
        out_shape, aliases = (shift, sums, total), {}
    else:
        out_shape, aliases = (sums, total), {base + 1: 0, base + 2: 1}
    got = pl.pallas_call(
        functools.partial(project_kernel, cycle, hops, [len(parts) for parts in pieces], first, last),
        out_shape=out_shape,
        in_specs=[VMEM] * (base + len(state)),
        out_specs=jax.tree.map(lambda _: VMEM, out_shape),
        scratch_shapes=[
            pltpu.VMEM((len(hops), tok + EXTRA, width), jnp.bfloat16),
        ],
        input_output_aliases=aliases,
        compiler_params=pltpu.CompilerParams(vmem_limit_bytes=12 * MIB),
        cost_estimate=pl.CostEstimate(
            flops=2 * len(hops) * (tok + EXTRA) * width * columns,
            bytes_accessed=0,
            transcendentals=0,
        ),
        name="project",
    )(*flat, pltpu.with_memory_space_constraint(weight, pltpu.VMEM), *state)
    if last:
        return got
    return got if first else (state[0], *got)


def solution(mesh):
    rows, cols = mesh.shape["row"], mesh.shape["col"]
    chips_y = rows // CORES
    cycle = cycle_of(cols)
    half = cols // 2

    sibling = [(r, r ^ 1) for r in range(rows)]
    ahead = [(cycle[i], cycle[(i + 1) % cols]) for i in range(cols)]
    behind = [(cycle[(i + 1) % cols], cycle[i]) for i in range(cols)]

    def per_device(hidden, down_weight, residual, gain, qk_weight):
        tok = residual.shape[0]

        give, keep, down_weight = down(hidden, down_weight, tok, chips_y, False)
        got = lax.ppermute(give, "row", sibling)
        both = (keep.astype(jnp.float32) + got.astype(jnp.float32)).astype(jnp.bfloat16)
        both, hidden = lax.optimization_barrier((both, hidden))
        parts = []
        for step in range(1, chips_y):
            move = [(r, (r + CORES * step) % rows) for r in range(rows)]
            parts.append(lax.ppermute(both[step - 1], "row", move))
        give, keep = down(hidden, down_weight, tok, chips_y, True)
        parts += [keep[0], lax.ppermute(give[0], "row", sibling)]
        stream, upper, lower = merge(parts, residual, gain[None, :])

        up, back = [upper, lower], [upper, lower]
        pieces, hops, state = [], [], None
        for step in range(1, half):
            for i in range(2):
                up[i], back[i] = lax.ppermute(up[i], "col", ahead), lax.ppermute(back[i], "col", behind)
            if pieces:
                state = project(pieces, hops, qk_weight, state, cycle, False)
                up[1], back[1], state = lax.optimization_barrier((up[1], back[1], state))
            pieces, hops = [list(up), list(back)], [-step, step]
            if step == 1:
                pieces, hops = [[upper, lower]] + pieces, [0] + hops
        opposite = [lax.ppermute(up[0], "col", ahead), lax.ppermute(back[1], "col", behind)]
        state = project(pieces, hops, qk_weight, state, cycle, False)
        opposite, state = lax.optimization_barrier((opposite, state))
        return stream, project([opposite], [half], qk_weight, state, cycle, True)

    placed = (P(None, "row"), P("row", "col"), P("row", "col"), P("col"), P(None, "col"))
    return jax.shard_map(
        per_device,
        mesh=mesh,
        in_specs=placed,
        out_specs=(P("row", "col"), P("row", "col")),
        check_vma=False,
    )
```

```python
import functools

import jax
import jax.numpy as jnp
from jax import lax
from jax.experimental import pallas as pl
from jax.experimental.pallas import tpu as pltpu
from jax.sharding import PartitionSpec as P

CORES = 2
EXTRA = 16
GAIN = 8
MIB = 1024 * 1024
HBM = pl.BlockSpec(memory_space=pl.ANY)
VMEM = pl.BlockSpec(memory_space=pltpu.VMEM)


def grid_of(count):
    x = 1
    while (2 * x) * (2 * x) <= count:
        x *= 2
    return count // x, x


def cycle_of(count):
    z, x = grid_of(count)
    walk = [0]
    for i in range(z):
        line = list(range(1, x))
        walk += [i * x + j for j in (line if i % 2 == 0 else line[::-1])]
    return walk + [i * x for i in range(z - 1, 0, -1)]


def pick(index, table):
    value = jnp.int32(table[0])
    for i in range(1, len(table)):
        value = jnp.where(index == i, jnp.int32(table[i]), value)
    return value


def cut(size, most):
    fits = [part for part in range(256, most + 1, 256) if size % part == 0]
    return fits[-1] if fits else size


def down_kernel(chips_y, tok, own, hidden, weight, *refs):
    if own:
        (give, keep), held = refs[:2], weight
    else:
        give, keep, held = refs[:3]
    h_buf, total, sems = refs[-3:]
    parts, depth, _ = held.shape
    me = lax.axis_index("row")
    chip, core = me // CORES, me % CORES
    chips = [0] if own else list(range(1, chips_y))
    block = CORES * tok

    def copies(k):
        span = pl.ds(k * depth, depth)
        for i, step in enumerate(chips):
            start = pl.multiple_of(lax.rem(chip + step, chips_y) * block, block)
            yield pltpu.make_async_copy(
                hidden.at[pl.ds(start, block), span], h_buf.at[k, pl.ds(i * block, block)], sems.at[1 + i, k]
            )
        if not own:
            yield pltpu.make_async_copy(weight.at[span, :], held.at[k], sems.at[0, k])

    for k in range(parts):
        for copy in copies(k):
            copy.start()
    width = held.shape[2]
    strip = cut(width, 256)
    for k in range(parts):
        for copy in copies(k):
            copy.wait()
        for n in range(0, width, strip):
            span = pl.ds(n, strip)
            product = jnp.dot(h_buf[k], held[k, :, span], preferred_element_type=jnp.float32)
            total[:, span] = product if k == 0 else total[:, span] + product
    for i in range(len(chips)):
        for out, which in ((give, 1 - core), (keep, core)):
            start = pl.multiple_of((i * CORES + which) * tok, tok)
            out[i] = total[pl.ds(start, tok), :].astype(out.dtype)


def down(hidden, weight, tok, chips_y, own):
    inner = hidden.shape[1]
    if own:
        parts, depth, width = weight.shape
    else:
        width = weight.shape[1]
        depth = cut(inner, 768)
        parts = inner // depth
    chips = 1 if own else chips_y - 1
    tokens = chips * CORES * tok
    block = pltpu.VMEM((chips, tok, width), jnp.bfloat16)
    out_shape = (block, block) if own else (block, block, pltpu.VMEM((parts, depth, width), jnp.bfloat16))
    return pl.pallas_call(
        functools.partial(down_kernel, chips_y, tok, own),
        out_shape=out_shape,
        in_specs=[HBM, VMEM if own else HBM],
        out_specs=(VMEM,) * len(out_shape),
        scratch_shapes=[
            pltpu.VMEM((parts, tokens, depth), jnp.bfloat16),
            pltpu.VMEM((tokens, width), jnp.float32),
            pltpu.SemaphoreType.DMA((1 + chips, parts)),
        ],
        compiler_params=pltpu.CompilerParams(vmem_limit_bytes=24 * MIB),
        cost_estimate=pl.CostEstimate(
            flops=2 * tokens * inner * width,
            bytes_accessed=2 * inner * (tokens if own else width + tokens),
            transcendentals=0,
        ),
        name="down",
    )(
        pltpu.with_memory_space_constraint(hidden, pltpu.HBM),
        pltpu.with_memory_space_constraint(weight, pltpu.VMEM if own else pltpu.HBM),
    )


def merge_kernel(others, keep, got, gain, stream, upper, lower):
    tok, width = others.shape
    own = keep[...].astype(jnp.float32) + got[...].astype(jnp.float32)
    value = (others[...] + own).astype(stream.dtype)
    stream[...] = value
    upper[...] = value[: tok // 2]
    lower[0 : tok // 2, :] = value[tok // 2 :]
    rows = jnp.broadcast_to(gain[...].astype(jnp.float32), (GAIN, width))
    lower[tok // 2 : tok // 2 + GAIN, :] = rows.astype(lower.dtype)


def merge(others, keep, got, gain):
    tok, width = others.shape
    return pl.pallas_call(
        merge_kernel,
        out_shape=[pltpu.VMEM((n, width), jnp.bfloat16) for n in (tok, tok // 2, tok // 2 + GAIN)],
        in_specs=[VMEM] * 4,
        out_specs=[VMEM] * 3,
        compiler_params=pltpu.CompilerParams(vmem_limit_bytes=8 * MIB),
        name="merge",
    )(others, keep, got, gain)


def project_kernel(cycle, hops, shapes, first, last, *refs):
    count = len(cycle)
    refs = list(refs)
    take = lambda n: [refs.pop(0) for _ in range(n)]
    pieces = [take(n) for n in shapes]
    (weight,) = take(1)
    shift_in, sums_in, total_in = [None] * 3 if first else take(3)
    if last:
        (out,) = take(1)
    elif first:
        shift_out, sums_out, total_out = take(3)
    else:
        sums_out, total_out = take(2)
    (lhs,) = take(1)
    total = total_in if last else total_out
    tok = shift_in.shape[0] if not first else shift_out.shape[0]
    width = lhs.shape[2]
    columns = weight.shape[1]
    strip = cut(columns, 512)
    strips = columns // strip

    me = lax.axis_index("col")
    place = pick(me, [cycle.index(c) for c in range(count)])
    ids = [pick(lax.rem(place + hop + count, count), cycle) for hop in hops]

    if not first:
        shift = shift_in[...]
        one, two = sums_in[0], sums_in[1]
    for i, parts in enumerate(pieces):
        whole = jnp.concatenate([part[...].astype(jnp.float32) for part in parts], axis=0)
        values, row = whole[0:tok], whole[tok : tok + 1]
        if first and i == 0:
            shift = jnp.mean(values, axis=1, keepdims=True)
            shift_out[...] = shift
            one = two = jnp.zeros_like(shift)
        dev = values - shift
        one = one + jnp.sum(dev, axis=1, keepdims=True)
        two = two + jnp.sum(dev * dev, axis=1, keepdims=True)
        lhs[i, 0:tok, :] = (dev * row).astype(lhs.dtype)
        lhs[i, tok : tok + EXTRA, :] = jnp.broadcast_to(row, (EXTRA, width)).astype(lhs.dtype)
    if not last:
        sums_out[0] = one
        sums_out[1] = two
    else:
        off = one / (width * count)
        var = jnp.maximum(two / (width * count) - off * off, 0.0)
        scale = 1.0 / jnp.sqrt(var + 1e-06)

    for n in range(strips):
        span = pl.ds(n * strip, strip)
        for i in range(len(hops)):
            rows = pl.ds(pl.multiple_of(ids[i] * width, width), width)
            product = jnp.dot(lhs[i], weight[rows, span], preferred_element_type=jnp.float32)
            if i == 0:
                value = product if first else total_in[:, span] + product
            else:
                value = value + product
        if last:
            out[:, span] = ((value[0:tok] - off * value[tok : tok + 1]) * scale).astype(out.dtype)
        else:
            total[:, span] = value


def project(pieces, hops, weight, state, cycle, last):
    first = state is None
    tok = sum(part.shape[0] for part in pieces[0]) - GAIN
    width = pieces[0][0].shape[1]
    columns = weight.shape[1]
    shift = pltpu.VMEM((tok, 1), jnp.float32)
    sums = pltpu.VMEM((2, tok, 1), jnp.float32)
    total = pltpu.VMEM((tok + EXTRA, columns), jnp.float32)
    flat = [part for parts in pieces for part in parts]
    base = len(flat) + 1
    state = () if first else state
    if last:
        out_shape, aliases = jax.ShapeDtypeStruct((tok, columns), jnp.bfloat16), {}
    elif first:
        out_shape, aliases = (shift, sums, total), {}
    else:
        out_shape, aliases = (sums, total), {base + 1: 0, base + 2: 1}
    got = pl.pallas_call(
        functools.partial(project_kernel, cycle, hops, [len(parts) for parts in pieces], first, last),
        out_shape=out_shape,
        in_specs=[VMEM] * (base + len(state)),
        out_specs=jax.tree.map(lambda _: VMEM, out_shape),
        scratch_shapes=[
            pltpu.VMEM((len(hops), tok + EXTRA, width), jnp.bfloat16),
        ],
        input_output_aliases=aliases,
        compiler_params=pltpu.CompilerParams(vmem_limit_bytes=12 * MIB),
        cost_estimate=pl.CostEstimate(
            flops=2 * len(hops) * (tok + EXTRA) * width * columns,
            bytes_accessed=0,
            transcendentals=0,
        ),
        name="project",
    )(*flat, pltpu.with_memory_space_constraint(weight, pltpu.VMEM), *state)
    if last:
        return got
    return got if first else (state[0], *got)


def solution(mesh):
    rows, cols = mesh.shape["row"], mesh.shape["col"]
    chips_y = rows // CORES
    cycle = cycle_of(cols)
    half = cols // 2

    sibling = [(r, r ^ 1) for r in range(rows)]
    ahead = [(cycle[i], cycle[(i + 1) % cols]) for i in range(cols)]
    behind = [(cycle[(i + 1) % cols], cycle[i]) for i in range(cols)]

    def per_device(hidden, down_weight, residual, gain, qk_weight):
        tok = residual.shape[0]

        give, keep, down_weight = down(hidden, down_weight, tok, chips_y, False)
        got = lax.ppermute(give, "row", sibling)
        both = (keep.astype(jnp.float32) + got.astype(jnp.float32)).astype(jnp.bfloat16)
        both, hidden = lax.optimization_barrier((both, hidden))
        others = residual.astype(jnp.float32)
        for step in range(1, chips_y):
            move = [(r, (r + CORES * step) % rows) for r in range(rows)]
            others = others + lax.ppermute(both[step - 1], "row", move).astype(jnp.float32)
        give, keep = down(hidden, down_weight, tok, chips_y, True)
        got = lax.ppermute(give[0], "row", sibling)
        stream, upper, lower = merge(others, keep[0], got, gain[None, :])

        up, back = [upper, lower], [upper, lower]
        pieces, hops, state = [], [], None
        for step in range(1, half):
            for i in range(2):
                up[i], back[i] = lax.ppermute(up[i], "col", ahead), lax.ppermute(back[i], "col", behind)
            if pieces:
                state = project(pieces, hops, qk_weight, state, cycle, False)
                up[1], back[1], state = lax.optimization_barrier((up[1], back[1], state))
            pieces, hops = [list(up), list(back)], [-step, step]
            if step == 1:
                pieces, hops = [[upper, lower]] + pieces, [0] + hops
        opposite = [lax.ppermute(up[0], "col", ahead), lax.ppermute(back[1], "col", behind)]
        state = project(pieces, hops, qk_weight, state, cycle, False)
        opposite, state = lax.optimization_barrier((opposite, state))
        return stream, project([opposite], [half], qk_weight, state, cycle, True)

    placed = (P(None, "row"), P("row", "col"), P("row", "col"), P("col"), P(None, "col"))
    return jax.shard_map(
        per_device,
        mesh=mesh,
        in_specs=placed,
        out_specs=(P("row", "col"), P("row", "col")),
        check_vma=False,
    )
```

```python
import functools

import jax
import jax.numpy as jnp
from jax import lax
from jax.experimental import pallas as pl
from jax.experimental.pallas import tpu as pltpu
from jax.sharding import PartitionSpec as P

CORES = 2
EXTRA = 16
GAIN = 8
MIB = 1024 * 1024
HBM = pl.BlockSpec(memory_space=pl.ANY)
VMEM = pl.BlockSpec(memory_space=pltpu.VMEM)


def grid_of(count):
    x = 1
    while (2 * x) * (2 * x) <= count:
        x *= 2
    return count // x, x


def cycle_of(count):
    z, x = grid_of(count)
    walk = [0]
    for i in range(z):
        line = list(range(1, x))
        walk += [i * x + j for j in (line if i % 2 == 0 else line[::-1])]
    return walk + [i * x for i in range(z - 1, 0, -1)]


def pick(index, table):
    value = jnp.int32(table[0])
    for i in range(1, len(table)):
        value = jnp.where(index == i, jnp.int32(table[i]), value)
    return value


def cut(size, most):
    fits = [part for part in range(256, most + 1, 256) if size % part == 0]
    return fits[-1] if fits else size


def down_kernel(chips_y, tok, own, hidden, weight, *refs):
    if own:
        (give, keep), held = refs[:2], weight
    else:
        give, keep, held = refs[:3]
    h_buf, total, sems = refs[-3:]
    parts, depth, _ = held.shape
    me = lax.axis_index("row")
    chip, core = me // CORES, me % CORES
    chips = [0] if own else list(range(1, chips_y))
    block = CORES * tok

    def copies(k):
        span = pl.ds(pl.multiple_of(k * depth, depth), depth)
        for i, step in enumerate(chips):
            start = pl.multiple_of(lax.rem(chip + step, chips_y) * block, block)
            yield pltpu.make_async_copy(
                hidden.at[pl.ds(start, block), span], h_buf.at[k, pl.ds(i * block, block)], sems.at[1 + i, k]
            )
        if not own:
            yield pltpu.make_async_copy(weight.at[span, :], held.at[k], sems.at[0, k])

    for k in range(parts):
        for copy in copies(k):
            copy.start(priority=1)
    width = held.shape[2]
    strip = cut(width, 256)

    def add(k, first):
        for copy in copies(k):
            copy.wait()
        for n in range(0, width, strip):
            span = pl.ds(n, strip)
            product = jnp.dot(h_buf[k], held[k, :, span], preferred_element_type=jnp.float32)
            total[:, span] = product if first else total[:, span] + product

    add(0, True)
    lax.fori_loop(1, parts, lambda k, _: add(k, False), None)
    for i in range(len(chips)):
        for out, which in ((give, 1 - core), (keep, core)):
            start = pl.multiple_of((i * CORES + which) * tok, tok)
            out[i] = total[pl.ds(start, tok), :].astype(out.dtype)


def down(hidden, weight, tok, chips_y, own):
    inner = hidden.shape[1]
    if own:
        parts, depth, width = weight.shape
    else:
        width = weight.shape[1]
        depth = cut(inner, 768)
        parts = inner // depth
    chips = 1 if own else chips_y - 1
    tokens = chips * CORES * tok
    block = pltpu.VMEM((chips, tok, width), jnp.bfloat16)
    out_shape = (block, block) if own else (block, block, pltpu.VMEM((parts, depth, width), jnp.bfloat16))
    return pl.pallas_call(
        functools.partial(down_kernel, chips_y, tok, own),
        out_shape=out_shape,
        in_specs=[HBM, VMEM if own else HBM],
        out_specs=(VMEM,) * len(out_shape),
        scratch_shapes=[
            pltpu.VMEM((parts, tokens, depth), jnp.bfloat16),
            pltpu.VMEM((tokens, width), jnp.float32),
            pltpu.SemaphoreType.DMA((1 + chips, parts)),
        ],
        compiler_params=pltpu.CompilerParams(vmem_limit_bytes=24 * MIB),
        cost_estimate=pl.CostEstimate(
            flops=2 * tokens * inner * width,
            bytes_accessed=2 * inner * (tokens if own else width + tokens),
            transcendentals=0,
        ),
        name="down",
    )(
        pltpu.with_memory_space_constraint(hidden, pltpu.HBM),
        pltpu.with_memory_space_constraint(weight, pltpu.VMEM if own else pltpu.HBM),
    )


def merge_kernel(others, keep, got, gain, stream, upper, lower):
    tok, width = others.shape
    own = keep[...].astype(jnp.float32) + got[...].astype(jnp.float32)
    value = (others[...] + own).astype(stream.dtype)
    stream[...] = value
    upper[...] = value[: tok // 2]
    lower[0 : tok // 2, :] = value[tok // 2 :]
    rows = jnp.broadcast_to(gain[...].astype(jnp.float32), (GAIN, width))
    lower[tok // 2 : tok // 2 + GAIN, :] = rows.astype(lower.dtype)


def merge(others, keep, got, gain):
    tok, width = others.shape
    return pl.pallas_call(
        merge_kernel,
        out_shape=[pltpu.VMEM((n, width), jnp.bfloat16) for n in (tok, tok // 2, tok // 2 + GAIN)],
        in_specs=[VMEM] * 4,
        out_specs=[VMEM] * 3,
        compiler_params=pltpu.CompilerParams(vmem_limit_bytes=8 * MIB),
        name="merge",
    )(others, keep, got, gain)


def project_kernel(cycle, hops, shapes, first, last, *refs):
    count = len(cycle)
    refs = list(refs)
    take = lambda n: [refs.pop(0) for _ in range(n)]
    pieces = [take(n) for n in shapes]
    (weight,) = take(1)
    shift_in, sums_in, total_in = [None] * 3 if first else take(3)
    if last:
        (out,) = take(1)
    elif first:
        shift_out, sums_out, total_out = take(3)
    else:
        sums_out, total_out = take(2)
    (lhs,) = take(1)
    total = total_in if last else total_out
    tok = shift_in.shape[0] if not first else shift_out.shape[0]
    width = lhs.shape[2]
    columns = weight.shape[1]
    strip = cut(columns, 512)
    strips = columns // strip

    me = lax.axis_index("col")
    place = pick(me, [cycle.index(c) for c in range(count)])
    ids = [pick(lax.rem(place + hop + count, count), cycle) for hop in hops]

    if not first:
        shift = shift_in[...]
        one, two = sums_in[0], sums_in[1]
    for i, parts in enumerate(pieces):
        whole = jnp.concatenate([part[...].astype(jnp.float32) for part in parts], axis=0)
        values, row = whole[0:tok], whole[tok : tok + 1]
        if first and i == 0:
            shift = jnp.mean(values, axis=1, keepdims=True)
            shift_out[...] = shift
            one = two = jnp.zeros_like(shift)
        dev = values - shift
        one = one + jnp.sum(dev, axis=1, keepdims=True)
        two = two + jnp.sum(dev * dev, axis=1, keepdims=True)
        lhs[i, 0:tok, :] = (dev * row).astype(lhs.dtype)
        lhs[i, tok : tok + EXTRA, :] = jnp.broadcast_to(row, (EXTRA, width)).astype(lhs.dtype)
    if not last:
        sums_out[0] = one
        sums_out[1] = two
    else:
        off = one / (width * count)
        var = jnp.maximum(two / (width * count) - off * off, 0.0)
        scale = 1.0 / jnp.sqrt(var + 1e-06)

    for n in range(strips):
        span = pl.ds(n * strip, strip)
        for i in range(len(hops)):
            rows = pl.ds(pl.multiple_of(ids[i] * width, width), width)
            product = jnp.dot(lhs[i], weight[rows, span], preferred_element_type=jnp.float32)
            if i == 0:
                value = product if first else total_in[:, span] + product
            else:
                value = value + product
        if last:
            out[:, span] = ((value[0:tok] - off * value[tok : tok + 1]) * scale).astype(out.dtype)
        else:
            total[:, span] = value


def project(pieces, hops, weight, state, cycle, last):
    first = state is None
    tok = sum(part.shape[0] for part in pieces[0]) - GAIN
    width = pieces[0][0].shape[1]
    columns = weight.shape[1]
    shift = pltpu.VMEM((tok, 1), jnp.float32)
    sums = pltpu.VMEM((2, tok, 1), jnp.float32)
    total = pltpu.VMEM((tok + EXTRA, columns), jnp.float32)
    flat = [part for parts in pieces for part in parts]
    base = len(flat) + 1
    state = () if first else state
    if last:
        out_shape, aliases = jax.ShapeDtypeStruct((tok, columns), jnp.bfloat16), {}
    elif first:
        out_shape, aliases = (shift, sums, total), {}
    else:
        out_shape, aliases = (sums, total), {base + 1: 0, base + 2: 1}
    got = pl.pallas_call(
        functools.partial(project_kernel, cycle, hops, [len(parts) for parts in pieces], first, last),
        out_shape=out_shape,
        in_specs=[VMEM] * (base + len(state)),
        out_specs=jax.tree.map(lambda _: VMEM, out_shape),
        scratch_shapes=[
            pltpu.VMEM((len(hops), tok + EXTRA, width), jnp.bfloat16),
        ],
        input_output_aliases=aliases,
        compiler_params=pltpu.CompilerParams(vmem_limit_bytes=12 * MIB),
        cost_estimate=pl.CostEstimate(
            flops=2 * len(hops) * (tok + EXTRA) * width * columns,
            bytes_accessed=0,
            transcendentals=0,
        ),
        name="project",
    )(*flat, pltpu.with_memory_space_constraint(weight, pltpu.VMEM), *state)
    if last:
        return got
    return got if first else (state[0], *got)


def solution(mesh):
    rows, cols = mesh.shape["row"], mesh.shape["col"]
    chips_y = rows // CORES
    cycle = cycle_of(cols)
    half = cols // 2

    sibling = [(r, r ^ 1) for r in range(rows)]

    def shift(hop):
        return [(cycle[i], cycle[(i + hop) % cols]) for i in range(cols)]

    def per_device(hidden, down_weight, residual, gain, qk_weight):
        tok = residual.shape[0]

        give, keep, down_weight = down(hidden, down_weight, tok, chips_y, False)
        got = lax.ppermute(give, "row", sibling)
        both = (keep.astype(jnp.float32) + got.astype(jnp.float32)).astype(jnp.bfloat16)
        both, hidden = lax.optimization_barrier((both, hidden))
        others = residual.astype(jnp.float32)
        for step in range(1, chips_y):
            move = [(r, (r + CORES * step) % rows) for r in range(rows)]
            others = others + lax.ppermute(both[step - 1], "row", move).astype(jnp.float32)
        give, keep = down(hidden, down_weight, tok, chips_y, True)
        got = lax.ppermute(give[0], "row", sibling)
        stream, upper, lower = merge(others, keep[0], got, gain[None, :])

        up, back = [upper, lower], [upper, lower]
        pieces, hops, state, opposite = [], [], None, None
        for step in range(1, half):
            if step == half - 1:
                opposite = up[0], back[1]
            for i in range(2):
                up[i], back[i] = lax.ppermute(up[i], "col", shift(1)), lax.ppermute(back[i], "col", shift(-1))
            if opposite:
                opposite = lax.ppermute(opposite[0], "col", shift(2)), lax.ppermute(opposite[1], "col", shift(-2))
            if pieces:
                state = project(pieces, hops, qk_weight, state, cycle, False)
                up[1], back[1], state = lax.optimization_barrier((up[1], back[1], state))
            pieces, hops = [list(up), list(back)], [-step, step]
            if step == 1:
                pieces, hops = [[upper, lower]] + pieces, [0] + hops
        state = project(pieces, hops, qk_weight, state, cycle, False)
        return stream, project([opposite], [half], qk_weight, state, cycle, True)

    placed = (P(None, "row"), P("row", "col"), P("row", "col"), P("col"), P(None, "col"))
    return jax.shard_map(
        per_device,
        mesh=mesh,
        in_specs=placed,
        out_specs=(P("row", "col"), P("row", "col")),
        check_vma=False,
    )
```

```python
import functools

import jax
import jax.numpy as jnp
from jax import lax
from jax.experimental import pallas as pl
from jax.experimental.pallas import tpu as pltpu
from jax.sharding import PartitionSpec as P

CORES = 2
EXTRA = 16
GAIN = 8
MIB = 1024 * 1024
HBM = pl.BlockSpec(memory_space=pl.ANY)
VMEM = pl.BlockSpec(memory_space=pltpu.VMEM)


def grid_of(count):
    x = 1
    while (2 * x) * (2 * x) <= count:
        x *= 2
    return count // x, x


def cycle_of(count):
    z, x = grid_of(count)
    walk = [0]
    for i in range(z):
        line = list(range(1, x))
        walk += [i * x + j for j in (line if i % 2 == 0 else line[::-1])]
    return walk + [i * x for i in range(z - 1, 0, -1)]


def pick(index, table):
    value = jnp.int32(table[0])
    for i in range(1, len(table)):
        value = jnp.where(index == i, jnp.int32(table[i]), value)
    return value


def cut(size, most):
    fits = [part for part in range(256, most + 1, 256) if size % part == 0]
    return fits[-1] if fits else size


def down_kernel(chips_y, tok, own, hidden, weight, *refs):
    if own:
        (give, keep), held = refs[:2], weight
    else:
        give, keep, held = refs[:3]
    h_buf, total, sems = refs[-3:]
    parts, depth, _ = held.shape
    me = lax.axis_index("row")
    chip, core = me // CORES, me % CORES
    chips = [0] if own else list(range(1, chips_y))
    block = CORES * tok

    def copies(k):
        span = pl.ds(pl.multiple_of(k * depth, depth), depth)
        for i, step in enumerate(chips):
            start = pl.multiple_of(lax.rem(chip + step, chips_y) * block, block)
            yield pltpu.make_async_copy(
                hidden.at[pl.ds(start, block), span], h_buf.at[k, pl.ds(i * block, block)], sems.at[1 + i, k]
            )
        if not own:
            yield pltpu.make_async_copy(weight.at[span, :], held.at[k], sems.at[0, k])

    for k in range(parts):
        for copy in copies(k):
            copy.start(priority=1)
    for copy in copies(0):
        copy.wait()
    total[...] = jnp.dot(h_buf[0], held[0], preferred_element_type=jnp.float32)

    def body(k, _):
        for copy in copies(k):
            copy.wait()
        total[...] += jnp.dot(h_buf[k], held[k], preferred_element_type=jnp.float32)
        return _

    lax.fori_loop(1, parts, body, 0)
    for i in range(len(chips)):
        for out, which in ((give, 1 - core), (keep, core)):
            start = pl.multiple_of((i * CORES + which) * tok, tok)
            out[i] = total[pl.ds(start, tok), :].astype(out.dtype)


def down(hidden, weight, tok, chips_y, own):
    inner = hidden.shape[1]
    if own:
        parts, depth, width = weight.shape
    else:
        width = weight.shape[1]
        depth = cut(inner, 768)
        parts = inner // depth
    chips = 1 if own else chips_y - 1
    tokens = chips * CORES * tok
    block = pltpu.VMEM((chips, tok, width), jnp.bfloat16)
    out_shape = (block, block) if own else (block, block, pltpu.VMEM((parts, depth, width), jnp.bfloat16))
    return pl.pallas_call(
        functools.partial(down_kernel, chips_y, tok, own),
        out_shape=out_shape,
        in_specs=[HBM, VMEM if own else HBM],
        out_specs=(VMEM,) * len(out_shape),
        scratch_shapes=[
            pltpu.VMEM((parts, tokens, depth), jnp.bfloat16),
            pltpu.VMEM((tokens, width), jnp.float32),
            pltpu.SemaphoreType.DMA((1 + chips, parts)),
        ],
        compiler_params=pltpu.CompilerParams(vmem_limit_bytes=24 * MIB),
        cost_estimate=pl.CostEstimate(
            flops=2 * tokens * inner * width,
            bytes_accessed=2 * inner * (tokens if own else width + tokens),
            transcendentals=0,
        ),
        name="down",
    )(
        pltpu.with_memory_space_constraint(hidden, pltpu.HBM),
        pltpu.with_memory_space_constraint(weight, pltpu.VMEM if own else pltpu.HBM),
    )


def begin(values, row, weight, lhs, shift_ref, sums_ref, total_ref):
    tok, width = values.shape
    shift = jnp.mean(values, axis=1, keepdims=True)
    dev = values - shift
    shift_ref[...] = shift
    sums_ref[0] = jnp.sum(dev, axis=1, keepdims=True)
    sums_ref[1] = jnp.sum(dev * dev, axis=1, keepdims=True)
    lhs[0:tok, :] = (dev * row).astype(lhs.dtype)
    lhs[tok : tok + EXTRA, :] = jnp.broadcast_to(row, (EXTRA, width)).astype(lhs.dtype)
    start = pl.multiple_of(lax.axis_index("col") * width, width)
    columns = weight.shape[1]
    strip = cut(columns, 512)
    for n in range(0, columns, strip):
        span = pl.ds(n, strip)
        total_ref[:, span] = jnp.dot(lhs[...], weight[pl.ds(start, width), span], preferred_element_type=jnp.float32)


def merge_kernel(others, keep, got, gain, weight, piece, shift, sums, total, lhs):
    tok, width = others.shape
    own = keep[...].astype(jnp.float32) + got[...].astype(jnp.float32)
    value = (others[...] + own).astype(piece.dtype)
    row = gain[...].astype(jnp.float32)
    piece[0:tok, :] = value
    piece[tok : tok + GAIN, :] = jnp.broadcast_to(row, (GAIN, width)).astype(piece.dtype)

    @pl.when(lax.axis_index("row") % CORES == 1)
    def _():
        begin(value.astype(jnp.float32), row, weight, lhs, shift, sums, total)


def state_of(tok, columns):
    shapes = (tok, 1), (2, tok, 1), (tok + EXTRA, columns)
    return [pltpu.VMEM(shape, jnp.float32) for shape in shapes]


def merge(others, keep, got, gain, weight):
    tok, width = others.shape
    out_shape = [pltpu.VMEM((tok + GAIN, width), jnp.bfloat16), *state_of(tok, weight.shape[1])]
    piece, *state = pl.pallas_call(
        merge_kernel,
        out_shape=out_shape,
        in_specs=[VMEM] * 5,
        out_specs=[VMEM] * 4,
        scratch_shapes=[pltpu.VMEM((tok + EXTRA, width), jnp.bfloat16)],
        compiler_params=pltpu.CompilerParams(vmem_limit_bytes=12 * MIB),
        name="merge",
    )(others, keep, got, gain, pltpu.with_memory_space_constraint(weight, pltpu.VMEM))
    return piece, state


def settle_kernel(piece, weight, _, __, ___, stream, shift, sums, total, lhs):
    tok = stream.shape[0]
    stream[...] = piece[0:tok, :]

    @pl.when(lax.axis_index("row") % CORES == 0)
    def _():
        row = piece[tok : tok + GAIN, :].astype(jnp.float32)[0:1]
        begin(piece[0:tok, :].astype(jnp.float32), row, weight, lhs, shift, sums, total)


def settle(piece, weight, state):
    tok, width = piece.shape[0] - GAIN, piece.shape[1]
    stream, *state = pl.pallas_call(
        settle_kernel,
        out_shape=[jax.ShapeDtypeStruct((tok, width), jnp.bfloat16), *state_of(tok, weight.shape[1])],
        in_specs=[VMEM] * 5,
        out_specs=[VMEM] * 4,
        scratch_shapes=[pltpu.VMEM((tok + EXTRA, width), jnp.bfloat16)],
        input_output_aliases={2: 1, 3: 2, 4: 3},
        compiler_params=pltpu.CompilerParams(vmem_limit_bytes=12 * MIB),
        cost_estimate=pl.CostEstimate(
            flops=2 * (tok + EXTRA) * width * weight.shape[1], bytes_accessed=2 * tok * width, transcendentals=0
        ),
        name="settle",
    )(piece, pltpu.with_memory_space_constraint(weight, pltpu.VMEM), *state)
    return stream, state


def project_kernel(cycle, hops, shapes, last, *refs):
    count = len(cycle)
    refs = list(refs)
    take = lambda n: [refs.pop(0) for _ in range(n)]
    pieces = [take(n) for n in shapes]
    weight, shift_in, sums_in, total_in = take(4)
    outs, lhs = refs[:-1], refs[-1]
    tok = shift_in.shape[0]
    width = lhs.shape[2]
    columns = weight.shape[1]
    strip = cut(columns, 512)

    me = lax.axis_index("col")
    place = pick(me, [cycle.index(c) for c in range(count)])
    ids = [pick(lax.rem(place + hop + count, count), cycle) for hop in hops]
    one, two = sums_in[0], sums_in[1]
    for i, parts in enumerate(pieces):
        whole = jnp.concatenate([part[...].astype(jnp.float32) for part in parts], axis=0)
        row = whole[tok : tok + 1]
        dev = whole[0:tok] - shift_in[...]
        one = one + jnp.sum(dev, axis=1, keepdims=True)
        two = two + jnp.sum(dev * dev, axis=1, keepdims=True)
        lhs[i, 0:tok, :] = (dev * row).astype(lhs.dtype)
        lhs[i, tok : tok + EXTRA, :] = jnp.broadcast_to(row, (EXTRA, width)).astype(lhs.dtype)
    if last:
        off = one / (width * count)
        var = jnp.maximum(two / (width * count) - off * off, 0.0)
        scale = 1.0 / jnp.sqrt(var + 1e-06)
    else:
        outs[0][0] = one
        outs[0][1] = two

    for n in range(0, columns, strip):
        span = pl.ds(n, strip)
        value = total_in[:, span]
        for i in range(len(hops)):
            rows = pl.ds(pl.multiple_of(ids[i] * width, width), width)
            value = value + jnp.dot(lhs[i], weight[rows, span], preferred_element_type=jnp.float32)
        if last:
            outs[0][:, span] = ((value[0:tok] - off * value[tok : tok + 1]) * scale).astype(outs[0].dtype)
        else:
            outs[1][:, span] = value


def project(pieces, hops, weight, state, cycle, last):
    tok, width = state[0].shape[0], pieces[0][0].shape[1]
    columns = weight.shape[1]
    flat = [part for parts in pieces for part in parts]
    base = len(flat) + 1
    if last:
        out_shape, aliases = [jax.ShapeDtypeStruct((tok, columns), jnp.bfloat16)], {}
    else:
        out_shape, aliases = state_of(tok, columns)[1:], {base + 1: 0, base + 2: 1}
    got = pl.pallas_call(
        functools.partial(project_kernel, cycle, hops, [len(parts) for parts in pieces], last),
        out_shape=out_shape,
        in_specs=[VMEM] * (base + 3),
        out_specs=[VMEM] * len(out_shape),
        scratch_shapes=[pltpu.VMEM((len(hops), tok + EXTRA, width), jnp.bfloat16)],
        input_output_aliases=aliases,
        compiler_params=pltpu.CompilerParams(vmem_limit_bytes=12 * MIB),
        cost_estimate=pl.CostEstimate(
            flops=2 * len(hops) * (tok + EXTRA) * width * columns, bytes_accessed=0, transcendentals=0
        ),
        name="project",
    )(*flat, pltpu.with_memory_space_constraint(weight, pltpu.VMEM), *state)
    return got[0] if last else [state[0], *got]


def solution(mesh):
    rows, cols = mesh.shape["row"], mesh.shape["col"]
    chips_y = rows // CORES
    cycle = cycle_of(cols)
    half = cols // 2

    sibling = [(r, r ^ 1) for r in range(rows)]

    def shift(hop):
        return [(cycle[i], cycle[(i + hop) % cols]) for i in range(cols)]

    def per_device(hidden, down_weight, residual, gain, qk_weight):
        tok = residual.shape[0]

        give, keep, down_weight = down(hidden, down_weight, tok, chips_y, False)
        got = lax.ppermute(give, "row", sibling)
        both = (keep.astype(jnp.float32) + got.astype(jnp.float32)).astype(jnp.bfloat16)
        both, hidden = lax.optimization_barrier((both, hidden))
        others = residual.astype(jnp.float32)
        for step in range(1, chips_y):
            move = [(r, (r + CORES * step) % rows) for r in range(rows)]
            others = others + lax.ppermute(both[step - 1], "row", move).astype(jnp.float32)
        give, keep = down(hidden, down_weight, tok, chips_y, True)
        got = lax.ppermute(give[0], "row", sibling)
        piece, state = merge(others, keep[0], got, gain[None, :], qk_weight)

        up, back, pieces = piece, piece, None
        for step in range(1, half + 1):
            if step == half:
                up, back = up[: tok // 2], back[tok // 2 :]
            up, back = lax.ppermute(up, "col", shift(1)), lax.ppermute(back, "col", shift(-1))
            if step == 1:
                stream, state = settle(piece, qk_weight, state)
            else:
                state = project(pieces, [1 - step, step - 1], qk_weight, state, cycle, False)
            back, state = lax.optimization_barrier((back, state))
            pieces = [[up], [back]]
        return stream, project([[up, back]], [half], qk_weight, state, cycle, True)

    placed = (P(None, "row"), P("row", "col"), P("row", "col"), P("col"), P(None, "col"))
    return jax.shard_map(
        per_device,
        mesh=mesh,
        in_specs=placed,
        out_specs=(P("row", "col"), P("row", "col")),
        check_vma=False,
    )
```

```python
import functools

import jax
import jax.numpy as jnp
from jax import lax
from jax.experimental import pallas as pl
from jax.experimental.pallas import tpu as pltpu
from jax.sharding import PartitionSpec as P

CORES = 2
EXTRA = 16
GAIN = 8
MIB = 1024 * 1024
HBM = pl.BlockSpec(memory_space=pl.ANY)
VMEM = pl.BlockSpec(memory_space=pltpu.VMEM)


def grid_of(count):
    x = 1
    while (2 * x) * (2 * x) <= count:
        x *= 2
    return count // x, x


def cycle_of(count):
    z, x = grid_of(count)
    walk = [0]
    for i in range(z):
        line = list(range(1, x))
        walk += [i * x + j for j in (line if i % 2 == 0 else line[::-1])]
    return walk + [i * x for i in range(z - 1, 0, -1)]


def pick(index, table):
    value = jnp.int32(table[0])
    for i in range(1, len(table)):
        value = jnp.where(index == i, jnp.int32(table[i]), value)
    return value


def cut(size, most):
    fits = [part for part in range(256, most + 1, 256) if size % part == 0]
    return fits[-1] if fits else size


def down_kernel(chips_y, tok, own, hidden, weight, *refs):
    if own:
        (give, keep), held = refs[:2], weight
    else:
        give, keep, held = refs[:3]
    h_buf, total, sems = refs[-3:]
    parts, depth, _ = held.shape
    me = lax.axis_index("row")
    chip, core = me // CORES, me % CORES
    chips = [0] if own else list(range(1, chips_y))
    block = CORES * tok

    def copies(k):
        span = pl.ds(pl.multiple_of(k * depth, depth), depth)
        for i, step in enumerate(chips):
            start = pl.multiple_of(lax.rem(chip + step, chips_y) * block, block)
            yield pltpu.make_async_copy(
                hidden.at[pl.ds(start, block), span], h_buf.at[k, pl.ds(i * block, block)], sems.at[1 + i, k]
            )
        if not own:
            yield pltpu.make_async_copy(weight.at[span, :], held.at[k], sems.at[0, k])

    for k in range(parts):
        for copy in copies(k):
            copy.start(priority=1)
    for copy in copies(0):
        copy.wait()
    total[...] = jnp.dot(h_buf[0], held[0], preferred_element_type=jnp.float32)

    def body(k, _):
        for copy in copies(k):
            copy.wait()
        total[...] += jnp.dot(h_buf[k], held[k], preferred_element_type=jnp.float32)
        return _

    lax.fori_loop(1, parts, body, 0)
    for i in range(len(chips)):
        for out, which in ((give, 1 - core), (keep, core)):
            start = pl.multiple_of((i * CORES + which) * tok, tok)
            out[i] = total[pl.ds(start, tok), :].astype(out.dtype)


def down(hidden, weight, tok, chips_y, own):
    inner = hidden.shape[1]
    if own:
        parts, depth, width = weight.shape
    else:
        width = weight.shape[1]
        depth = cut(inner, 768)
        parts = inner // depth
    chips = 1 if own else chips_y - 1
    tokens = chips * CORES * tok
    block = pltpu.VMEM((chips, tok, width), jnp.bfloat16)
    out_shape = (block, block) if own else (block, block, pltpu.VMEM((parts, depth, width), jnp.bfloat16))
    return pl.pallas_call(
        functools.partial(down_kernel, chips_y, tok, own),
        out_shape=out_shape,
        in_specs=[HBM, VMEM if own else HBM],
        out_specs=(VMEM,) * len(out_shape),
        scratch_shapes=[
            pltpu.VMEM((parts, tokens, depth), jnp.bfloat16),
            pltpu.VMEM((tokens, width), jnp.float32),
            pltpu.SemaphoreType.DMA((1 + chips, parts)),
        ],
        compiler_params=pltpu.CompilerParams(vmem_limit_bytes=24 * MIB),
        cost_estimate=pl.CostEstimate(
            flops=2 * tokens * inner * width,
            bytes_accessed=2 * inner * (tokens if own else width + tokens),
            transcendentals=0,
        ),
        name="down",
    )(
        pltpu.with_memory_space_constraint(hidden, pltpu.HBM),
        pltpu.with_memory_space_constraint(weight, pltpu.VMEM if own else pltpu.HBM),
    )


def begin(values, row, weight, lhs, shift_ref, sums_ref, total_ref):
    tok, width = values.shape
    shift = jnp.mean(values, axis=1, keepdims=True)
    dev = values - shift
    shift_ref[...] = shift
    sums_ref[0] = jnp.sum(dev, axis=1, keepdims=True)
    sums_ref[1] = jnp.sum(dev * dev, axis=1, keepdims=True)
    lhs[0:tok, :] = (dev * row).astype(lhs.dtype)
    lhs[tok : tok + EXTRA, :] = jnp.broadcast_to(row, (EXTRA, width)).astype(lhs.dtype)
    start = pl.multiple_of(lax.axis_index("col") * width, width)
    columns = weight.shape[1]
    strip = cut(columns, 512)
    for n in range(0, columns, strip):
        span = pl.ds(n, strip)
        total_ref[:, span] = jnp.dot(lhs[...], weight[pl.ds(start, width), span], preferred_element_type=jnp.float32)


def merge_kernel(others, keep, got, gain, piece):
    tok, width = others.shape
    own = keep[...].astype(jnp.float32) + got[...].astype(jnp.float32)
    piece[0:tok, :] = (others[...] + own).astype(piece.dtype)
    rows = jnp.broadcast_to(gain[...].astype(jnp.float32), (GAIN, width))
    piece[tok : tok + GAIN, :] = rows.astype(piece.dtype)


def state_of(tok, columns):
    shapes = (tok, 1), (2, tok, 1), (tok + EXTRA, columns)
    return [pltpu.VMEM(shape, jnp.float32) for shape in shapes]


def merge(others, keep, got, gain):
    tok, width = others.shape
    return pl.pallas_call(
        merge_kernel,
        out_shape=pltpu.VMEM((tok + GAIN, width), jnp.bfloat16),
        in_specs=[VMEM] * 4,
        out_specs=VMEM,
        compiler_params=pltpu.CompilerParams(vmem_limit_bytes=8 * MIB),
        name="merge",
    )(others, keep, got, gain)


def settle_kernel(piece, weight, stream, shift, sums, total, lhs):
    tok = stream.shape[0]
    stream[...] = piece[0:tok, :]
    row = piece[tok : tok + GAIN, :].astype(jnp.float32)[0:1]
    begin(piece[0:tok, :].astype(jnp.float32), row, weight, lhs, shift, sums, total)


def settle(piece, weight):
    tok, width = piece.shape[0] - GAIN, piece.shape[1]
    stream, *state = pl.pallas_call(
        settle_kernel,
        out_shape=[jax.ShapeDtypeStruct((tok, width), jnp.bfloat16), *state_of(tok, weight.shape[1])],
        in_specs=[VMEM] * 2,
        out_specs=[VMEM] * 4,
        scratch_shapes=[pltpu.VMEM((tok + EXTRA, width), jnp.bfloat16)],
        compiler_params=pltpu.CompilerParams(vmem_limit_bytes=12 * MIB),
        cost_estimate=pl.CostEstimate(
            flops=2 * (tok + EXTRA) * width * weight.shape[1], bytes_accessed=2 * tok * width, transcendentals=0
        ),
        name="settle",
    )(piece, pltpu.with_memory_space_constraint(weight, pltpu.VMEM))
    return stream, state


def project_kernel(cycle, hops, last, *refs):
    count = len(cycle)
    pieces, refs = refs[: len(hops)], refs[len(hops) :]
    weight, shift_in, sums_in, total_in, *outs, lhs = refs
    tok = shift_in.shape[0]
    width = lhs.shape[2]
    columns = weight.shape[1]
    strip = cut(columns, 512)

    me = lax.axis_index("col")
    place = pick(me, [cycle.index(c) for c in range(count)])
    turn = 2 * (lax.axis_index("row") % CORES) - 1
    ids = [pick(lax.rem(place + turn * hop + count, count), cycle) for hop in hops]
    one, two = sums_in[0], sums_in[1]
    for i, piece in enumerate(pieces):
        whole = piece[...].astype(jnp.float32)
        row = whole[tok : tok + 1]
        dev = whole[0:tok] - shift_in[...]
        one = one + jnp.sum(dev, axis=1, keepdims=True)
        two = two + jnp.sum(dev * dev, axis=1, keepdims=True)
        lhs[i, 0:tok, :] = (dev * row).astype(lhs.dtype)
        lhs[i, tok : tok + EXTRA, :] = jnp.broadcast_to(row, (EXTRA, width)).astype(lhs.dtype)
    if last:
        off = one / (width * count)
        var = jnp.maximum(two / (width * count) - off * off, 0.0)
        scale = 1.0 / jnp.sqrt(var + 1e-06)
    else:
        outs[0][0] = one
        outs[0][1] = two

    for n in range(0, columns, strip):
        span = pl.ds(n, strip)
        value = total_in[:, span]
        for i in range(len(hops)):
            rows = pl.ds(pl.multiple_of(ids[i] * width, width), width)
            value = value + jnp.dot(lhs[i], weight[rows, span], preferred_element_type=jnp.float32)
        if last:
            outs[0][:, span] = ((value[0:tok] - off * value[tok : tok + 1]) * scale).astype(outs[0].dtype)
        else:
            outs[1][:, span] = value


def project(pieces, hops, weight, state, cycle, last):
    tok, width = state[0].shape[0], pieces[0].shape[1]
    columns = weight.shape[1]
    base = len(pieces) + 1
    if last:
        out_shape, aliases = [jax.ShapeDtypeStruct((tok, columns), jnp.bfloat16)], {}
    else:
        out_shape, aliases = state_of(tok, columns)[1:], {base + 1: 0, base + 2: 1}
    got = pl.pallas_call(
        functools.partial(project_kernel, cycle, hops, last),
        out_shape=out_shape,
        in_specs=[VMEM] * (base + 3),
        out_specs=[VMEM] * len(out_shape),
        scratch_shapes=[pltpu.VMEM((len(hops), tok + EXTRA, width), jnp.bfloat16)],
        input_output_aliases=aliases,
        compiler_params=pltpu.CompilerParams(vmem_limit_bytes=12 * MIB),
        cost_estimate=pl.CostEstimate(
            flops=2 * len(hops) * (tok + EXTRA) * width * columns, bytes_accessed=0, transcendentals=0
        ),
        name="project",
    )(*pieces, pltpu.with_memory_space_constraint(weight, pltpu.VMEM), *state)
    return got[0] if last else [state[0], *got]


def solution(mesh):
    rows, cols = mesh.shape["row"], mesh.shape["col"]
    chips_y = rows // CORES
    cycle = cycle_of(cols)
    half = cols // 2

    sibling = [(r, r ^ 1) for r in range(rows)]

    def shift(hop):
        pairs = []
        for r in range(rows):
            turn = hop * (2 * (r % CORES) - 1)
            pairs += [(r * cols + cycle[i], r * cols + cycle[(i + turn) % cols]) for i in range(cols)]
        return pairs

    def per_device(hidden, down_weight, residual, gain, qk_weight):
        tok = residual.shape[0]

        give, keep, down_weight = down(hidden, down_weight, tok, chips_y, False)
        got = lax.ppermute(give, "row", sibling)
        both = (keep.astype(jnp.float32) + got.astype(jnp.float32)).astype(jnp.bfloat16)
        both, hidden = lax.optimization_barrier((both, hidden))
        others = residual.astype(jnp.float32)
        for step in range(1, chips_y):
            move = [(r, (r + CORES * step) % rows) for r in range(rows)]
            others = others + lax.ppermute(both[step - 1], "row", move).astype(jnp.float32)
        give, keep = down(hidden, down_weight, tok, chips_y, True)
        got = lax.ppermute(give[0], "row", sibling)
        piece = merge(others, keep[0], got, gain[None, :])

        first = lax.ppermute(piece, ("row", "col"), shift(1))
        stream, state = settle(piece, qk_weight)
        piece, state = lax.optimization_barrier((piece, state))
        second, late = lax.ppermute(piece, ("row", "col"), shift(-1)), []
        for step in range(1, half):
            onward = lax.ppermute(first, ("row", "col"), shift(1))
            pieces, hops = [first, *late], [-step, step - 1][: 1 + len(late)]
            state = project(pieces, hops, qk_weight, state, cycle, False)
            late, first = [second], onward
            if step + 1 < half:
                second, state = lax.optimization_barrier((second, state))
                late = [second]
                second = lax.ppermute(second, ("row", "col"), shift(-1))
        state = project(late, [half - 1], qk_weight, state, cycle, False)
        return stream, project([first], [half], qk_weight, state, cycle, True)

    placed = (P(None, "row"), P("row", "col"), P("row", "col"), P("col"), P(None, "col"))
    return jax.shard_map(
        per_device,
        mesh=mesh,
        in_specs=placed,
        out_specs=(P("row", "col"), P("row", "col")),
        check_vma=False,
    )
```

```python
import functools

import jax
import jax.numpy as jnp
from jax import lax
from jax.experimental import pallas as pl
from jax.experimental.pallas import tpu as pltpu
from jax.sharding import PartitionSpec as P

CORES = 2
EXTRA = 16
GAIN = 8
MIB = 1024 * 1024
HBM = pl.BlockSpec(memory_space=pl.ANY)
VMEM = pl.BlockSpec(memory_space=pltpu.VMEM)


def grid_of(count):
    x = 1
    while (2 * x) * (2 * x) <= count:
        x *= 2
    return count // x, x


def cycle_of(count):
    z, x = grid_of(count)
    walk = [0]
    for i in range(z):
        line = list(range(1, x))
        walk += [i * x + j for j in (line if i % 2 == 0 else line[::-1])]
    return walk + [i * x for i in range(z - 1, 0, -1)]


def pick(index, table):
    value = jnp.int32(table[0])
    for i in range(1, len(table)):
        value = jnp.where(index == i, jnp.int32(table[i]), value)
    return value


def cut(size, most):
    fits = [part for part in range(256, most + 1, 256) if size % part == 0]
    return fits[-1] if fits else size


def down_kernel(chips_y, tok, parts, own, hidden, weight, *refs):
    if own:
        (give, keep), held = refs[:2], weight
    else:
        give, keep, held = refs[:3]
    h_buf, total, sems = refs[-3:]
    depth = held.shape[0] // parts
    me = lax.axis_index("row")
    chip, core = me // CORES, me % CORES
    chips = [0] if own else list(range(1, chips_y))
    block = CORES * tok

    def span(k):
        return pl.ds(pl.multiple_of(k * depth, depth), depth)

    def copies(k):
        for i, step in enumerate(chips):
            start = pl.multiple_of(lax.rem(chip + step, chips_y) * block, block)
            yield pltpu.make_async_copy(
                hidden.at[pl.ds(start, block), span(k)], h_buf.at[k, pl.ds(i * block, block)], sems.at[1 + i, k]
            )
        if not own:
            yield pltpu.make_async_copy(weight.at[span(k), :], held.at[span(k), :], sems.at[0, k])

    for k in range(parts):
        for copy in copies(k):
            copy.start(priority=1)
    for copy in copies(0):
        copy.wait()
    total[...] = jnp.dot(h_buf[0], held[span(0), :], preferred_element_type=jnp.float32)

    def body(k, _):
        for copy in copies(k):
            copy.wait()
        total[...] += jnp.dot(h_buf[k], held[span(k), :], preferred_element_type=jnp.float32)
        return _

    lax.fori_loop(1, parts, body, 0)
    for i in range(len(chips)):
        for out, which in ((give, 1 - core), (keep, core)):
            start = pl.multiple_of((i * CORES + which) * tok, tok)
            out[i] = total[pl.ds(start, tok), :].astype(out.dtype)


def down(hidden, weight, tok, chips_y, own):
    inner, width = weight.shape
    depth = cut(inner, 3072 if own else 1536)
    parts = inner // depth
    chips = 1 if own else chips_y - 1
    tokens = chips * CORES * tok
    block = pltpu.VMEM((chips, tok, width), jnp.bfloat16)
    out_shape = (block, block) if own else (block, block, pltpu.VMEM((inner, width), jnp.bfloat16))
    return pl.pallas_call(
        functools.partial(down_kernel, chips_y, tok, parts, own),
        out_shape=out_shape,
        in_specs=[HBM, VMEM if own else HBM],
        out_specs=(VMEM,) * len(out_shape),
        scratch_shapes=[
            pltpu.VMEM((parts, tokens, depth), jnp.bfloat16),
            pltpu.VMEM((tokens, width), jnp.float32),
            pltpu.SemaphoreType.DMA((1 + chips, parts)),
        ],
        compiler_params=pltpu.CompilerParams(vmem_limit_bytes=24 * MIB),
        cost_estimate=pl.CostEstimate(
            flops=2 * tokens * inner * width,
            bytes_accessed=2 * inner * (tokens if own else width + tokens),
            transcendentals=0,
        ),
        name="down",
    )(
        pltpu.with_memory_space_constraint(hidden, pltpu.HBM),
        pltpu.with_memory_space_constraint(weight, pltpu.VMEM if own else pltpu.HBM),
    )


def merge_kernel(others, keep, got, gain, upper, lower):
    tok, width = others.shape
    own = keep[...].astype(jnp.float32) + got[...].astype(jnp.float32)
    value = (others[...] + own).astype(upper.dtype)
    upper[...] = value[: tok // 2]
    lower[0 : tok // 2, :] = value[tok // 2 :]
    rows = jnp.broadcast_to(gain[...].astype(jnp.float32), (GAIN, width))
    lower[tok // 2 : tok // 2 + GAIN, :] = rows.astype(lower.dtype)


def merge(others, keep, got, gain):
    tok, width = others.shape
    return pl.pallas_call(
        merge_kernel,
        out_shape=[pltpu.VMEM((n, width), jnp.bfloat16) for n in (tok // 2, tok // 2 + GAIN)],
        in_specs=[VMEM] * 4,
        out_specs=[VMEM] * 2,
        compiler_params=pltpu.CompilerParams(vmem_limit_bytes=8 * MIB),
        name="merge",
    )(others, keep, got, gain)


def project_kernel(cycle, hops, shapes, first, last, *refs):
    count = len(cycle)
    refs = list(refs)
    take = lambda n: [refs.pop(0) for _ in range(n)]
    pieces = [take(n) for n in shapes]
    (weight,) = take(1)
    shift_in, sums_in, total_in = [None] * 3 if first else take(3)
    if last:
        (out,) = take(1)
    elif first:
        stream, shift_out, sums_out, total_out = take(4)
    else:
        sums_out, total_out = take(2)
    (lhs,) = take(1)
    total = total_in if last else total_out
    tok = shift_in.shape[0] if not first else shift_out.shape[0]
    width = lhs.shape[2]
    columns = weight.shape[1]
    strip = cut(columns, 512)
    strips = columns // strip

    me = lax.axis_index("col")
    place = pick(me, [cycle.index(c) for c in range(count)])
    ids = [pick(lax.rem(place + hop + count, count), cycle) for hop in hops]

    if not first:
        shift = shift_in[...]
        one, two = sums_in[0], sums_in[1]
    for i, parts in enumerate(pieces):
        whole = jnp.concatenate([part[...].astype(jnp.float32) for part in parts], axis=0)
        values, row = whole[0:tok], whole[tok : tok + 1]
        if first and i == 0:
            stream[...] = values.astype(stream.dtype)
            shift = jnp.mean(values, axis=1, keepdims=True)
            shift_out[...] = shift
            one = two = jnp.zeros_like(shift)
        dev = values - shift
        one = one + jnp.sum(dev, axis=1, keepdims=True)
        two = two + jnp.sum(dev * dev, axis=1, keepdims=True)
        lhs[i, 0:tok, :] = (dev * row).astype(lhs.dtype)
        lhs[i, tok : tok + EXTRA, :] = jnp.broadcast_to(row, (EXTRA, width)).astype(lhs.dtype)
    if not last:
        sums_out[0] = one
        sums_out[1] = two
    else:
        off = one / (width * count)
        var = jnp.maximum(two / (width * count) - off * off, 0.0)
        scale = 1.0 / jnp.sqrt(var + 1e-06)

    for n in range(strips):
        span = pl.ds(n * strip, strip)
        for i in range(len(hops)):
            rows = pl.ds(pl.multiple_of(ids[i] * width, width), width)
            product = jnp.dot(lhs[i], weight[rows, span], preferred_element_type=jnp.float32)
            if i == 0:
                value = product if first else total_in[:, span] + product
            else:
                value = value + product
        if last:
            out[:, span] = ((value[0:tok] - off * value[tok : tok + 1]) * scale).astype(out.dtype)
        else:
            total[:, span] = value


def project(pieces, hops, weight, state, cycle, last):
    first = state is None
    tok = sum(part.shape[0] for part in pieces[0]) - GAIN
    width = pieces[0][0].shape[1]
    columns = weight.shape[1]
    shift = pltpu.VMEM((tok, 1), jnp.float32)
    sums = pltpu.VMEM((2, tok, 1), jnp.float32)
    total = pltpu.VMEM((tok + EXTRA, columns), jnp.float32)
    flat = [part for parts in pieces for part in parts]
    base = len(flat) + 1
    state = () if first else state
    if last:
        out_shape, aliases = jax.ShapeDtypeStruct((tok, columns), jnp.bfloat16), {}
    elif first:
        out_shape, aliases = (jax.ShapeDtypeStruct((tok, width), jnp.bfloat16), shift, sums, total), {}
    else:
        out_shape, aliases = (sums, total), {base + 1: 0, base + 2: 1}
    got = pl.pallas_call(
        functools.partial(project_kernel, cycle, hops, [len(parts) for parts in pieces], first, last),
        out_shape=out_shape,
        in_specs=[VMEM] * (base + len(state)),
        out_specs=jax.tree.map(lambda _: VMEM, out_shape),
        scratch_shapes=[
            pltpu.VMEM((len(hops), tok + EXTRA, width), jnp.bfloat16),
        ],
        input_output_aliases=aliases,
        compiler_params=pltpu.CompilerParams(vmem_limit_bytes=12 * MIB),
        cost_estimate=pl.CostEstimate(
            flops=2 * len(hops) * (tok + EXTRA) * width * columns,
            bytes_accessed=0,
            transcendentals=0,
        ),
        name="project",
    )(*flat, pltpu.with_memory_space_constraint(weight, pltpu.VMEM), *state)
    if last:
        return got
    return (got[0], got[1:]) if first else (state[0], *got)


def solution(mesh):
    rows, cols = mesh.shape["row"], mesh.shape["col"]
    chips_y = rows // CORES
    cycle = cycle_of(cols)
    half = cols // 2

    sibling = [(r, r ^ 1) for r in range(rows)]

    def shift(hop):
        return [(cycle[i], cycle[(i + hop) % cols]) for i in range(cols)]

    def per_device(hidden, down_weight, residual, gain, qk_weight):
        tok = residual.shape[0]

        give, keep, down_weight = down(hidden, down_weight, tok, chips_y, False)
        got = lax.ppermute(give, "row", sibling)
        both = (keep.astype(jnp.float32) + got.astype(jnp.float32)).astype(jnp.bfloat16)
        both, hidden = lax.optimization_barrier((both, hidden))
        others = residual.astype(jnp.float32)
        for step in range(1, chips_y):
            move = [(r, (r + CORES * step) % rows) for r in range(rows)]
            others = others + lax.ppermute(both[step - 1], "row", move).astype(jnp.float32)
        give, keep = down(hidden, down_weight, tok, chips_y, True)
        got = lax.ppermute(give[0], "row", sibling)
        upper, lower = merge(others, keep[0], got, gain[None, :])

        up, back = [upper, lower], [upper, lower]
        pieces, hops, state, opposite = [], [], None, None
        for step in range(1, half):
            if step == half - 1:
                opposite = up[0], back[1]
            for i in range(2):
                up[i], back[i] = lax.ppermute(up[i], "col", shift(1)), lax.ppermute(back[i], "col", shift(-1))
            if opposite:
                opposite = lax.ppermute(opposite[0], "col", shift(2)), lax.ppermute(opposite[1], "col", shift(-2))
            if pieces:
                state = project(pieces, hops, qk_weight, state, cycle, False)
                if step == 2:
                    stream, state = state
                up[1], back[1], state = lax.optimization_barrier((up[1], back[1], state))
            pieces, hops = [list(up), list(back)], [-step, step]
            if step == 1:
                pieces, hops = [[upper, lower]] + pieces, [0] + hops
        state = project(pieces, hops, qk_weight, state, cycle, False)
        return stream, project([opposite], [half], qk_weight, state, cycle, True)

    placed = (P(None, "row"), P("row", "col"), P("row", "col"), P("col"), P(None, "col"))
    return jax.shard_map(
        per_device,
        mesh=mesh,
        in_specs=placed,
        out_specs=(P("row", "col"), P("row", "col")),
        check_vma=False,
    )
```

```python
import functools

import jax
import jax.numpy as jnp
from jax import lax
from jax.experimental import pallas as pl
from jax.experimental.pallas import tpu as pltpu
from jax.sharding import PartitionSpec as P

CORES = 2
EXTRA = 16
GAIN = 8
MIB = 1024 * 1024
HBM = pl.BlockSpec(memory_space=pl.ANY)
VMEM = pl.BlockSpec(memory_space=pltpu.VMEM)


def grid_of(count):
    x = 1
    while (2 * x) * (2 * x) <= count:
        x *= 2
    return count // x, x


def cycle_of(count):
    z, x = grid_of(count)
    walk = [0]
    for i in range(z):
        line = list(range(1, x))
        walk += [i * x + j for j in (line if i % 2 == 0 else line[::-1])]
    return walk + [i * x for i in range(z - 1, 0, -1)]


def pick(index, table):
    value = jnp.int32(table[0])
    for i in range(1, len(table)):
        value = jnp.where(index == i, jnp.int32(table[i]), value)
    return value


def cut(size, most):
    fits = [part for part in range(256, most + 1, 256) if size % part == 0]
    return fits[-1] if fits else size


def down_kernel(chips_y, tok, parts, own, hidden, weight, *refs):
    if own:
        (give, keep), held = refs[:2], weight
    else:
        give, keep, held = refs[:3]
    h_buf, total, sems = refs[-3:]
    depth = held.shape[0] // parts
    me = lax.axis_index("row")
    chip, core = me // CORES, me % CORES
    chips = [0] if own else list(range(1, chips_y))
    block = CORES * tok

    def span(k):
        return pl.ds(pl.multiple_of(k * depth, depth), depth)

    def copies(k):
        for i, step in enumerate(chips):
            start = pl.multiple_of(lax.rem(chip + step, chips_y) * block, block)
            yield pltpu.make_async_copy(
                hidden.at[pl.ds(start, block), span(k)], h_buf.at[k, pl.ds(i * block, block)], sems.at[1 + i, k]
            )
        if not own:
            yield pltpu.make_async_copy(weight.at[span(k), :], held.at[span(k), :], sems.at[0, k])

    for k in range(parts):
        for copy in copies(k):
            copy.start(priority=1)
    tokens, width = total.shape
    total[...] = jnp.zeros_like(total)

    def body(k, _):
        for copy in copies(k):
            copy.wait()
        for row in range(0, tokens, 128):
            for column in range(0, width, 512):
                place = pl.ds(row, 128), pl.ds(column, min(512, width - column))
                total[place] += jnp.dot(h_buf[k, place[0], :], held[span(k), place[1]], preferred_element_type=jnp.float32)
        return _

    lax.fori_loop(0, parts, body, 0)
    for i in range(len(chips)):
        for out, which in ((give, 1 - core), (keep, core)):
            start = pl.multiple_of((i * CORES + which) * tok, tok)
            out[i] = total[pl.ds(start, tok), :].astype(out.dtype)


def down(hidden, weight, tok, chips_y, own):
    inner, width = weight.shape
    depth = cut(inner, 1536)
    parts = inner // depth
    chips = 1 if own else chips_y - 1
    tokens = chips * CORES * tok
    block = pltpu.VMEM((chips, tok, width), jnp.bfloat16)
    out_shape = (block, block) if own else (block, block, pltpu.VMEM((inner, width), jnp.bfloat16))
    return pl.pallas_call(
        functools.partial(down_kernel, chips_y, tok, parts, own),
        out_shape=out_shape,
        in_specs=[HBM, VMEM if own else HBM],
        out_specs=(VMEM,) * len(out_shape),
        scratch_shapes=[
            pltpu.VMEM((parts, tokens, depth), jnp.bfloat16),
            pltpu.VMEM((tokens, width), jnp.float32),
            pltpu.SemaphoreType.DMA((1 + chips, parts)),
        ],
        compiler_params=pltpu.CompilerParams(vmem_limit_bytes=24 * MIB),
        cost_estimate=pl.CostEstimate(
            flops=2 * tokens * inner * width,
            bytes_accessed=2 * inner * (tokens if own else width + tokens),
            transcendentals=0,
        ),
        name="down",
    )(
        pltpu.with_memory_space_constraint(hidden, pltpu.HBM),
        pltpu.with_memory_space_constraint(weight, pltpu.VMEM if own else pltpu.HBM),
    )


def merge_kernel(others, keep, got, gain, upper, lower):
    tok, width = others.shape
    own = keep[...].astype(jnp.float32) + got[...].astype(jnp.float32)
    value = (others[...] + own).astype(upper.dtype)
    upper[...] = value[: tok // 2]
    lower[0 : tok // 2, :] = value[tok // 2 :]
    rows = jnp.broadcast_to(gain[...].astype(jnp.float32), (GAIN, width))
    lower[tok // 2 : tok // 2 + GAIN, :] = rows.astype(lower.dtype)


def merge(others, keep, got, gain):
    tok, width = others.shape
    return pl.pallas_call(
        merge_kernel,
        out_shape=[pltpu.VMEM((n, width), jnp.bfloat16) for n in (tok // 2, tok // 2 + GAIN)],
        in_specs=[VMEM] * 4,
        out_specs=[VMEM] * 2,
        compiler_params=pltpu.CompilerParams(vmem_limit_bytes=8 * MIB),
        name="merge",
    )(others, keep, got, gain)


def project_kernel(cycle, hops, shapes, first, last, *refs):
    count = len(cycle)
    refs = list(refs)
    take = lambda n: [refs.pop(0) for _ in range(n)]
    pieces = [take(n) for n in shapes]
    (weight,) = take(1)
    shift_in, sums_in, total_in = [None] * 3 if first else take(3)
    if last:
        (out,) = take(1)
    elif first:
        stream, shift_out, sums_out, total_out = take(4)
    else:
        sums_out, total_out = take(2)
    (lhs,) = take(1)
    total = total_in if last else total_out
    tok = shift_in.shape[0] if not first else shift_out.shape[0]
    width = lhs.shape[2]
    columns = weight.shape[1]
    strip = cut(columns, 512)
    strips = columns // strip

    me = lax.axis_index("col")
    place = pick(me, [cycle.index(c) for c in range(count)])
    ids = [pick(lax.rem(place + hop + count, count), cycle) for hop in hops]

    if not first:
        shift = shift_in[...]
        one, two = sums_in[0], sums_in[1]
    for i, parts in enumerate(pieces):
        whole = jnp.concatenate([part[...].astype(jnp.float32) for part in parts], axis=0)
        values, row = whole[0:tok], whole[tok : tok + 1]
        if first and i == 0:
            stream[...] = values.astype(stream.dtype)
            shift = jnp.mean(values, axis=1, keepdims=True)
            shift_out[...] = shift
            one = two = jnp.zeros_like(shift)
        dev = values - shift
        one = one + jnp.sum(dev, axis=1, keepdims=True)
        two = two + jnp.sum(dev * dev, axis=1, keepdims=True)
        lhs[i, 0:tok, :] = (dev * row).astype(lhs.dtype)
        lhs[i, tok : tok + EXTRA, :] = jnp.broadcast_to(row, (EXTRA, width)).astype(lhs.dtype)
    if not last:
        sums_out[0] = one
        sums_out[1] = two
    else:
        off = one / (width * count)
        var = jnp.maximum(two / (width * count) - off * off, 0.0)
        scale = 1.0 / jnp.sqrt(var + 1e-06)

    for n in range(strips):
        span = pl.ds(n * strip, strip)
        for i in range(len(hops)):
            rows = pl.ds(pl.multiple_of(ids[i] * width, width), width)
            product = jnp.dot(lhs[i], weight[rows, span], preferred_element_type=jnp.float32)
            if i == 0:
                value = product if first else total_in[:, span] + product
            else:
                value = value + product
        if last:
            out[:, span] = ((value[0:tok] - off * value[tok : tok + 1]) * scale).astype(out.dtype)
        else:
            total[:, span] = value


def project(pieces, hops, weight, state, cycle, last):
    first = state is None
    tok = sum(part.shape[0] for part in pieces[0]) - GAIN
    width = pieces[0][0].shape[1]
    columns = weight.shape[1]
    shift = pltpu.VMEM((tok, 1), jnp.float32)
    sums = pltpu.VMEM((2, tok, 1), jnp.float32)
    total = pltpu.VMEM((tok + EXTRA, columns), jnp.float32)
    flat = [part for parts in pieces for part in parts]
    base = len(flat) + 1
    state = () if first else state
    if last:
        out_shape, aliases = jax.ShapeDtypeStruct((tok, columns), jnp.bfloat16), {}
    elif first:
        out_shape, aliases = (jax.ShapeDtypeStruct((tok, width), jnp.bfloat16), shift, sums, total), {}
    else:
        out_shape, aliases = (sums, total), {base + 1: 0, base + 2: 1}
    got = pl.pallas_call(
        functools.partial(project_kernel, cycle, hops, [len(parts) for parts in pieces], first, last),
        out_shape=out_shape,
        in_specs=[VMEM] * (base + len(state)),
        out_specs=jax.tree.map(lambda _: VMEM, out_shape),
        scratch_shapes=[
            pltpu.VMEM((len(hops), tok + EXTRA, width), jnp.bfloat16),
        ],
        input_output_aliases=aliases,
        compiler_params=pltpu.CompilerParams(vmem_limit_bytes=12 * MIB),
        cost_estimate=pl.CostEstimate(
            flops=2 * len(hops) * (tok + EXTRA) * width * columns,
            bytes_accessed=0,
            transcendentals=0,
        ),
        name="project",
    )(*flat, pltpu.with_memory_space_constraint(weight, pltpu.VMEM), *state)
    if last:
        return got
    return (got[0], got[1:]) if first else (state[0], *got)


def solution(mesh):
    rows, cols = mesh.shape["row"], mesh.shape["col"]
    chips_y = rows // CORES
    cycle = cycle_of(cols)
    half = cols // 2

    sibling = [(r, r ^ 1) for r in range(rows)]

    def shift(hop):
        return [(cycle[i], cycle[(i + hop) % cols]) for i in range(cols)]

    def per_device(hidden, down_weight, residual, gain, qk_weight):
        tok = residual.shape[0]

        give, keep, down_weight = down(hidden, down_weight, tok, chips_y, False)
        got = lax.ppermute(give, "row", sibling)
        both = (keep.astype(jnp.float32) + got.astype(jnp.float32)).astype(jnp.bfloat16)
        both, hidden = lax.optimization_barrier((both, hidden))
        others = residual.astype(jnp.float32)
        for step in range(1, chips_y):
            move = [(r, (r + CORES * step) % rows) for r in range(rows)]
            others = others + lax.ppermute(both[step - 1], "row", move).astype(jnp.float32)
        give, keep = down(hidden, down_weight, tok, chips_y, True)
        got = lax.ppermute(give[0], "row", sibling)
        upper, lower = merge(others, keep[0], got, gain[None, :])

        up, back = [upper, lower], [upper, lower]
        pieces, opposite = [[upper, lower]], None
        for step in range(1, half):
            if step == half - 1:
                opposite = up[0], back[1]
            for i in range(2):
                up[i], back[i] = lax.ppermute(up[i], "col", shift(1)), lax.ppermute(back[i], "col", shift(-1))
            if opposite:
                opposite = lax.ppermute(opposite[0], "col", shift(2)), lax.ppermute(opposite[1], "col", shift(-2))
            pieces += [list(up), list(back)]
        hops = [0] + [hop for step in range(1, half) for hop in (-step, step)]
        stream, state = project(pieces[:-2], hops[:-2], qk_weight, None, cycle, False)
        state = project(pieces[-2:], hops[-2:], qk_weight, state, cycle, False)
        return stream, project([opposite], [half], qk_weight, state, cycle, True)

    placed = (P(None, "row"), P("row", "col"), P("row", "col"), P("col"), P(None, "col"))
    return jax.shard_map(
        per_device,
        mesh=mesh,
        in_specs=placed,
        out_specs=(P("row", "col"), P("row", "col")),
        check_vma=False,
    )
```

```python
import functools

import jax
import jax.numpy as jnp
from jax import lax
from jax.experimental import pallas as pl
from jax.experimental.pallas import tpu as pltpu
from jax.sharding import PartitionSpec as P

CORES = 2
EXTRA = 16
GAIN = 8
MIB = 1024 * 1024
HBM = pl.BlockSpec(memory_space=pl.ANY)
VMEM = pl.BlockSpec(memory_space=pltpu.VMEM)


def grid_of(count):
    x = 1
    while (2 * x) * (2 * x) <= count:
        x *= 2
    return count // x, x


def cycle_of(count):
    z, x = grid_of(count)
    walk = [0]
    for i in range(z):
        line = list(range(1, x))
        walk += [i * x + j for j in (line if i % 2 == 0 else line[::-1])]
    return walk + [i * x for i in range(z - 1, 0, -1)]


def pick(index, table):
    value = jnp.int32(table[0])
    for i in range(1, len(table)):
        value = jnp.where(index == i, jnp.int32(table[i]), value)
    return value


def cut(size, most):
    fits = [part for part in range(256, most + 1, 256) if size % part == 0]
    return fits[-1] if fits else size


def down_kernel(chips_y, tok, parts, own, hidden, weight, *refs):
    if own:
        (give, keep), held = refs[:2], weight
    else:
        give, keep, held = refs[:3]
    h_buf, total, sems = refs[-3:]
    depth = held.shape[0] // parts
    me = lax.axis_index("row")
    chip, core = me // CORES, me % CORES
    chips = [0] if own else list(range(1, chips_y))
    block = CORES * tok

    def span(k):
        return pl.ds(pl.multiple_of(k * depth, depth), depth)

    def copies(k):
        for i, step in enumerate(chips):
            start = pl.multiple_of(lax.rem(chip + step, chips_y) * block, block)
            yield pltpu.make_async_copy(
                hidden.at[pl.ds(start, block), span(k)], h_buf.at[k, pl.ds(i * block, block)], sems.at[1 + i, k]
            )
        if not own:
            yield pltpu.make_async_copy(weight.at[span(k), :], held.at[span(k), :], sems.at[0, k])

    for k in range(parts):
        for copy in copies(k):
            copy.start(priority=1)
    tokens, width = total.shape
    total[...] = jnp.zeros_like(total)

    def body(k, _):
        for copy in copies(k):
            copy.wait()
        for row in range(0, tokens, 128):
            for column in range(0, width, 512):
                place = pl.ds(row, 128), pl.ds(column, min(512, width - column))
                total[place] += jnp.dot(h_buf[k, place[0], :], held[span(k), place[1]], preferred_element_type=jnp.float32)
        return _

    lax.fori_loop(0, parts, body, 0)
    for i in range(len(chips)):
        for out, which in ((give, 1 - core), (keep, core)):
            start = pl.multiple_of((i * CORES + which) * tok, tok)
            out[i] = total[pl.ds(start, tok), :].astype(out.dtype)


def down(hidden, weight, tok, chips_y, own):
    inner, width = weight.shape
    depth = cut(inner, 1536 if own else 768)
    parts = inner // depth
    chips = 1 if own else chips_y - 1
    tokens = chips * CORES * tok
    block = pltpu.VMEM((chips, tok, width), jnp.bfloat16)
    out_shape = (block, block) if own else (block, block, pltpu.VMEM((inner, width), jnp.bfloat16))
    return pl.pallas_call(
        functools.partial(down_kernel, chips_y, tok, parts, own),
        out_shape=out_shape,
        in_specs=[HBM, VMEM if own else HBM],
        out_specs=(VMEM,) * len(out_shape),
        scratch_shapes=[
            pltpu.VMEM((parts, tokens, depth), jnp.bfloat16),
            pltpu.VMEM((tokens, width), jnp.float32),
            pltpu.SemaphoreType.DMA((1 + chips, parts)),
        ],
        compiler_params=pltpu.CompilerParams(vmem_limit_bytes=24 * MIB),
        cost_estimate=pl.CostEstimate(
            flops=2 * tokens * inner * width,
            bytes_accessed=2 * inner * (tokens if own else width + tokens),
            transcendentals=0,
        ),
        name="down",
    )(
        pltpu.with_memory_space_constraint(hidden, pltpu.HBM),
        pltpu.with_memory_space_constraint(weight, pltpu.VMEM if own else pltpu.HBM),
    )


def merge_kernel(others, keep, got, gain, upper, lower):
    tok, width = others.shape
    own = keep[...].astype(jnp.float32) + got[...].astype(jnp.float32)
    value = (others[...] + own).astype(upper.dtype)
    upper[...] = value[: tok // 2]
    lower[0 : tok // 2, :] = value[tok // 2 :]
    rows = jnp.broadcast_to(gain[...].astype(jnp.float32), (GAIN, width))
    lower[tok // 2 : tok // 2 + GAIN, :] = rows.astype(lower.dtype)


def merge(others, keep, got, gain):
    tok, width = others.shape
    return pl.pallas_call(
        merge_kernel,
        out_shape=[pltpu.VMEM((n, width), jnp.bfloat16) for n in (tok // 2, tok // 2 + GAIN)],
        in_specs=[VMEM] * 4,
        out_specs=[VMEM] * 2,
        compiler_params=pltpu.CompilerParams(vmem_limit_bytes=8 * MIB),
        name="merge",
    )(others, keep, got, gain)


def project_kernel(cycle, hops, shapes, first, last, *refs):
    count = len(cycle)
    refs = list(refs)
    take = lambda n: [refs.pop(0) for _ in range(n)]
    pieces = [take(n) for n in shapes]
    (weight,) = take(1)
    shift_in, sums_in, total_in = [None] * 3 if first else take(3)
    if last:
        out, lhs, block, sems = refs
    elif first:
        stream, shift_out, sums_out, total_out, lhs = refs
    else:
        sums_out, total_out, lhs = refs
    total = total_in if last else total_out
    tok = shift_in.shape[0] if not first else shift_out.shape[0]
    width = lhs.shape[2]
    columns = weight.shape[1]
    strip = cut(columns, 512)
    strips = columns // strip

    me = lax.axis_index("col")
    place = pick(me, [cycle.index(c) for c in range(count)])
    ids = [pick(lax.rem(place + hop + count, count), cycle) for hop in hops]

    if not first:
        shift = shift_in[...]
        one, two = sums_in[0], sums_in[1]
    for i, parts in enumerate(pieces):
        whole = jnp.concatenate([part[...].astype(jnp.float32) for part in parts], axis=0)
        values, row = whole[0:tok], whole[tok : tok + 1]
        if first and i == 0:
            stream[...] = values.astype(stream.dtype)
            shift = jnp.mean(values, axis=1, keepdims=True)
            shift_out[...] = shift
            one = two = jnp.zeros_like(shift)
        dev = values - shift
        one = one + jnp.sum(dev, axis=1, keepdims=True)
        two = two + jnp.sum(dev * dev, axis=1, keepdims=True)
        lhs[i, 0:tok, :] = (dev * row).astype(lhs.dtype)
        lhs[i, tok : tok + EXTRA, :] = jnp.broadcast_to(row, (EXTRA, width)).astype(lhs.dtype)
    if not last:
        sums_out[0] = one
        sums_out[1] = two
    else:
        off = one / (width * count)
        var = jnp.maximum(two / (width * count) - off * off, 0.0)
        scale = 1.0 / jnp.sqrt(var + 1e-06)

    def leave(n):
        span = pl.ds(n * strip, strip)
        return pltpu.make_async_copy(block.at[:, span], out.at[:, span], sems.at[n])

    for n in range(strips):
        span = pl.ds(n * strip, strip)
        for i in range(len(hops)):
            rows = pl.ds(pl.multiple_of(ids[i] * width, width), width)
            product = jnp.dot(lhs[i], weight[rows, span], preferred_element_type=jnp.float32)
            if i == 0:
                value = product if first else total_in[:, span] + product
            else:
                value = value + product
        if last:
            block[:, span] = ((value[0:tok] - off * value[tok : tok + 1]) * scale).astype(block.dtype)
            leave(n).start()
        else:
            total[:, span] = value
    if last:
        for n in range(strips):
            leave(n).wait()


def project(pieces, hops, weight, state, cycle, last):
    first = state is None
    tok = sum(part.shape[0] for part in pieces[0]) - GAIN
    width = pieces[0][0].shape[1]
    columns = weight.shape[1]
    shift = pltpu.VMEM((tok, 1), jnp.float32)
    sums = pltpu.VMEM((2, tok, 1), jnp.float32)
    total = pltpu.VMEM((tok + EXTRA, columns), jnp.float32)
    flat = [part for parts in pieces for part in parts]
    base = len(flat) + 1
    state = () if first else state
    extra = []
    if last:
        out_shape, aliases = jax.ShapeDtypeStruct((tok, columns), jnp.bfloat16), {}
        extra = [pltpu.VMEM((tok, columns), jnp.bfloat16), pltpu.SemaphoreType.DMA((columns // cut(columns, 512),))]
    elif first:
        out_shape, aliases = (jax.ShapeDtypeStruct((tok, width), jnp.bfloat16), shift, sums, total), {}
    else:
        out_shape, aliases = (sums, total), {base + 1: 0, base + 2: 1}
    got = pl.pallas_call(
        functools.partial(project_kernel, cycle, hops, [len(parts) for parts in pieces], first, last),
        out_shape=out_shape,
        in_specs=[VMEM] * (base + len(state)),
        out_specs=jax.tree.map(lambda _: HBM if last else VMEM, out_shape),
        scratch_shapes=[pltpu.VMEM((len(hops), tok + EXTRA, width), jnp.bfloat16), *extra],
        input_output_aliases=aliases,
        compiler_params=pltpu.CompilerParams(vmem_limit_bytes=12 * MIB),
        cost_estimate=pl.CostEstimate(
            flops=2 * len(hops) * (tok + EXTRA) * width * columns,
            bytes_accessed=0,
            transcendentals=0,
        ),
        name="project",
    )(*flat, pltpu.with_memory_space_constraint(weight, pltpu.VMEM), *state)
    if last:
        return got
    return (got[0], got[1:]) if first else (state[0], *got)


def solution(mesh):
    rows, cols = mesh.shape["row"], mesh.shape["col"]
    chips_y = rows // CORES
    cycle = cycle_of(cols)
    half = cols // 2

    sibling = [(r, r ^ 1) for r in range(rows)]

    def shift(hop):
        return [(cycle[i], cycle[(i + hop) % cols]) for i in range(cols)]

    def per_device(hidden, down_weight, residual, gain, qk_weight):
        tok = residual.shape[0]

        give, keep, down_weight = down(hidden, down_weight, tok, chips_y, False)
        got = lax.ppermute(give, "row", sibling)
        both = (keep.astype(jnp.float32) + got.astype(jnp.float32)).astype(jnp.bfloat16)
        both, hidden = lax.optimization_barrier((both, hidden))
        others = residual.astype(jnp.float32)
        for step in range(1, chips_y):
            move = [(r, (r + CORES * step) % rows) for r in range(rows)]
            others = others + lax.ppermute(both[step - 1], "row", move).astype(jnp.float32)
        give, keep = down(hidden, down_weight, tok, chips_y, True)
        got = lax.ppermute(give[0], "row", sibling)
        upper, lower = merge(others, keep[0], got, gain[None, :])

        up, back = [upper, lower], [upper, lower]
        pieces, hops = [[upper, lower]], [0]
        for step in range(1, half):
            for i in range(2):
                up[i], back[i] = lax.ppermute(up[i], "col", shift(1)), lax.ppermute(back[i], "col", shift(-1))
            pieces += [list(up), list(back)]
            hops += [-step, step]
        stream, state = project(pieces[:-2], hops[:-2], qk_weight, None, cycle, False)
        back[1], state = lax.optimization_barrier((back[1], state))
        opposite = [lax.ppermute(up[0], "col", shift(1)), lax.ppermute(back[1], "col", shift(-1))]
        state = project(pieces[-2:], hops[-2:], qk_weight, state, cycle, False)
        return stream, project([opposite], [half], qk_weight, state, cycle, True)

    placed = (P(None, "row"), P("row", "col"), P("row", "col"), P("col"), P(None, "col"))
    return jax.shard_map(
        per_device,
        mesh=mesh,
        in_specs=placed,
        out_specs=(P("row", "col"), P("row", "col")),
        check_vma=False,
    )
```

```python
import functools

import jax
import jax.numpy as jnp
from jax import lax
from jax.experimental import pallas as pl
from jax.experimental.pallas import tpu as pltpu
from jax.sharding import PartitionSpec as P

CORES = 2
EXTRA = 16
GAIN = 8
MIB = 1024 * 1024
HBM = pl.BlockSpec(memory_space=pl.ANY)
VMEM = pl.BlockSpec(memory_space=pltpu.VMEM)


def grid_of(count):
    x = 1
    while (2 * x) * (2 * x) <= count:
        x *= 2
    return count // x, x


def cycle_of(count):
    z, x = grid_of(count)
    walk = [0]
    for i in range(z):
        line = list(range(1, x))
        walk += [i * x + j for j in (line if i % 2 == 0 else line[::-1])]
    return walk + [i * x for i in range(z - 1, 0, -1)]


def pick(index, table):
    value = jnp.int32(table[0])
    for i in range(1, len(table)):
        value = jnp.where(index == i, jnp.int32(table[i]), value)
    return value


def cut(size, most):
    fits = [part for part in range(256, most + 1, 256) if size % part == 0]
    return fits[-1] if fits else size


def down_kernel(chips_y, tok, parts, own, hidden, weight, *refs):
    if own:
        (give, keep), held = refs[:2], weight
    else:
        give, keep, held = refs[:3]
    h_buf, total, sems = refs[-3:]
    depth = held.shape[0] // parts
    me = lax.axis_index("row")
    chip, core = me // CORES, me % CORES
    chips = [0] if own else list(range(1, chips_y))
    block = CORES * tok

    def span(k):
        return pl.ds(pl.multiple_of(k * depth, depth), depth)

    def copies(k):
        for i, step in enumerate(chips):
            start = pl.multiple_of(lax.rem(chip + step, chips_y) * block, block)
            yield pltpu.make_async_copy(
                hidden.at[pl.ds(start, block), span(k)], h_buf.at[k, pl.ds(i * block, block)], sems.at[1 + i, k]
            )
        if not own:
            yield pltpu.make_async_copy(weight.at[span(k), :], held.at[span(k), :], sems.at[0, k])

    for k in range(parts):
        for copy in copies(k):
            copy.start(priority=1)
    tokens, width = total.shape
    total[...] = jnp.zeros_like(total)

    def body(k, _):
        for copy in copies(k):
            copy.wait()
        for row in range(0, tokens, 128):
            for column in range(0, width, 512):
                place = pl.ds(row, 128), pl.ds(column, min(512, width - column))
                total[place] += jnp.dot(h_buf[k, place[0], :], held[span(k), place[1]], preferred_element_type=jnp.float32)
        return _

    lax.fori_loop(0, parts, body, 0)
    for i in range(len(chips)):
        for out, which in ((give, 1 - core), (keep, core)):
            start = pl.multiple_of((i * CORES + which) * tok, tok)
            out[i] = total[pl.ds(start, tok), :].astype(out.dtype)


def down(hidden, weight, tok, chips_y, own):
    inner, width = weight.shape
    depth = cut(inner, 1536 if own else 768)
    parts = inner // depth
    chips = 1 if own else chips_y - 1
    tokens = chips * CORES * tok
    block = pltpu.VMEM((chips, tok, width), jnp.bfloat16)
    out_shape = (block, block) if own else (block, block, pltpu.VMEM((inner, width), jnp.bfloat16))
    return pl.pallas_call(
        functools.partial(down_kernel, chips_y, tok, parts, own),
        out_shape=out_shape,
        in_specs=[HBM, VMEM if own else HBM],
        out_specs=(VMEM,) * len(out_shape),
        scratch_shapes=[
            pltpu.VMEM((parts, tokens, depth), jnp.bfloat16),
            pltpu.VMEM((tokens, width), jnp.float32),
            pltpu.SemaphoreType.DMA((1 + chips, parts)),
        ],
        compiler_params=pltpu.CompilerParams(vmem_limit_bytes=24 * MIB),
        cost_estimate=pl.CostEstimate(
            flops=2 * tokens * inner * width,
            bytes_accessed=2 * inner * (tokens if own else width + tokens),
            transcendentals=0,
        ),
        name="down",
    )(
        pltpu.with_memory_space_constraint(hidden, pltpu.HBM),
        pltpu.with_memory_space_constraint(weight, pltpu.VMEM if own else pltpu.HBM),
    )


def merge_kernel(others, keep, got, gain, upper, lower):
    tok, width = others.shape
    own = keep[...].astype(jnp.float32) + got[...].astype(jnp.float32)
    value = (others[...] + own).astype(upper.dtype)
    upper[...] = value[: tok // 2]
    lower[0 : tok // 2, :] = value[tok // 2 :]
    rows = jnp.broadcast_to(gain[...].astype(jnp.float32), (GAIN, width))
    lower[tok // 2 : tok // 2 + GAIN, :] = rows.astype(lower.dtype)


def merge(others, keep, got, gain):
    tok, width = others.shape
    return pl.pallas_call(
        merge_kernel,
        out_shape=[pltpu.VMEM((n, width), jnp.bfloat16) for n in (tok // 2, tok // 2 + GAIN)],
        in_specs=[VMEM] * 4,
        out_specs=[VMEM] * 2,
        compiler_params=pltpu.CompilerParams(vmem_limit_bytes=8 * MIB),
        name="merge",
    )(others, keep, got, gain)


def project_kernel(cycle, hops, shapes, first, last, *refs):
    count = len(cycle)
    refs = list(refs)
    take = lambda n: [refs.pop(0) for _ in range(n)]
    pieces = [take(n) for n in shapes]
    (weight,) = take(1)
    shift_in, sums_in, total_in = [None] * 3 if first else take(3)
    if last:
        out, lhs, block, sems = refs
    elif first:
        stream, shift_out, sums_out, total_out, lhs = refs
    else:
        sums_out, total_out, lhs = refs
    total = total_in if last else total_out
    tok = shift_in.shape[0] if not first else shift_out.shape[0]
    width = lhs.shape[2]
    columns = weight.shape[1]
    strip = cut(columns, 512)
    strips = columns // strip

    me = lax.axis_index("col")
    place = pick(me, [cycle.index(c) for c in range(count)])
    ids = [pick(lax.rem(place + hop + count, count), cycle) for hop in hops]

    if not first:
        shift = shift_in[...]
        one, two = sums_in[0], sums_in[1]
    for i, parts in enumerate(pieces):
        whole = jnp.concatenate([part[...].astype(jnp.float32) for part in parts], axis=0)
        values, row = whole[0:tok], whole[tok : tok + 1]
        if first and i == 0:
            stream[...] = values.astype(stream.dtype)
            shift = jnp.mean(values, axis=1, keepdims=True)
            shift_out[...] = shift
            one = two = jnp.zeros_like(shift)
        dev = values - shift
        one = one + jnp.sum(dev, axis=1, keepdims=True)
        two = two + jnp.sum(dev * dev, axis=1, keepdims=True)
        lhs[i, 0:tok, :] = (dev * row).astype(lhs.dtype)
        lhs[i, tok : tok + EXTRA, :] = jnp.broadcast_to(row, (EXTRA, width)).astype(lhs.dtype)
    if not last:
        sums_out[0] = one
        sums_out[1] = two
    else:
        off = one / (width * count)
        var = jnp.maximum(two / (width * count) - off * off, 0.0)
        scale = 1.0 / jnp.sqrt(var + 1e-06)

    def leave(n):
        span = pl.ds(n * strip, strip)
        return pltpu.make_async_copy(block.at[:, span], out.at[:, span], sems.at[n])

    for n in range(strips):
        span = pl.ds(n * strip, strip)
        for i in range(len(hops)):
            rows = pl.ds(pl.multiple_of(ids[i] * width, width), width)
            product = jnp.dot(lhs[i], weight[rows, span], preferred_element_type=jnp.float32)
            if i == 0:
                value = product if first else total_in[:, span] + product
            else:
                value = value + product
        if last:
            block[:, span] = ((value[0:tok] - off * value[tok : tok + 1]) * scale).astype(block.dtype)
            leave(n).start()
        else:
            total[:, span] = value
    if last:
        for n in range(strips):
            leave(n).wait()


def project(pieces, hops, weight, state, cycle, last):
    first = state is None
    tok = sum(part.shape[0] for part in pieces[0]) - GAIN
    width = pieces[0][0].shape[1]
    columns = weight.shape[1]
    shift = pltpu.VMEM((tok, 1), jnp.float32)
    sums = pltpu.VMEM((2, tok, 1), jnp.float32)
    total = pltpu.VMEM((tok + EXTRA, columns), jnp.float32)
    flat = [part for parts in pieces for part in parts]
    base = len(flat) + 1
    state = () if first else state
    extra = []
    if last:
        out_shape, aliases = jax.ShapeDtypeStruct((tok, columns), jnp.bfloat16), {}
        extra = [pltpu.VMEM((tok, columns), jnp.bfloat16), pltpu.SemaphoreType.DMA((columns // cut(columns, 512),))]
    elif first:
        out_shape, aliases = (jax.ShapeDtypeStruct((tok, width), jnp.bfloat16), shift, sums, total), {}
    else:
        out_shape, aliases = (sums, total), {base + 1: 0, base + 2: 1}
    got = pl.pallas_call(
        functools.partial(project_kernel, cycle, hops, [len(parts) for parts in pieces], first, last),
        out_shape=out_shape,
        in_specs=[VMEM] * (base + len(state)),
        out_specs=jax.tree.map(lambda _: HBM if last else VMEM, out_shape),
        scratch_shapes=[pltpu.VMEM((len(hops), tok + EXTRA, width), jnp.bfloat16), *extra],
        input_output_aliases=aliases,
        compiler_params=pltpu.CompilerParams(vmem_limit_bytes=12 * MIB),
        cost_estimate=pl.CostEstimate(
            flops=2 * len(hops) * (tok + EXTRA) * width * columns,
            bytes_accessed=0,
            transcendentals=0,
        ),
        name="project",
    )(*flat, pltpu.with_memory_space_constraint(weight, pltpu.VMEM), *state)
    if last:
        return got
    return (got[0], got[1:]) if first else (state[0], *got)


def solution(mesh):
    rows, cols = mesh.shape["row"], mesh.shape["col"]
    chips_y = rows // CORES
    cycle = cycle_of(cols)
    half = cols // 2

    sibling = [(r, r ^ 1) for r in range(rows)]

    def shift(hop):
        return [(cycle[i], cycle[(i + hop) % cols]) for i in range(cols)]

    def per_device(hidden, down_weight, residual, gain, qk_weight):
        tok = residual.shape[0]

        give, keep, down_weight = down(hidden, down_weight, tok, chips_y, False)
        got = lax.ppermute(give, "row", sibling)
        both = (keep.astype(jnp.float32) + got.astype(jnp.float32)).astype(jnp.bfloat16)
        both, hidden = lax.optimization_barrier((both, hidden))
        others = residual.astype(jnp.float32)
        for step in range(1, chips_y):
            move = [(r, (r + CORES * step) % rows) for r in range(rows)]
            others = others + lax.ppermute(both[step - 1], "row", move).astype(jnp.float32)
        give, keep = down(hidden, down_weight, tok, chips_y, True)
        got = lax.ppermute(give[0], "row", sibling)
        upper, lower = merge(others, keep[0], got, gain[None, :])

        up, back = [upper, lower], [upper, lower]
        pieces, hops, opposite = [[upper, lower]], [0], None
        for step in range(1, half):
            if step == half - 1:
                opposite = up[0], back[1]
            for i in range(2):
                up[i], back[i] = lax.ppermute(up[i], "col", shift(1)), lax.ppermute(back[i], "col", shift(-1))
            if opposite:
                opposite = lax.ppermute(opposite[0], "col", shift(2)), lax.ppermute(opposite[1], "col", shift(-2))
            pieces += [list(up), list(back)]
            hops += [-step, step]
        stream, state = project(pieces[:-2], hops[:-2], qk_weight, None, cycle, False)
        state = project([opposite], [half], qk_weight, state, cycle, False)
        return stream, project(pieces[-2:], hops[-2:], qk_weight, state, cycle, True)

    placed = (P(None, "row"), P("row", "col"), P("row", "col"), P("col"), P(None, "col"))
    return jax.shard_map(
        per_device,
        mesh=mesh,
        in_specs=placed,
        out_specs=(P("row", "col"), P("row", "col")),
        check_vma=False,
    )
```

```python
import functools

import jax
import jax.numpy as jnp
from jax import lax
from jax.experimental import pallas as pl
from jax.experimental.pallas import tpu as pltpu
from jax.sharding import PartitionSpec as P

CORES = 2
EXTRA = 16
GAIN = 8
MIB = 1024 * 1024
HBM = pl.BlockSpec(memory_space=pl.ANY)
VMEM = pl.BlockSpec(memory_space=pltpu.VMEM)


def grid_of(count):
    x = 1
    while (2 * x) * (2 * x) <= count:
        x *= 2
    return count // x, x


def cycle_of(count):
    z, x = grid_of(count)
    walk = [0]
    for i in range(z):
        line = list(range(1, x))
        walk += [i * x + j for j in (line if i % 2 == 0 else line[::-1])]
    return walk + [i * x for i in range(z - 1, 0, -1)]


def pick(index, table):
    value = jnp.int32(table[0])
    for i in range(1, len(table)):
        value = jnp.where(index == i, jnp.int32(table[i]), value)
    return value


def cut(size, most):
    fits = [part for part in range(256, most + 1, 256) if size % part == 0]
    return fits[-1] if fits else size


def down_kernel(chips_y, tok, parts, hidden, weight, give, keep, held, h_buf, total, sems):
    me = lax.axis_index("row")
    chip, core = me // CORES, me % CORES
    block = CORES * tok
    starts = [pl.multiple_of(lax.rem(chip + step, chips_y) * block, block) for step in range(1, chips_y)]
    multiply(parts, starts, block, hidden, weight, held, h_buf, total, sems)
    for i in range(chips_y - 1):
        for out, which in ((give, 1 - core), (keep, core)):
            start = pl.multiple_of((i * CORES + which) * tok, tok)
            out[i] = total[pl.ds(start, tok), :].astype(out.dtype)


def own_kernel(tok, parts, flip, hidden, held, out, h_buf, total, sems):
    me = lax.axis_index("row")
    block = me // CORES * CORES + (1 - me % CORES if flip else me % CORES)
    multiply(parts, [pl.multiple_of(block * tok, tok)], tok, hidden, None, held, h_buf, total, sems)
    out[...] = total[...].astype(out.dtype)


def multiply(parts, starts, block, hidden, weight, held, h_buf, total, sems):
    depth = held.shape[0] // parts

    def span(k):
        return pl.ds(pl.multiple_of(k * depth, depth), depth)

    def copies(k):
        for i, start in enumerate(starts):
            yield pltpu.make_async_copy(
                hidden.at[pl.ds(start, block), span(k)], h_buf.at[k, pl.ds(i * block, block)], sems.at[1 + i, k]
            )
        if weight is not None:
            yield pltpu.make_async_copy(weight.at[span(k), :], held.at[span(k), :], sems.at[0, k])

    for k in range(parts):
        for copy in copies(k):
            copy.start(priority=1)
    tokens, width = total.shape
    total[...] = jnp.zeros_like(total)

    def body(k, _):
        for copy in copies(k):
            copy.wait()
        for row in range(0, tokens, 128):
            for column in range(0, width, 512):
                place = pl.ds(row, 128), pl.ds(column, min(512, width - column))
                total[place] += jnp.dot(h_buf[k, place[0], :], held[span(k), place[1]], preferred_element_type=jnp.float32)
        return _

    lax.fori_loop(0, parts, body, 0)


def down(hidden, weight, tok, chips_y, flip=None):
    own = flip is not None
    inner, width = weight.shape
    parts = inner // cut(inner, 1536 if own else 768)
    chips = chips_y - 1
    tokens = tok if own else chips * CORES * tok
    block = pltpu.VMEM((chips, tok, width), jnp.bfloat16)
    if own:
        kernel = functools.partial(own_kernel, tok, parts, flip)
        out_shape = pltpu.VMEM((tok, width), jnp.bfloat16)
    else:
        kernel = functools.partial(down_kernel, chips_y, tok, parts)
        out_shape = block, block, pltpu.VMEM((inner, width), jnp.bfloat16)
    return pl.pallas_call(
        kernel,
        out_shape=out_shape,
        in_specs=[HBM, VMEM if own else HBM],
        out_specs=jax.tree.map(lambda _: VMEM, out_shape),
        scratch_shapes=[
            pltpu.VMEM((parts, tokens, inner // parts), jnp.bfloat16),
            pltpu.VMEM((tokens, width), jnp.float32),
            pltpu.SemaphoreType.DMA((1 + chips, parts)),
        ],
        compiler_params=pltpu.CompilerParams(vmem_limit_bytes=24 * MIB),
        cost_estimate=pl.CostEstimate(
            flops=2 * tokens * inner * width,
            bytes_accessed=2 * inner * (tokens if own else width + tokens),
            transcendentals=0,
        ),
        name="down",
    )(
        pltpu.with_memory_space_constraint(hidden, pltpu.HBM),
        pltpu.with_memory_space_constraint(weight, pltpu.VMEM if own else pltpu.HBM),
    )


def merge_kernel(others, keep, got, gain, upper, lower):
    tok, width = others.shape
    own = keep[...].astype(jnp.float32) + got[...].astype(jnp.float32)
    value = (others[...] + own).astype(upper.dtype)
    upper[...] = value[: tok // 2]
    lower[0 : tok // 2, :] = value[tok // 2 :]
    rows = jnp.broadcast_to(gain[...].astype(jnp.float32), (GAIN, width))
    lower[tok // 2 : tok // 2 + GAIN, :] = rows.astype(lower.dtype)


def merge(others, keep, got, gain):
    tok, width = others.shape
    return pl.pallas_call(
        merge_kernel,
        out_shape=[pltpu.VMEM((n, width), jnp.bfloat16) for n in (tok // 2, tok // 2 + GAIN)],
        in_specs=[VMEM] * 4,
        out_specs=[VMEM] * 2,
        compiler_params=pltpu.CompilerParams(vmem_limit_bytes=8 * MIB),
        name="merge",
    )(others, keep, got, gain)


def project_kernel(cycle, hops, shapes, first, last, *refs):
    count = len(cycle)
    refs = list(refs)
    take = lambda n: [refs.pop(0) for _ in range(n)]
    pieces = [take(n) for n in shapes]
    (weight,) = take(1)
    shift_in, sums_in, total_in = [None] * 3 if first else take(3)
    if last:
        out, lhs, block, sems = refs
    elif first:
        stream, shift_out, sums_out, total_out, lhs = refs
    else:
        sums_out, total_out, lhs = refs
    total = total_in if last else total_out
    tok = shift_in.shape[0] if not first else shift_out.shape[0]
    width = lhs.shape[2]
    columns = weight.shape[1]
    strip = cut(columns, 512)
    strips = columns // strip

    me = lax.axis_index("col")
    place = pick(me, [cycle.index(c) for c in range(count)])
    ids = [pick(lax.rem(place + hop + count, count), cycle) for hop in hops]

    if not first:
        shift = shift_in[...]
        one, two = sums_in[0], sums_in[1]
    for i, parts in enumerate(pieces):
        whole = jnp.concatenate([part[...].astype(jnp.float32) for part in parts], axis=0)
        values, row = whole[0:tok], whole[tok : tok + 1]
        if first and i == 0:
            stream[...] = values.astype(stream.dtype)
            shift = jnp.mean(values, axis=1, keepdims=True)
            shift_out[...] = shift
            one = two = jnp.zeros_like(shift)
        dev = values - shift
        one = one + jnp.sum(dev, axis=1, keepdims=True)
        two = two + jnp.sum(dev * dev, axis=1, keepdims=True)
        lhs[i, 0:tok, :] = (dev * row).astype(lhs.dtype)
        lhs[i, tok : tok + EXTRA, :] = jnp.broadcast_to(row, (EXTRA, width)).astype(lhs.dtype)
    if not last:
        sums_out[0] = one
        sums_out[1] = two
    else:
        off = one / (width * count)
        var = jnp.maximum(two / (width * count) - off * off, 0.0)
        scale = 1.0 / jnp.sqrt(var + 1e-06)

    def leave(n):
        span = pl.ds(n * strip, strip)
        return pltpu.make_async_copy(block.at[:, span], out.at[:, span], sems.at[n])

    for n in range(strips):
        span = pl.ds(n * strip, strip)
        for i in range(len(hops)):
            rows = pl.ds(pl.multiple_of(ids[i] * width, width), width)
            product = jnp.dot(lhs[i], weight[rows, span], preferred_element_type=jnp.float32)
            if i == 0:
                value = product if first else total_in[:, span] + product
            else:
                value = value + product
        if last:
            block[:, span] = ((value[0:tok] - off * value[tok : tok + 1]) * scale).astype(block.dtype)
            leave(n).start()
        else:
            total[:, span] = value
    if last:
        for n in range(strips):
            leave(n).wait()


def project(pieces, hops, weight, state, cycle, last):
    first = state is None
    tok = sum(part.shape[0] for part in pieces[0]) - GAIN
    width = pieces[0][0].shape[1]
    columns = weight.shape[1]
    shift = pltpu.VMEM((tok, 1), jnp.float32)
    sums = pltpu.VMEM((2, tok, 1), jnp.float32)
    total = pltpu.VMEM((tok + EXTRA, columns), jnp.float32)
    flat = [part for parts in pieces for part in parts]
    base = len(flat) + 1
    state = () if first else state
    extra = []
    if last:
        out_shape, aliases = jax.ShapeDtypeStruct((tok, columns), jnp.bfloat16), {}
        extra = [pltpu.VMEM((tok, columns), jnp.bfloat16), pltpu.SemaphoreType.DMA((columns // cut(columns, 512),))]
    elif first:
        out_shape, aliases = (jax.ShapeDtypeStruct((tok, width), jnp.bfloat16), shift, sums, total), {}
    else:
        out_shape, aliases = (sums, total), {base + 1: 0, base + 2: 1}
    got = pl.pallas_call(
        functools.partial(project_kernel, cycle, hops, [len(parts) for parts in pieces], first, last),
        out_shape=out_shape,
        in_specs=[VMEM] * (base + len(state)),
        out_specs=jax.tree.map(lambda _: HBM if last else VMEM, out_shape),
        scratch_shapes=[pltpu.VMEM((len(hops), tok + EXTRA, width), jnp.bfloat16), *extra],
        input_output_aliases=aliases,
        compiler_params=pltpu.CompilerParams(vmem_limit_bytes=12 * MIB),
        cost_estimate=pl.CostEstimate(
            flops=2 * len(hops) * (tok + EXTRA) * width * columns,
            bytes_accessed=0,
            transcendentals=0,
        ),
        name="project",
    )(*flat, pltpu.with_memory_space_constraint(weight, pltpu.VMEM), *state)
    if last:
        return got
    return (got[0], got[1:]) if first else (state[0], *got)


def solution(mesh):
    rows, cols = mesh.shape["row"], mesh.shape["col"]
    chips_y = rows // CORES
    cycle = cycle_of(cols)
    half = cols // 2

    sibling = [(r, r ^ 1) for r in range(rows)]

    def shift(hop):
        return [(cycle[i], cycle[(i + hop) % cols]) for i in range(cols)]

    def per_device(hidden, down_weight, residual, gain, qk_weight):
        tok = residual.shape[0]

        give, keep, down_weight = down(hidden, down_weight, tok, chips_y)
        got = lax.ppermute(give, "row", sibling)
        both = (keep.astype(jnp.float32) + got.astype(jnp.float32)).astype(jnp.bfloat16)
        both, hidden = lax.optimization_barrier((both, hidden))
        others = residual.astype(jnp.float32)
        for step in range(1, chips_y):
            move = [(r, (r + CORES * step) % rows) for r in range(rows)]
            others = others + lax.ppermute(both[step - 1], "row", move).astype(jnp.float32)
        got = lax.ppermute(down(hidden, down_weight, tok, chips_y, True), "row", sibling)
        keep = down(hidden, down_weight, tok, chips_y, False)
        upper, lower = merge(others, keep, got, gain[None, :])

        up, back = [upper, lower], [upper, lower]
        pieces, hops, opposite = [[upper, lower]], [0], None
        for step in range(1, half):
            if step == half - 1:
                opposite = up[0], back[1]
            for i in range(2):
                up[i], back[i] = lax.ppermute(up[i], "col", shift(1)), lax.ppermute(back[i], "col", shift(-1))
            if opposite:
                opposite = lax.ppermute(opposite[0], "col", shift(2)), lax.ppermute(opposite[1], "col", shift(-2))
            pieces += [list(up), list(back)]
            hops += [-step, step]
        stream, state = project(pieces[:-2], hops[:-2], qk_weight, None, cycle, False)
        state = project([opposite], [half], qk_weight, state, cycle, False)
        return stream, project(pieces[-2:], hops[-2:], qk_weight, state, cycle, True)

    placed = (P(None, "row"), P("row", "col"), P("row", "col"), P("col"), P(None, "col"))
    return jax.shard_map(
        per_device,
        mesh=mesh,
        in_specs=placed,
        out_specs=(P("row", "col"), P("row", "col")),
        check_vma=False,
    )
```

```python
import functools

import jax
import jax.numpy as jnp
from jax import lax
from jax.experimental import pallas as pl
from jax.experimental.pallas import tpu as pltpu
from jax.sharding import PartitionSpec as P

CORES = 2
EXTRA = 16
GAIN = 8
MIB = 1024 * 1024
HBM = pl.BlockSpec(memory_space=pl.ANY)
VMEM = pl.BlockSpec(memory_space=pltpu.VMEM)


def grid_of(count):
    x = 1
    while (2 * x) * (2 * x) <= count:
        x *= 2
    return count // x, x


def cycle_of(count):
    z, x = grid_of(count)
    walk = [0]
    for i in range(z):
        line = list(range(1, x))
        walk += [i * x + j for j in (line if i % 2 == 0 else line[::-1])]
    return walk + [i * x for i in range(z - 1, 0, -1)]


def pick(index, table):
    value = jnp.int32(table[0])
    for i in range(1, len(table)):
        value = jnp.where(index == i, jnp.int32(table[i]), value)
    return value


def cut(size, most):
    fits = [part for part in range(256, most + 1, 256) if size % part == 0]
    return fits[-1] if fits else size


def down_kernel(chips_y, tok, parts, own, hidden, weight, *refs):
    if own:
        (give, keep), held = refs[:2], weight
    else:
        give, keep, held = refs[:3]
    h_buf, total, sems = refs[-3:]
    depth = held.shape[0] // parts
    me = lax.axis_index("row")
    chip, core = me // CORES, me % CORES
    chips = [0] if own else list(range(1, chips_y))
    block = CORES * tok

    def span(k):
        return pl.ds(pl.multiple_of(k * depth, depth), depth)

    def copies(k):
        for i, step in enumerate(chips):
            start = pl.multiple_of(lax.rem(chip + step, chips_y) * block, block)
            yield pltpu.make_async_copy(
                hidden.at[pl.ds(start, block), span(k)], h_buf.at[k, pl.ds(i * block, block)], sems.at[1 + i, k]
            )
        if not own:
            yield pltpu.make_async_copy(weight.at[span(k), :], held.at[span(k), :], sems.at[0, k])

    for k in range(parts):
        for copy in copies(k):
            copy.start(priority=1)
    tokens, width = total.shape
    total[...] = jnp.zeros_like(total)

    def body(k, _):
        for copy in copies(k):
            copy.wait()
        for row in range(0, tokens, 128):
            for column in range(0, width, 512):
                place = pl.ds(row, 128), pl.ds(column, min(512, width - column))
                cuts = [0, depth] if width - column >= 512 or depth % 512 else [0, depth // 2, depth]
                value = total[place]
                for low, high in zip(cuts, cuts[1:]):
                    left = h_buf[k, place[0], low:high]
                    right = held[pl.ds(pl.multiple_of(k * depth + low, 256), high - low), place[1]]
                    value = value + jnp.dot(left, right, preferred_element_type=jnp.float32)
                total[place] = value
        return _

    lax.fori_loop(0, parts, body, 0)
    for i in range(len(chips)):
        for out, which in ((give, 1 - core), (keep, core)):
            start = pl.multiple_of((i * CORES + which) * tok, tok)
            out[i] = total[pl.ds(start, tok), :].astype(out.dtype)


def down(hidden, weight, tok, chips_y, own):
    inner, width = weight.shape
    depth = cut(inner, 1536)
    parts = inner // depth
    chips = 1 if own else chips_y - 1
    tokens = chips * CORES * tok
    block = pltpu.VMEM((chips, tok, width), jnp.bfloat16)
    out_shape = (block, block) if own else (block, block, pltpu.VMEM((inner, width), jnp.bfloat16))
    return pl.pallas_call(
        functools.partial(down_kernel, chips_y, tok, parts, own),
        out_shape=out_shape,
        in_specs=[HBM, VMEM if own else HBM],
        out_specs=(VMEM,) * len(out_shape),
        scratch_shapes=[
            pltpu.VMEM((parts, tokens, depth), jnp.bfloat16),
            pltpu.VMEM((tokens, width), jnp.float32),
            pltpu.SemaphoreType.DMA((1 + chips, parts)),
        ],
        compiler_params=pltpu.CompilerParams(vmem_limit_bytes=24 * MIB),
        cost_estimate=pl.CostEstimate(
            flops=2 * tokens * inner * width,
            bytes_accessed=2 * inner * (tokens if own else width + tokens),
            transcendentals=0,
        ),
        name="down",
    )(
        pltpu.with_memory_space_constraint(hidden, pltpu.HBM),
        pltpu.with_memory_space_constraint(weight, pltpu.VMEM if own else pltpu.HBM),
    )


def merge_kernel(others, keep, got, gain, upper, lower):
    tok, width = others.shape
    own = keep[...].astype(jnp.float32) + got[...].astype(jnp.float32)
    value = (others[...] + own).astype(upper.dtype)
    upper[...] = value[: tok // 2]
    lower[0 : tok // 2, :] = value[tok // 2 :]
    rows = jnp.broadcast_to(gain[...].astype(jnp.float32), (GAIN, width))
    lower[tok // 2 : tok // 2 + GAIN, :] = rows.astype(lower.dtype)


def merge(others, keep, got, gain):
    tok, width = others.shape
    return pl.pallas_call(
        merge_kernel,
        out_shape=[pltpu.VMEM((n, width), jnp.bfloat16) for n in (tok // 2, tok // 2 + GAIN)],
        in_specs=[VMEM] * 4,
        out_specs=[VMEM] * 2,
        compiler_params=pltpu.CompilerParams(vmem_limit_bytes=8 * MIB),
        name="merge",
    )(others, keep, got, gain)


def project_kernel(cycle, hops, shapes, first, last, *refs):
    count = len(cycle)
    refs = list(refs)
    take = lambda n: [refs.pop(0) for _ in range(n)]
    pieces = [take(n) for n in shapes]
    (weight,) = take(1)
    shift_in, sums_in, total_in = [None] * 3 if first else take(3)
    if last:
        out, lhs, block, sems = refs
    elif first:
        stream, shift_out, sums_out, total_out, lhs = refs
    else:
        sums_out, total_out, lhs = refs
    total = total_in if last else total_out
    tok = shift_in.shape[0] if not first else shift_out.shape[0]
    width = lhs.shape[2]
    columns = weight.shape[1]
    strip = cut(columns, 512)
    strips = columns // strip

    me = lax.axis_index("col")
    place = pick(me, [cycle.index(c) for c in range(count)])
    ids = [pick(lax.rem(place + hop + count, count), cycle) for hop in hops]

    if not first:
        shift = shift_in[...]
        one, two = sums_in[0], sums_in[1]
    for i, parts in enumerate(pieces):
        whole = jnp.concatenate([part[...].astype(jnp.float32) for part in parts], axis=0)
        values, row = whole[0:tok], whole[tok : tok + 1]
        if first and i == 0:
            stream[...] = values.astype(stream.dtype)
            shift = jnp.mean(values, axis=1, keepdims=True)
            shift_out[...] = shift
            one = two = jnp.zeros_like(shift)
        dev = values - shift
        one = one + jnp.sum(dev, axis=1, keepdims=True)
        two = two + jnp.sum(dev * dev, axis=1, keepdims=True)
        lhs[i, 0:tok, :] = (dev * row).astype(lhs.dtype)
        lhs[i, tok : tok + EXTRA, :] = jnp.broadcast_to(row, (EXTRA, width)).astype(lhs.dtype)
    if not last:
        sums_out[0] = one
        sums_out[1] = two
    else:
        off = one / (width * count)
        var = jnp.maximum(two / (width * count) - off * off, 0.0)
        scale = 1.0 / jnp.sqrt(var + 1e-06)

    def leave(n):
        span = pl.ds(n * strip, strip)
        return pltpu.make_async_copy(block.at[:, span], out.at[:, span], sems.at[n])

    for n in range(strips):
        span = pl.ds(n * strip, strip)
        for i in range(len(hops)):
            rows = pl.ds(pl.multiple_of(ids[i] * width, width), width)
            product = jnp.dot(lhs[i], weight[rows, span], preferred_element_type=jnp.float32)
            if i == 0:
                value = product if first else total_in[:, span] + product
            else:
                value = value + product
        if last:
            block[:, span] = ((value[0:tok] - off * value[tok : tok + 1]) * scale).astype(block.dtype)
            leave(n).start()
        else:
            total[:, span] = value
    if last:
        for n in range(strips):
            leave(n).wait()


def project(pieces, hops, weight, state, cycle, last):
    first = state is None
    tok = sum(part.shape[0] for part in pieces[0]) - GAIN
    width = pieces[0][0].shape[1]
    columns = weight.shape[1]
    shift = pltpu.VMEM((tok, 1), jnp.float32)
    sums = pltpu.VMEM((2, tok, 1), jnp.float32)
    total = pltpu.VMEM((tok + EXTRA, columns), jnp.float32)
    flat = [part for parts in pieces for part in parts]
    base = len(flat) + 1
    state = () if first else state
    extra = []
    if last:
        out_shape, aliases = jax.ShapeDtypeStruct((tok, columns), jnp.bfloat16), {}
        extra = [pltpu.VMEM((tok, columns), jnp.bfloat16), pltpu.SemaphoreType.DMA((columns // cut(columns, 512),))]
    elif first:
        out_shape, aliases = (jax.ShapeDtypeStruct((tok, width), jnp.bfloat16), shift, sums, total), {}
    else:
        out_shape, aliases = (sums, total), {base + 1: 0, base + 2: 1}
    got = pl.pallas_call(
        functools.partial(project_kernel, cycle, hops, [len(parts) for parts in pieces], first, last),
        out_shape=out_shape,
        in_specs=[VMEM] * (base + len(state)),
        out_specs=jax.tree.map(lambda _: HBM if last else VMEM, out_shape),
        scratch_shapes=[pltpu.VMEM((len(hops), tok + EXTRA, width), jnp.bfloat16), *extra],
        input_output_aliases=aliases,
        compiler_params=pltpu.CompilerParams(vmem_limit_bytes=12 * MIB),
        cost_estimate=pl.CostEstimate(
            flops=2 * len(hops) * (tok + EXTRA) * width * columns,
            bytes_accessed=0,
            transcendentals=0,
        ),
        name="project",
    )(*flat, pltpu.with_memory_space_constraint(weight, pltpu.VMEM), *state)
    if last:
        return got
    return (got[0], got[1:]) if first else (state[0], *got)


def solution(mesh):
    rows, cols = mesh.shape["row"], mesh.shape["col"]
    chips_y = rows // CORES
    cycle = cycle_of(cols)
    half = cols // 2

    sibling = [(r, r ^ 1) for r in range(rows)]

    def shift(hop):
        return [(cycle[i], cycle[(i + hop) % cols]) for i in range(cols)]

    def per_device(hidden, down_weight, residual, gain, qk_weight):
        tok = residual.shape[0]

        give, keep, down_weight = down(hidden, down_weight, tok, chips_y, False)
        got = lax.ppermute(give, "row", sibling)
        both = (keep.astype(jnp.float32) + got.astype(jnp.float32)).astype(jnp.bfloat16)
        both, hidden = lax.optimization_barrier((both, hidden))
        others = residual.astype(jnp.float32)
        for step in range(1, chips_y):
            move = [(r, (r + CORES * step) % rows) for r in range(rows)]
            others = others + lax.ppermute(both[step - 1], "row", move).astype(jnp.float32)
        give, keep = down(hidden, down_weight, tok, chips_y, True)
        got = lax.ppermute(give[0], "row", sibling)
        upper, lower = merge(others, keep[0], got, gain[None, :])

        up, back = [upper, lower], [upper, lower]
        pieces, hops = [[upper, lower]], [0]
        for step in range(1, half - 1):
            for i in range(2):
                up[i], back[i] = lax.ppermute(up[i], "col", shift(1)), lax.ppermute(back[i], "col", shift(-1))
            pieces += [list(up), list(back)]
            hops += [-step, step]
        opposite = lax.ppermute(up[0], "col", shift(2)), lax.ppermute(back[1], "col", shift(-2))
        far = [[lax.ppermute(jnp.concatenate(way), "col", shift(hop))] for way, hop in ((up, 1), (back, -1))]
        stream, state = project(pieces, hops, qk_weight, None, cycle, False)
        state = project([opposite], [half], qk_weight, state, cycle, False)
        return stream, project(far, [1 - half, half - 1], qk_weight, state, cycle, True)

    placed = (P(None, "row"), P("row", "col"), P("row", "col"), P("col"), P(None, "col"))
    return jax.shard_map(
        per_device,
        mesh=mesh,
        in_specs=placed,
        out_specs=(P("row", "col"), P("row", "col")),
        check_vma=False,
    )
```

```python
import functools

import jax
import jax.numpy as jnp
from jax import lax
from jax.experimental import pallas as pl
from jax.experimental.pallas import tpu as pltpu
from jax.sharding import PartitionSpec as P

CORES = 2
EXTRA = 16
GAIN = 8
MIB = 1024 * 1024
HBM = pl.BlockSpec(memory_space=pl.ANY)
VMEM = pl.BlockSpec(memory_space=pltpu.VMEM)


def grid_of(count):
    x = 1
    while (2 * x) * (2 * x) <= count:
        x *= 2
    return count // x, x


def cycle_of(count):
    z, x = grid_of(count)
    walk = [0]
    for i in range(z):
        line = list(range(1, x))
        walk += [i * x + j for j in (line if i % 2 == 0 else line[::-1])]
    return walk + [i * x for i in range(z - 1, 0, -1)]


def pick(index, table):
    value = jnp.int32(table[0])
    for i in range(1, len(table)):
        value = jnp.where(index == i, jnp.int32(table[i]), value)
    return value


def cut(size, most):
    fits = [part for part in range(256, most + 1, 256) if size % part == 0]
    return fits[-1] if fits else size


def down_kernel(chips_y, tok, parts, own, hidden, weight, *refs):
    if own:
        (give, keep), held = refs[:2], weight
    else:
        give, keep, held = refs[:3]
    h_buf, total, sems = refs[-3:]
    depth = held.shape[0] // parts
    me = lax.axis_index("row")
    chip, core = me // CORES, me % CORES
    chips = [0] if own else list(range(1, chips_y))
    block = CORES * tok

    def span(k):
        return pl.ds(pl.multiple_of(k * depth, depth), depth)

    def copies(k):
        for i, step in enumerate(chips):
            start = pl.multiple_of(lax.rem(chip + step, chips_y) * block, block)
            yield pltpu.make_async_copy(
                hidden.at[pl.ds(start, block), span(k)], h_buf.at[k, pl.ds(i * block, block)], sems.at[1 + i, k]
            )
        if not own:
            yield pltpu.make_async_copy(weight.at[span(k), :], held.at[span(k), :], sems.at[0, k])

    for k in range(parts):
        for copy in copies(k):
            copy.start(priority=1)
    tokens, width = total.shape
    total[...] = jnp.zeros_like(total)

    def body(k, _):
        for copy in copies(k):
            copy.wait()
        for row in range(0, tokens, 128):
            place = pl.ds(row, 128)
            total[place, :] += jnp.dot(h_buf[k, place, :], held[span(k), :], preferred_element_type=jnp.float32)
        return _

    lax.fori_loop(0, parts, body, 0)
    for i in range(len(chips)):
        for out, which in ((give, 1 - core), (keep, core)):
            start = pl.multiple_of((i * CORES + which) * tok, tok)
            out[i] = total[pl.ds(start, tok), :].astype(out.dtype)


def down(hidden, weight, tok, chips_y, own):
    inner, width = weight.shape
    depth = cut(inner, 1536 if own else 768)
    parts = inner // depth
    chips = 1 if own else chips_y - 1
    tokens = chips * CORES * tok
    block = pltpu.VMEM((chips, tok, width), jnp.bfloat16)
    out_shape = (block, block) if own else (block, block, pltpu.VMEM((inner, width), jnp.bfloat16))
    return pl.pallas_call(
        functools.partial(down_kernel, chips_y, tok, parts, own),
        out_shape=out_shape,
        in_specs=[HBM, VMEM if own else HBM],
        out_specs=(VMEM,) * len(out_shape),
        scratch_shapes=[
            pltpu.VMEM((parts, tokens, depth), jnp.bfloat16),
            pltpu.VMEM((tokens, width), jnp.float32),
            pltpu.SemaphoreType.DMA((1 + chips, parts)),
        ],
        compiler_params=pltpu.CompilerParams(vmem_limit_bytes=24 * MIB),
        cost_estimate=pl.CostEstimate(
            flops=2 * tokens * inner * width,
            bytes_accessed=2 * inner * (tokens if own else width + tokens),
            transcendentals=0,
        ),
        name="down",
    )(
        pltpu.with_memory_space_constraint(hidden, pltpu.HBM),
        pltpu.with_memory_space_constraint(weight, pltpu.VMEM if own else pltpu.HBM),
    )


def merge_kernel(others, keep, got, gain, upper, lower):
    tok, width = others.shape
    own = keep[...].astype(jnp.float32) + got[...].astype(jnp.float32)
    value = (others[...] + own).astype(upper.dtype)
    upper[...] = value[: tok // 2]
    lower[0 : tok // 2, :] = value[tok // 2 :]
    rows = jnp.broadcast_to(gain[...].astype(jnp.float32), (GAIN, width))
    lower[tok // 2 : tok // 2 + GAIN, :] = rows.astype(lower.dtype)


def merge(others, keep, got, gain):
    tok, width = others.shape
    return pl.pallas_call(
        merge_kernel,
        out_shape=[pltpu.VMEM((n, width), jnp.bfloat16) for n in (tok // 2, tok // 2 + GAIN)],
        in_specs=[VMEM] * 4,
        out_specs=[VMEM] * 2,
        compiler_params=pltpu.CompilerParams(vmem_limit_bytes=8 * MIB),
        name="merge",
    )(others, keep, got, gain)


def project_kernel(cycle, hops, shapes, first, last, *refs):
    count = len(cycle)
    refs = list(refs)
    take = lambda n: [refs.pop(0) for _ in range(n)]
    pieces = [take(n) for n in shapes]
    (weight,) = take(1)
    shift_in, sums_in, total_in = [None] * 3 if first else take(3)
    if last:
        out, lhs, block, sems = refs
    elif first:
        stream, shift_out, sums_out, total_out, lhs = refs
    else:
        sums_out, total_out, lhs = refs
    total = total_in if last else total_out
    tok = shift_in.shape[0] if not first else shift_out.shape[0]
    width = lhs.shape[2]
    columns = weight.shape[1]
    strip = cut(columns, 512)
    strips = columns // strip

    me = lax.axis_index("col")
    place = pick(me, [cycle.index(c) for c in range(count)])
    ids = [pick(lax.rem(place + hop + count, count), cycle) for hop in hops]

    if not first:
        shift = shift_in[...]
        one, two = sums_in[0], sums_in[1]
    for i, parts in enumerate(pieces):
        whole = jnp.concatenate([part[...].astype(jnp.float32) for part in parts], axis=0)
        values, row = whole[0:tok], whole[tok : tok + 1]
        if first and i == 0:
            stream[...] = values.astype(stream.dtype)
            shift = jnp.mean(values, axis=1, keepdims=True)
            shift_out[...] = shift
            one = two = jnp.zeros_like(shift)
        dev = values - shift
        one = one + jnp.sum(dev, axis=1, keepdims=True)
        two = two + jnp.sum(dev * dev, axis=1, keepdims=True)
        lhs[i, 0:tok, :] = (dev * row).astype(lhs.dtype)
        lhs[i, tok : tok + EXTRA, :] = jnp.broadcast_to(row, (EXTRA, width)).astype(lhs.dtype)
    if not last:
        sums_out[0] = one
        sums_out[1] = two
    else:
        off = one / (width * count)
        var = jnp.maximum(two / (width * count) - off * off, 0.0)
        scale = 1.0 / jnp.sqrt(var + 1e-06)

    def leave(n):
        span = pl.ds(n * strip, strip)
        return pltpu.make_async_copy(block.at[:, span], out.at[:, span], sems.at[n])

    for n in range(strips):
        span = pl.ds(n * strip, strip)
        for i in range(len(hops)):
            rows = pl.ds(pl.multiple_of(ids[i] * width, width), width)
            product = jnp.dot(lhs[i], weight[rows, span], preferred_element_type=jnp.float32)
            if i == 0:
                value = product if first else total_in[:, span] + product
            else:
                value = value + product
        if last:
            block[:, span] = ((value[0:tok] - off * value[tok : tok + 1]) * scale).astype(block.dtype)
            leave(n).start()
        else:
            total[:, span] = value
    if last:
        for n in range(strips):
            leave(n).wait()


def project(pieces, hops, weight, state, cycle, last):
    first = state is None
    tok = sum(part.shape[0] for part in pieces[0]) - GAIN
    width = pieces[0][0].shape[1]
    columns = weight.shape[1]
    shift = pltpu.VMEM((tok, 1), jnp.float32)
    sums = pltpu.VMEM((2, tok, 1), jnp.float32)
    total = pltpu.VMEM((tok + EXTRA, columns), jnp.float32)
    flat = [part for parts in pieces for part in parts]
    base = len(flat) + 1
    state = () if first else state
    extra = []
    if last:
        out_shape, aliases = jax.ShapeDtypeStruct((tok, columns), jnp.bfloat16), {}
        extra = [pltpu.VMEM((tok, columns), jnp.bfloat16), pltpu.SemaphoreType.DMA((columns // cut(columns, 512),))]
    elif first:
        out_shape, aliases = (jax.ShapeDtypeStruct((tok, width), jnp.bfloat16), shift, sums, total), {}
    else:
        out_shape, aliases = (sums, total), {base + 1: 0, base + 2: 1}
    got = pl.pallas_call(
        functools.partial(project_kernel, cycle, hops, [len(parts) for parts in pieces], first, last),
        out_shape=out_shape,
        in_specs=[VMEM] * (base + len(state)),
        out_specs=jax.tree.map(lambda _: HBM if last else VMEM, out_shape),
        scratch_shapes=[pltpu.VMEM((len(hops), tok + EXTRA, width), jnp.bfloat16), *extra],
        input_output_aliases=aliases,
        compiler_params=pltpu.CompilerParams(vmem_limit_bytes=12 * MIB),
        cost_estimate=pl.CostEstimate(
            flops=2 * len(hops) * (tok + EXTRA) * width * columns,
            bytes_accessed=0,
            transcendentals=0,
        ),
        name="project",
    )(*flat, pltpu.with_memory_space_constraint(weight, pltpu.VMEM), *state)
    if last:
        return got
    return (got[0], got[1:]) if first else (state[0], *got)


def solution(mesh):
    rows, cols = mesh.shape["row"], mesh.shape["col"]
    chips_y = rows // CORES
    cycle = cycle_of(cols)
    half = cols // 2

    sibling = [(r, r ^ 1) for r in range(rows)]

    def shift(hop):
        return [(cycle[i], cycle[(i + hop) % cols]) for i in range(cols)]

    def per_device(hidden, down_weight, residual, gain, qk_weight):
        tok = residual.shape[0]

        give, keep, down_weight = down(hidden, down_weight, tok, chips_y, False)
        got = lax.ppermute(give, "row", sibling)
        both = (keep.astype(jnp.float32) + got.astype(jnp.float32)).astype(jnp.bfloat16)
        both, hidden = lax.optimization_barrier((both, hidden))
        others = residual.astype(jnp.float32)
        for step in range(1, chips_y):
            move = [(r, (r + CORES * step) % rows) for r in range(rows)]
            others = others + lax.ppermute(both[step - 1], "row", move).astype(jnp.float32)
        give, keep = down(hidden, down_weight, tok, chips_y, True)
        got = lax.ppermute(give[0], "row", sibling)
        upper, lower = merge(others, keep[0], got, gain[None, :])

        up, back = [upper, lower], [upper, lower]
        pieces, hops, opposite = [[upper, lower]], [0], None
        for step in range(1, half):
            if step == half - 1:
                opposite = up[0], back[1]
            for i in range(2):
                up[i], back[i] = lax.ppermute(up[i], "col", shift(1)), lax.ppermute(back[i], "col", shift(-1))
            if opposite:
                opposite = lax.ppermute(opposite[0], "col", shift(2)), lax.ppermute(opposite[1], "col", shift(-2))
            pieces += [list(up), list(back)]
            hops += [-step, step]
        stream, state = project(pieces[:-2], hops[:-2], qk_weight, None, cycle, False)
        state = project([opposite], [half], qk_weight, state, cycle, False)
        return stream, project(pieces[-2:], hops[-2:], qk_weight, state, cycle, True)

    placed = (P(None, "row"), P("row", "col"), P("row", "col"), P("col"), P(None, "col"))
    return jax.shard_map(
        per_device,
        mesh=mesh,
        in_specs=placed,
        out_specs=(P("row", "col"), P("row", "col")),
        check_vma=False,
    )
```

```python
import functools

import jax
import jax.numpy as jnp
from jax import lax
from jax.experimental import pallas as pl
from jax.experimental.pallas import tpu as pltpu
from jax.sharding import PartitionSpec as P

CORES = 2
EXTRA = 16
GAIN = 8
MIB = 1024 * 1024
HBM = pl.BlockSpec(memory_space=pl.ANY)
VMEM = pl.BlockSpec(memory_space=pltpu.VMEM)


def grid_of(count):
    x = 1
    while (2 * x) * (2 * x) <= count:
        x *= 2
    return count // x, x


def cycle_of(count):
    z, x = grid_of(count)
    walk = [0]
    for i in range(z):
        line = list(range(1, x))
        walk += [i * x + j for j in (line if i % 2 == 0 else line[::-1])]
    return walk + [i * x for i in range(z - 1, 0, -1)]


def pick(index, table):
    value = jnp.int32(table[0])
    for i in range(1, len(table)):
        value = jnp.where(index == i, jnp.int32(table[i]), value)
    return value


def cut(size, most):
    fits = [part for part in range(256, most + 1, 256) if size % part == 0]
    return fits[-1] if fits else size


def down_kernel(chips_y, tok, parts, own, hidden, weight, *refs):
    if own:
        (give, keep), held = refs[:2], weight
    else:
        give, keep, held = refs[:3]
    h_buf, total, sems = refs[-3:]
    depth = held.shape[0] // parts
    me = lax.axis_index("row")
    chip, core = me // CORES, me % CORES
    chips = [0] if own else list(range(1, chips_y))
    block = CORES * tok

    def span(k):
        return pl.ds(pl.multiple_of(k * depth, depth), depth)

    def copies(k):
        for i, step in enumerate(chips):
            start = pl.multiple_of(lax.rem(chip + step, chips_y) * block, block)
            yield pltpu.make_async_copy(
                hidden.at[pl.ds(start, block), span(k)], h_buf.at[k, pl.ds(i * block, block)], sems.at[1 + i, k]
            )
        if not own:
            yield pltpu.make_async_copy(weight.at[span(k), :], held.at[span(k), :], sems.at[0, k])

    for k in range(parts):
        for copy in copies(k):
            copy.start(priority=1)
    tokens, width = total.shape
    total[...] = jnp.zeros_like(total)

    def body(k, _):
        for copy in copies(k):
            copy.wait()
        for row in range(0, tokens, 128):
            place = pl.ds(row, 128)
            total[place, :] += jnp.dot(h_buf[k, place, :], held[span(k), :], preferred_element_type=jnp.float32)
        return _

    lax.fori_loop(0, parts, body, 0)
    for i in range(len(chips)):
        for out, which in ((give, 1 - core), (keep, core)):
            start = pl.multiple_of((i * CORES + which) * tok, tok)
            out[i] = total[pl.ds(start, tok), :].astype(out.dtype)


def down(hidden, weight, tok, chips_y, own):
    inner, width = weight.shape
    depth = cut(inner, 1536 if own else 768)
    parts = inner // depth
    chips = 1 if own else chips_y - 1
    tokens = chips * CORES * tok
    block = pltpu.VMEM((chips, tok, width), jnp.bfloat16)
    out_shape = (block, block) if own else (block, block, pltpu.VMEM((inner, width), jnp.bfloat16))
    return pl.pallas_call(
        functools.partial(down_kernel, chips_y, tok, parts, own),
        out_shape=out_shape,
        in_specs=[HBM, VMEM if own else HBM],
        out_specs=(VMEM,) * len(out_shape),
        scratch_shapes=[
            pltpu.VMEM((parts, tokens, depth), jnp.bfloat16),
            pltpu.VMEM((tokens, width), jnp.float32),
            pltpu.SemaphoreType.DMA((1 + chips, parts)),
        ],
        compiler_params=pltpu.CompilerParams(vmem_limit_bytes=24 * MIB),
        cost_estimate=pl.CostEstimate(
            flops=2 * tokens * inner * width,
            bytes_accessed=2 * inner * (tokens if own else width + tokens),
            transcendentals=0,
        ),
        name="down",
    )(
        pltpu.with_memory_space_constraint(hidden, pltpu.HBM),
        pltpu.with_memory_space_constraint(weight, pltpu.VMEM if own else pltpu.HBM),
    )


def merge_kernel(others, keep, got, gain, upper, lower):
    tok, width = others.shape
    own = keep[...].astype(jnp.float32) + got[...].astype(jnp.float32)
    value = (others[...] + own).astype(upper.dtype)
    upper[...] = value[: tok // 2]
    lower[0 : tok // 2, :] = value[tok // 2 :]
    rows = jnp.broadcast_to(gain[...].astype(jnp.float32), (GAIN, width))
    lower[tok // 2 : tok // 2 + GAIN, :] = rows.astype(lower.dtype)


def merge(others, keep, got, gain):
    tok, width = others.shape
    return pl.pallas_call(
        merge_kernel,
        out_shape=[pltpu.VMEM((n, width), jnp.bfloat16) for n in (tok // 2, tok // 2 + GAIN)],
        in_specs=[VMEM] * 4,
        out_specs=[VMEM] * 2,
        compiler_params=pltpu.CompilerParams(vmem_limit_bytes=8 * MIB),
        name="merge",
    )(others, keep, got, gain)


def project_kernel(cycle, hops, shapes, first, last, *refs):
    count = len(cycle)
    refs = list(refs)
    take = lambda n: [refs.pop(0) for _ in range(n)]
    pieces = [take(n) for n in shapes]
    (weight,) = take(1)
    shift_in, sums_in, total_in = [None] * 3 if first else take(3)
    if last:
        out, lhs, block, sems = refs
    elif first:
        stream, shift_out, sums_out, total_out, lhs = refs
    else:
        sums_out, total_out, lhs = refs
    total = total_in if last else total_out
    tok = shift_in.shape[0] if not first else shift_out.shape[0]
    width = lhs.shape[2]
    columns = weight.shape[1]
    strip = cut(columns, 512)
    strips = columns // strip

    me = lax.axis_index("col")
    place = pick(me, [cycle.index(c) for c in range(count)])
    ids = [pick(lax.rem(place + hop + count, count), cycle) for hop in hops]

    if not first:
        shift = shift_in[...]
        one, two = sums_in[0], sums_in[1]
    for i, parts in enumerate(pieces):
        whole = jnp.concatenate([part[...].astype(jnp.float32) for part in parts], axis=0)
        values, row = whole[0:tok], whole[tok : tok + 1]
        if first and i == 0:
            stream[...] = values.astype(stream.dtype)
            shift = jnp.mean(values, axis=1, keepdims=True)
            shift_out[...] = shift
            one = two = jnp.zeros_like(shift)
        dev = values - shift
        one = one + jnp.sum(dev, axis=1, keepdims=True)
        two = two + jnp.sum(dev * dev, axis=1, keepdims=True)
        lhs[i, 0:tok, :] = (dev * row).astype(lhs.dtype)
        lhs[i, tok : tok + EXTRA, :] = jnp.broadcast_to(row, (EXTRA, width)).astype(lhs.dtype)
    if not last:
        sums_out[0] = one
        sums_out[1] = two
    else:
        off = one / (width * count)
        var = jnp.maximum(two / (width * count) - off * off, 0.0)
        scale = 1.0 / jnp.sqrt(var + 1e-06)

    def leave(n):
        span = pl.ds(n * strip, strip)
        return pltpu.make_async_copy(block.at[:, span], out.at[:, span], sems.at[n])

    for n in range(strips):
        span = pl.ds(n * strip, strip)
        for i in range(len(hops)):
            rows = pl.ds(pl.multiple_of(ids[i] * width, width), width)
            product = jnp.dot(lhs[i], weight[rows, span], preferred_element_type=jnp.float32)
            if i == 0:
                value = product if first else total_in[:, span] + product
            else:
                value = value + product
        if last:
            block[:, span] = ((value[0:tok] - off * value[tok : tok + 1]) * scale).astype(block.dtype)
            leave(n).start()
        else:
            total[:, span] = value
    if last:
        for n in range(strips):
            leave(n).wait()


def project(pieces, hops, weight, state, cycle, last):
    first = state is None
    tok = sum(part.shape[0] for part in pieces[0]) - GAIN
    width = pieces[0][0].shape[1]
    columns = weight.shape[1]
    shift = pltpu.VMEM((tok, 1), jnp.float32)
    sums = pltpu.VMEM((2, tok, 1), jnp.float32)
    total = pltpu.VMEM((tok + EXTRA, columns), jnp.float32)
    flat = [part for parts in pieces for part in parts]
    base = len(flat) + 1
    state = () if first else state
    extra = []
    if last:
        out_shape, aliases = jax.ShapeDtypeStruct((tok, columns), jnp.bfloat16), {}
        extra = [pltpu.VMEM((tok, columns), jnp.bfloat16), pltpu.SemaphoreType.DMA((columns // cut(columns, 512),))]
    elif first:
        out_shape, aliases = (jax.ShapeDtypeStruct((tok, width), jnp.bfloat16), shift, sums, total), {}
    else:
        out_shape, aliases = (sums, total), {base + 1: 0, base + 2: 1}
    got = pl.pallas_call(
        functools.partial(project_kernel, cycle, hops, [len(parts) for parts in pieces], first, last),
        out_shape=out_shape,
        in_specs=[VMEM] * (base + len(state)),
        out_specs=jax.tree.map(lambda _: HBM if last else VMEM, out_shape),
        scratch_shapes=[pltpu.VMEM((len(hops), tok + EXTRA, width), jnp.bfloat16), *extra],
        input_output_aliases=aliases,
        compiler_params=pltpu.CompilerParams(vmem_limit_bytes=12 * MIB),
        cost_estimate=pl.CostEstimate(
            flops=2 * len(hops) * (tok + EXTRA) * width * columns,
            bytes_accessed=0,
            transcendentals=0,
        ),
        name="project",
    )(*flat, pltpu.with_memory_space_constraint(weight, pltpu.VMEM), *state)
    if last:
        return got
    return (got[0], got[1:]) if first else (state[0], *got)


def solution(mesh):
    rows, cols = mesh.shape["row"], mesh.shape["col"]
    chips_y = rows // CORES
    cycle = cycle_of(cols)
    half = cols // 2

    sibling = [(r, r ^ 1) for r in range(rows)]

    def shift(hop):
        return [(cycle[i], cycle[(i + hop) % cols]) for i in range(cols)]

    def per_device(hidden, down_weight, residual, gain, qk_weight):
        tok = residual.shape[0]

        give, keep, down_weight = down(hidden, down_weight, tok, chips_y, False)
        got = lax.ppermute(give, "row", sibling)
        both = (keep.astype(jnp.float32) + got.astype(jnp.float32)).astype(jnp.bfloat16)
        both, hidden = lax.optimization_barrier((both, hidden))
        others = residual.astype(jnp.float32)
        for step in range(1, chips_y):
            move = [(r, (r + CORES * step) % rows) for r in range(rows)]
            others = others + lax.ppermute(both[step - 1], "row", move).astype(jnp.float32)
        give, keep = down(hidden, down_weight, tok, chips_y, True)
        got = lax.ppermute(give[0], "row", sibling)
        upper, lower = merge(others, keep[0], got, gain[None, :])

        up, back = [upper, lower], [upper, lower]
        pieces, hops, opposite = [[upper, lower]], [0], None
        for step in range(1, half):
            if step == half - 1:
                opposite = up[0], back[1]
            for i in range(2):
                up[i], back[i] = lax.ppermute(up[i], "col", shift(1)), lax.ppermute(back[i], "col", shift(-1))
            if opposite:
                opposite = lax.ppermute(opposite[0], "col", shift(2)), lax.ppermute(opposite[1], "col", shift(-2))
            pieces += [list(up), list(back)]
            hops += [-step, step]
        stream, state = project(pieces[:-2], hops[:-2], qk_weight, None, cycle, False)
        return stream, project([opposite, *pieces[-2:]], [half, *hops[-2:]], qk_weight, state, cycle, True)

    placed = (P(None, "row"), P("row", "col"), P("row", "col"), P("col"), P(None, "col"))
    return jax.shard_map(
        per_device,
        mesh=mesh,
        in_specs=placed,
        out_specs=(P("row", "col"), P("row", "col")),
        check_vma=False,
    )
```

```python
import functools

import jax
import jax.numpy as jnp
from jax import lax
from jax.experimental import pallas as pl
from jax.experimental.pallas import tpu as pltpu
from jax.sharding import PartitionSpec as P

CORES = 2
EXTRA = 16
GAIN = 8
MIB = 1024 * 1024
HBM = pl.BlockSpec(memory_space=pl.ANY)
VMEM = pl.BlockSpec(memory_space=pltpu.VMEM)


def grid_of(count):
    x = 1
    while (2 * x) * (2 * x) <= count:
        x *= 2
    return count // x, x


def cycle_of(count):
    z, x = grid_of(count)
    walk = [0]
    for i in range(z):
        line = list(range(1, x))
        walk += [i * x + j for j in (line if i % 2 == 0 else line[::-1])]
    return walk + [i * x for i in range(z - 1, 0, -1)]


def pick(index, table):
    value = jnp.int32(table[0])
    for i in range(1, len(table)):
        value = jnp.where(index == i, jnp.int32(table[i]), value)
    return value


def cut(size, most):
    fits = [part for part in range(256, most + 1, 256) if size % part == 0]
    return fits[-1] if fits else size


def down_kernel(chips_y, tok, parts, own, hidden, weight, *refs):
    if own:
        (give, keep), held = refs[:2], weight
    else:
        give, keep, held = refs[:3]
    h_buf, total, sems = refs[-3:]
    depth = held.shape[0] // parts
    me = lax.axis_index("row")
    chip, core = me // CORES, me % CORES
    chips = [0] if own else list(range(1, chips_y))
    block = CORES * tok

    def span(k):
        return pl.ds(pl.multiple_of(k * depth, depth), depth)

    def copies(k):
        for i, step in enumerate(chips):
            start = pl.multiple_of(lax.rem(chip + step, chips_y) * block, block)
            yield pltpu.make_async_copy(
                hidden.at[pl.ds(start, block), span(k)], h_buf.at[k, pl.ds(i * block, block)], sems.at[1 + i, k]
            )
        if not own:
            yield pltpu.make_async_copy(weight.at[span(k), :], held.at[span(k), :], sems.at[0, k])

    for k in range(parts):
        for copy in copies(k):
            copy.start(priority=1)
    tokens, width = total.shape
    total[...] = jnp.zeros_like(total)

    def body(k, _):
        for copy in copies(k):
            copy.wait()
        for row in range(0, tokens, 128):
            place = pl.ds(row, 128)
            total[place, :] += jnp.dot(h_buf[k, place, :], held[span(k), :], preferred_element_type=jnp.float32)
        return _

    lax.fori_loop(0, parts, body, 0)
    for i in range(len(chips)):
        for out, which in ((give, 1 - core), (keep, core)):
            start = pl.multiple_of((i * CORES + which) * tok, tok)
            out[i] = total[pl.ds(start, tok), :].astype(out.dtype)


def down(hidden, weight, tok, chips_y, own):
    inner, width = weight.shape
    depth = cut(inner, 1536 if own else 768)
    parts = inner // depth
    chips = 1 if own else chips_y - 1
    tokens = chips * CORES * tok
    block = pltpu.VMEM((chips, tok, width), jnp.bfloat16)
    out_shape = (block, block) if own else (block, block, pltpu.VMEM((inner, width), jnp.bfloat16))
    return pl.pallas_call(
        functools.partial(down_kernel, chips_y, tok, parts, own),
        out_shape=out_shape,
        in_specs=[HBM, VMEM if own else HBM],
        out_specs=(VMEM,) * len(out_shape),
        scratch_shapes=[
            pltpu.VMEM((parts, tokens, depth), jnp.bfloat16),
            pltpu.VMEM((tokens, width), jnp.float32),
            pltpu.SemaphoreType.DMA((1 + chips, parts)),
        ],
        compiler_params=pltpu.CompilerParams(vmem_limit_bytes=24 * MIB),
        cost_estimate=pl.CostEstimate(
            flops=2 * tokens * inner * width,
            bytes_accessed=2 * inner * (tokens if own else width + tokens),
            transcendentals=0,
        ),
        name="down",
    )(
        pltpu.with_memory_space_constraint(hidden, pltpu.HBM),
        pltpu.with_memory_space_constraint(weight, pltpu.VMEM if own else pltpu.HBM),
    )


def merge_kernel(others, keep, got, gain, upper, lower):
    tok, width = others.shape
    cut_at = upper.shape[0]
    own = keep[...].astype(jnp.float32) + got[...].astype(jnp.float32)
    value = (others[...] + own).astype(upper.dtype)
    upper[...] = value[:cut_at]
    lower[0 : tok - cut_at, :] = value[cut_at:]
    rows = jnp.broadcast_to(gain[...].astype(jnp.float32), (GAIN, width))
    lower[tok - cut_at : tok - cut_at + GAIN, :] = rows.astype(lower.dtype)


def merge(others, keep, got, gain):
    tok, width = others.shape
    return pl.pallas_call(
        merge_kernel,
        out_shape=[pltpu.VMEM((n, width), jnp.bfloat16) for n in (tok * 5 // 8, tok * 3 // 8 + GAIN)],
        in_specs=[VMEM] * 4,
        out_specs=[VMEM] * 2,
        compiler_params=pltpu.CompilerParams(vmem_limit_bytes=8 * MIB),
        name="merge",
    )(others, keep, got, gain)


def project_kernel(cycle, hops, shapes, first, last, *refs):
    count = len(cycle)
    refs = list(refs)
    take = lambda n: [refs.pop(0) for _ in range(n)]
    pieces = [take(n) for n in shapes]
    (weight,) = take(1)
    shift_in, sums_in, total_in = [None] * 3 if first else take(3)
    if last:
        out, lhs, block, sems = refs
    elif first:
        stream, shift_out, sums_out, total_out, lhs = refs
    else:
        sums_out, total_out, lhs = refs
    total = total_in if last else total_out
    tok = shift_in.shape[0] if not first else shift_out.shape[0]
    width = lhs.shape[2]
    columns = weight.shape[1]
    strip = cut(columns, 512)
    strips = columns // strip

    me = lax.axis_index("col")
    place = pick(me, [cycle.index(c) for c in range(count)])
    ids = [pick(lax.rem(place + hop + count, count), cycle) for hop in hops]

    if not first:
        shift = shift_in[...]
        one, two = sums_in[0], sums_in[1]
    for i, parts in enumerate(pieces):
        whole = jnp.concatenate([part[...].astype(jnp.float32) for part in parts], axis=0)
        values, row = whole[0:tok], whole[tok : tok + 1]
        if first and i == 0:
            stream[...] = values.astype(stream.dtype)
            shift = jnp.mean(values, axis=1, keepdims=True)
            shift_out[...] = shift
            one = two = jnp.zeros_like(shift)
        dev = values - shift
        one = one + jnp.sum(dev, axis=1, keepdims=True)
        two = two + jnp.sum(dev * dev, axis=1, keepdims=True)
        lhs[i, 0:tok, :] = (dev * row).astype(lhs.dtype)
        lhs[i, tok : tok + EXTRA, :] = jnp.broadcast_to(row, (EXTRA, width)).astype(lhs.dtype)
    if not last:
        sums_out[0] = one
        sums_out[1] = two
    else:
        off = one / (width * count)
        var = jnp.maximum(two / (width * count) - off * off, 0.0)
        scale = 1.0 / jnp.sqrt(var + 1e-06)

    def leave(n):
        span = pl.ds(n * strip, strip)
        return pltpu.make_async_copy(block.at[:, span], out.at[:, span], sems.at[n])

    for n in range(strips):
        span = pl.ds(n * strip, strip)
        for i in range(len(hops)):
            rows = pl.ds(pl.multiple_of(ids[i] * width, width), width)
            product = jnp.dot(lhs[i], weight[rows, span], preferred_element_type=jnp.float32)
            if i == 0:
                value = product if first else total_in[:, span] + product
            else:
                value = value + product
        if last:
            block[:, span] = ((value[0:tok] - off * value[tok : tok + 1]) * scale).astype(block.dtype)
            leave(n).start()
        else:
            total[:, span] = value
    if last:
        for n in range(strips):
            leave(n).wait()


def project(pieces, hops, weight, state, cycle, last):
    first = state is None
    tok = sum(part.shape[0] for part in pieces[0]) - GAIN
    width = pieces[0][0].shape[1]
    columns = weight.shape[1]
    shift = pltpu.VMEM((tok, 1), jnp.float32)
    sums = pltpu.VMEM((2, tok, 1), jnp.float32)
    total = pltpu.VMEM((tok + EXTRA, columns), jnp.float32)
    flat = [part for parts in pieces for part in parts]
    base = len(flat) + 1
    state = () if first else state
    extra = []
    if last:
        out_shape, aliases = jax.ShapeDtypeStruct((tok, columns), jnp.bfloat16), {}
        extra = [pltpu.VMEM((tok, columns), jnp.bfloat16), pltpu.SemaphoreType.DMA((columns // cut(columns, 512),))]
    elif first:
        out_shape, aliases = (jax.ShapeDtypeStruct((tok, width), jnp.bfloat16), shift, sums, total), {}
    else:
        out_shape, aliases = (sums, total), {base + 1: 0, base + 2: 1}
    got = pl.pallas_call(
        functools.partial(project_kernel, cycle, hops, [len(parts) for parts in pieces], first, last),
        out_shape=out_shape,
        in_specs=[VMEM] * (base + len(state)),
        out_specs=jax.tree.map(lambda _: HBM if last else VMEM, out_shape),
        scratch_shapes=[pltpu.VMEM((len(hops), tok + EXTRA, width), jnp.bfloat16), *extra],
        input_output_aliases=aliases,
        compiler_params=pltpu.CompilerParams(vmem_limit_bytes=12 * MIB),
        cost_estimate=pl.CostEstimate(
            flops=2 * len(hops) * (tok + EXTRA) * width * columns,
            bytes_accessed=0,
            transcendentals=0,
        ),
        name="project",
    )(*flat, pltpu.with_memory_space_constraint(weight, pltpu.VMEM), *state)
    if last:
        return got
    return (got[0], got[1:]) if first else (state[0], *got)


def solution(mesh):
    rows, cols = mesh.shape["row"], mesh.shape["col"]
    chips_y = rows // CORES
    cycle = cycle_of(cols)
    half = cols // 2

    sibling = [(r, r ^ 1) for r in range(rows)]

    def shift(hop):
        return [(cycle[i], cycle[(i + hop) % cols]) for i in range(cols)]

    def per_device(hidden, down_weight, residual, gain, qk_weight):
        tok = residual.shape[0]

        give, keep, down_weight = down(hidden, down_weight, tok, chips_y, False)
        got = lax.ppermute(give, "row", sibling)
        both = (keep.astype(jnp.float32) + got.astype(jnp.float32)).astype(jnp.bfloat16)
        both, hidden = lax.optimization_barrier((both, hidden))
        others = residual.astype(jnp.float32)
        for step in range(1, chips_y):
            move = [(r, (r + CORES * step) % rows) for r in range(rows)]
            others = others + lax.ppermute(both[step - 1], "row", move).astype(jnp.float32)
        give, keep = down(hidden, down_weight, tok, chips_y, True)
        got = lax.ppermute(give[0], "row", sibling)
        upper, lower = merge(others, keep[0], got, gain[None, :])

        up, back = [upper, lower], [upper, lower]
        pieces, hops, opposite = [[upper, lower]], [0], None
        for step in range(1, half):
            if step == half - 1:
                opposite = up[0], back[1]
            for i in range(2):
                up[i], back[i] = lax.ppermute(up[i], "col", shift(1)), lax.ppermute(back[i], "col", shift(-1))
            if opposite:
                opposite = lax.ppermute(opposite[0], "col", shift(2)), lax.ppermute(opposite[1], "col", shift(-2))
            pieces += [list(up), list(back)]
            hops += [-step, step]
        stream, state = project(pieces[:-2], hops[:-2], qk_weight, None, cycle, False)
        state = project([opposite], [half], qk_weight, state, cycle, False)
        return stream, project(pieces[-2:], hops[-2:], qk_weight, state, cycle, True)

    placed = (P(None, "row"), P("row", "col"), P("row", "col"), P("col"), P(None, "col"))
    return jax.shard_map(
        per_device,
        mesh=mesh,
        in_specs=placed,
        out_specs=(P("row", "col"), P("row", "col")),
        check_vma=False,
    )
```

```python
import functools

import jax
import jax.numpy as jnp
from jax import lax
from jax.experimental import pallas as pl
from jax.experimental.pallas import tpu as pltpu
from jax.sharding import PartitionSpec as P

CORES = 2
EXTRA = 16
GAIN = 8
MIB = 1024 * 1024
HBM = pl.BlockSpec(memory_space=pl.ANY)
VMEM = pl.BlockSpec(memory_space=pltpu.VMEM)


def grid_of(count):
    x = 1
    while (2 * x) * (2 * x) <= count:
        x *= 2
    return count // x, x


def cycle_of(count):
    z, x = grid_of(count)
    walk = [0]
    for i in range(z):
        line = list(range(1, x))
        walk += [i * x + j for j in (line if i % 2 == 0 else line[::-1])]
    return walk + [i * x for i in range(z - 1, 0, -1)]


def pick(index, table):
    value = jnp.int32(table[0])
    for i in range(1, len(table)):
        value = jnp.where(index == i, jnp.int32(table[i]), value)
    return value


def cut(size, most):
    fits = [part for part in range(256, most + 1, 256) if size % part == 0]
    return fits[-1] if fits else size


def down_kernel(chips_y, tok, parts, own, hidden, weight, *refs):
    if own:
        (give, keep), held = refs[:2], weight
    else:
        give, keep, held = refs[:3]
    h_buf, total, sems = refs[-3:]
    depth = held.shape[0] // parts
    me = lax.axis_index("row")
    chip, core = me // CORES, me % CORES
    chips = [0] if own else list(range(1, chips_y))
    block = CORES * tok

    def span(k):
        return pl.ds(pl.multiple_of(k * depth, depth), depth)

    def copies(k):
        for i, step in enumerate(chips):
            start = pl.multiple_of(lax.rem(chip + step, chips_y) * block, block)
            yield pltpu.make_async_copy(
                hidden.at[pl.ds(start, block), span(k)], h_buf.at[k, pl.ds(i * block, block)], sems.at[1 + i, k]
            )
        if not own:
            yield pltpu.make_async_copy(weight.at[span(k), :], held.at[span(k), :], sems.at[0, k])

    for k in range(parts):
        for copy in copies(k):
            copy.start(priority=1)
    tokens, width = total.shape
    total[...] = jnp.zeros_like(total)

    def body(k, _):
        for copy in copies(k):
            copy.wait()
        for row in range(0, tokens, 128):
            place = pl.ds(row, 128)
            total[place, :] += jnp.dot(h_buf[k, place, :], held[span(k), :], preferred_element_type=jnp.float32)
        return _

    lax.fori_loop(0, parts, body, 0)
    for i in range(len(chips)):
        for out, which in ((give, 1 - core), (keep, core)):
            start = pl.multiple_of((i * CORES + which) * tok, tok)
            out[i] = total[pl.ds(start, tok), :].astype(out.dtype)


def down(hidden, weight, tok, chips_y, own):
    inner, width = weight.shape
    depth = cut(inner, 1536 if own else 768)
    parts = inner // depth
    chips = 1 if own else chips_y - 1
    tokens = chips * CORES * tok
    block = pltpu.VMEM((chips, tok, width), jnp.bfloat16)
    out_shape = (block, block) if own else (block, block, pltpu.VMEM((inner, width), jnp.bfloat16))
    return pl.pallas_call(
        functools.partial(down_kernel, chips_y, tok, parts, own),
        out_shape=out_shape,
        in_specs=[HBM, VMEM if own else HBM],
        out_specs=(VMEM,) * len(out_shape),
        scratch_shapes=[
            pltpu.VMEM((parts, tokens, depth), jnp.bfloat16),
            pltpu.VMEM((tokens, width), jnp.float32),
            pltpu.SemaphoreType.DMA((1 + chips, parts)),
        ],
        compiler_params=pltpu.CompilerParams(vmem_limit_bytes=24 * MIB),
        cost_estimate=pl.CostEstimate(
            flops=2 * tokens * inner * width,
            bytes_accessed=2 * inner * (tokens if own else width + tokens),
            transcendentals=0,
        ),
        name="down",
    )(
        pltpu.with_memory_space_constraint(hidden, pltpu.HBM),
        pltpu.with_memory_space_constraint(weight, pltpu.VMEM if own else pltpu.HBM),
    )


def merge_kernel(others, keep, got, gain, upper, lower):
    tok, width = others.shape
    cut_at = upper.shape[0]
    own = keep[...].astype(jnp.float32) + got[...].astype(jnp.float32)
    value = (others[...] + own).astype(upper.dtype)
    upper[...] = value[:cut_at]
    lower[0 : tok - cut_at, :] = value[cut_at:]
    rows = jnp.broadcast_to(gain[...].astype(jnp.float32), (GAIN, width))
    lower[tok - cut_at : tok - cut_at + GAIN, :] = rows.astype(lower.dtype)


def merge(others, keep, got, gain):
    tok, width = others.shape
    return pl.pallas_call(
        merge_kernel,
        out_shape=[pltpu.VMEM((n, width), jnp.bfloat16) for n in (tok * 3 // 8, tok * 5 // 8 + GAIN)],
        in_specs=[VMEM] * 4,
        out_specs=[VMEM] * 2,
        compiler_params=pltpu.CompilerParams(vmem_limit_bytes=8 * MIB),
        name="merge",
    )(others, keep, got, gain)


def project_kernel(cycle, hops, shapes, first, last, *refs):
    count = len(cycle)
    refs = list(refs)
    take = lambda n: [refs.pop(0) for _ in range(n)]
    pieces = [take(n) for n in shapes]
    (weight,) = take(1)
    shift_in, sums_in, total_in = [None] * 3 if first else take(3)
    if last:
        out, lhs, block, sems = refs
    elif first:
        stream, shift_out, sums_out, total_out, lhs = refs
    else:
        sums_out, total_out, lhs = refs
    total = total_in if last else total_out
    tok = shift_in.shape[0] if not first else shift_out.shape[0]
    width = lhs.shape[2]
    columns = weight.shape[1]
    strip = cut(columns, 512)
    strips = columns // strip

    me = lax.axis_index("col")
    place = pick(me, [cycle.index(c) for c in range(count)])
    ids = [pick(lax.rem(place + hop + count, count), cycle) for hop in hops]

    if not first:
        shift = shift_in[...]
        one, two = sums_in[0], sums_in[1]
    for i, parts in enumerate(pieces):
        whole = jnp.concatenate([part[...].astype(jnp.float32) for part in parts], axis=0)
        values, row = whole[0:tok], whole[tok : tok + 1]
        if first and i == 0:
            stream[...] = values.astype(stream.dtype)
            shift = jnp.mean(values, axis=1, keepdims=True)
            shift_out[...] = shift
            one = two = jnp.zeros_like(shift)
        dev = values - shift
        one = one + jnp.sum(dev, axis=1, keepdims=True)
        two = two + jnp.sum(dev * dev, axis=1, keepdims=True)
        lhs[i, 0:tok, :] = (dev * row).astype(lhs.dtype)
        lhs[i, tok : tok + EXTRA, :] = jnp.broadcast_to(row, (EXTRA, width)).astype(lhs.dtype)
    if not last:
        sums_out[0] = one
        sums_out[1] = two
    else:
        off = one / (width * count)
        var = jnp.maximum(two / (width * count) - off * off, 0.0)
        scale = 1.0 / jnp.sqrt(var + 1e-06)

    def leave(n):
        span = pl.ds(n * strip, strip)
        return pltpu.make_async_copy(block.at[:, span], out.at[:, span], sems.at[n])

    for n in range(strips):
        span = pl.ds(n * strip, strip)
        for i in range(len(hops)):
            rows = pl.ds(pl.multiple_of(ids[i] * width, width), width)
            product = jnp.dot(lhs[i], weight[rows, span], preferred_element_type=jnp.float32)
            if i == 0:
                value = product if first else total_in[:, span] + product
            else:
                value = value + product
        if last:
            block[:, span] = ((value[0:tok] - off * value[tok : tok + 1]) * scale).astype(block.dtype)
            leave(n).start()
        else:
            total[:, span] = value
    if last:
        for n in range(strips):
            leave(n).wait()


def project(pieces, hops, weight, state, cycle, last):
    first = state is None
    tok = sum(part.shape[0] for part in pieces[0]) - GAIN
    width = pieces[0][0].shape[1]
    columns = weight.shape[1]
    shift = pltpu.VMEM((tok, 1), jnp.float32)
    sums = pltpu.VMEM((2, tok, 1), jnp.float32)
    total = pltpu.VMEM((tok + EXTRA, columns), jnp.float32)
    flat = [part for parts in pieces for part in parts]
    base = len(flat) + 1
    state = () if first else state
    extra = []
    if last:
        out_shape, aliases = jax.ShapeDtypeStruct((tok, columns), jnp.bfloat16), {}
        extra = [pltpu.VMEM((tok, columns), jnp.bfloat16), pltpu.SemaphoreType.DMA((columns // cut(columns, 512),))]
    elif first:
        out_shape, aliases = (jax.ShapeDtypeStruct((tok, width), jnp.bfloat16), shift, sums, total), {}
    else:
        out_shape, aliases = (sums, total), {base + 1: 0, base + 2: 1}
    got = pl.pallas_call(
        functools.partial(project_kernel, cycle, hops, [len(parts) for parts in pieces], first, last),
        out_shape=out_shape,
        in_specs=[VMEM] * (base + len(state)),
        out_specs=jax.tree.map(lambda _: HBM if last else VMEM, out_shape),
        scratch_shapes=[pltpu.VMEM((len(hops), tok + EXTRA, width), jnp.bfloat16), *extra],
        input_output_aliases=aliases,
        compiler_params=pltpu.CompilerParams(vmem_limit_bytes=12 * MIB),
        cost_estimate=pl.CostEstimate(
            flops=2 * len(hops) * (tok + EXTRA) * width * columns,
            bytes_accessed=0,
            transcendentals=0,
        ),
        name="project",
    )(*flat, pltpu.with_memory_space_constraint(weight, pltpu.VMEM), *state)
    if last:
        return got
    return (got[0], got[1:]) if first else (state[0], *got)


def solution(mesh):
    rows, cols = mesh.shape["row"], mesh.shape["col"]
    chips_y = rows // CORES
    cycle = cycle_of(cols)
    half = cols // 2

    sibling = [(r, r ^ 1) for r in range(rows)]

    def shift(hop):
        return [(cycle[i], cycle[(i + hop) % cols]) for i in range(cols)]

    def per_device(hidden, down_weight, residual, gain, qk_weight):
        tok = residual.shape[0]

        give, keep, down_weight = down(hidden, down_weight, tok, chips_y, False)
        got = lax.ppermute(give, "row", sibling)
        both = (keep.astype(jnp.float32) + got.astype(jnp.float32)).astype(jnp.bfloat16)
        both, hidden = lax.optimization_barrier((both, hidden))
        others = residual.astype(jnp.float32)
        for step in range(1, chips_y):
            move = [(r, (r + CORES * step) % rows) for r in range(rows)]
            others = others + lax.ppermute(both[step - 1], "row", move).astype(jnp.float32)
        give, keep = down(hidden, down_weight, tok, chips_y, True)
        got = lax.ppermute(give[0], "row", sibling)
        upper, lower = merge(others, keep[0], got, gain[None, :])

        up, back = [upper, lower], [upper, lower]
        pieces, hops, opposite = [[upper, lower]], [0], None
        for step in range(1, half):
            if step == half - 1:
                opposite = up[0], back[1]
            for i in range(2):
                up[i], back[i] = lax.ppermute(up[i], "col", shift(1)), lax.ppermute(back[i], "col", shift(-1))
            if opposite:
                opposite = lax.ppermute(opposite[0], "col", shift(2)), lax.ppermute(opposite[1], "col", shift(-2))
            pieces += [list(up), list(back)]
            hops += [-step, step]
        stream, state = project(pieces[:-2], hops[:-2], qk_weight, None, cycle, False)
        state = project([opposite], [half], qk_weight, state, cycle, False)
        return stream, project(pieces[-2:], hops[-2:], qk_weight, state, cycle, True)

    placed = (P(None, "row"), P("row", "col"), P("row", "col"), P("col"), P(None, "col"))
    return jax.shard_map(
        per_device,
        mesh=mesh,
        in_specs=placed,
        out_specs=(P("row", "col"), P("row", "col")),
        check_vma=False,
    )
```
